128 devices in a mesh: grp: 8 (over z, core), ctx: 16 (over x, y).
Axes of the slice: x: 4, y: 4, z: 4, core: 2. Of those that a mesh axis runs over, the one named last changes fastest.
Arguments:
- query_rows: bfloat16 [131072, 512], P(('grp', 'ctx')), may hold values from -6 to 6
- key_rows: bfloat16 [131072, 512], P(('grp', 'ctx')), may hold values from -6 to 6
- value_rows: bfloat16 [131072, 512], P(('grp', 'ctx')), may hold values from -6 to 6
- cluster_ids: int32 [4, 131072], P(None, ('grp', 'ctx')), may hold values from 0 to 1023, as said below
Outputs:
- attended: bfloat16 [131072, 512], P(('grp', 'ctx'))
The draws below stay inside these ranges and needn't reach their ends.
Inputs may be any that keep to these rules, and one draw needn't show every extreme that they name: `cluster_ids`: for each head, the tokens of one device whose clusters share one value of id // 8 number at most 24; for each head one such range receives exactly 24 tokens from every device, and every other range at most 8 from one device. For each head and range, the sum over its clusters of their token counts rounded up to multiples of 128 is at most 3072, with equality for the range that is full.
All inputs are finite; a program needn't handle non-finite values.
Results may differ from the reference program's by a relative error of at most 0.0034.
Values may be sent and summed in bfloat16 or wider, within the bound.
No kernel may reach another device: no remote copies, remote signals or barrier semaphores. Data moves between devices by JAX's collectives and lax.ppermute only.
A program may use at most 128 MiB of HBM per device.

```python
import jax
import jax.numpy as jnp
from jax import lax

HEADS = 4
HD = 128
CL_DEV = 8
TILE = 128
TOK_DEV = 1024
TOKENS = 131072


def routing_plan(key):
    device_count = TOKENS // TOK_DEV
    capacity = 3 * TOK_DEV // device_count
    modest = TOK_DEV // device_count
    busy_rows = device_count * capacity
    tile_count = busy_rows // TILE
    pool_size = (device_count - 1) * modest
    root_key = jax.random.fold_in(key, 7101)
    label_list = []
    busiest_list = []
    for head_pos in range(HEADS):
        head_key = jax.random.fold_in(root_key, head_pos)
        busiest = jax.random.randint(jax.random.fold_in(head_key, 1), (), 0, device_count).astype(jnp.int32)
        pick_keys = jax.random.split(jax.random.fold_in(head_key, 2), device_count)
        picked = jax.vmap(lambda one_key: jax.random.permutation(one_key, pool_size)[:TOK_DEV - capacity])(pick_keys)
        others = (picked // modest).astype(jnp.int32)
        others = others + (others >= busiest).astype(jnp.int32)
        targets = jnp.concatenate([jnp.full((device_count, capacity), busiest, jnp.int32), others], axis=1)
        order_keys = jax.random.split(jax.random.fold_in(head_key, 3), device_count)
        targets = jax.vmap(lambda one_key, one_row: jax.random.permutation(one_key, one_row))(order_keys, targets)
        first_pick = jax.random.randint(jax.random.fold_in(head_key, 4), (device_count, TOK_DEV), 0, CL_DEV)
        second_pick = jax.random.randint(jax.random.fold_in(head_key, 5), (device_count, TOK_DEV), 0, CL_DEV)
        spread = jnp.minimum(first_pick, second_pick).astype(jnp.int32)
        cut_points = jnp.sort(jax.random.permutation(jax.random.fold_in(head_key, 6), tile_count - 1)[:CL_DEV - 1] + 1)
        row_index = jnp.arange(busy_rows, dtype=jnp.int32)
        busy_labels = jnp.sum((row_index[:, None] >= cut_points[None, :] * TILE).astype(jnp.int32), axis=1)
        busy_labels = jax.random.permutation(jax.random.fold_in(head_key, 7), busy_labels)
        at_busiest = (targets == busiest).astype(jnp.int32)
        busy_rank = jnp.cumsum(at_busiest, axis=1) - at_busiest
        source_index = jnp.arange(device_count, dtype=jnp.int32)[:, None]
        lookup = jnp.minimum(source_index * capacity + busy_rank, busy_rows - 1)
        local_ids = jnp.where(at_busiest == 1, busy_labels[lookup], spread)
        label_list.append((targets * CL_DEV + local_ids).reshape(-1).astype(jnp.int32))
        busiest_list.append(busiest)
    return jnp.stack(label_list, axis=0)


def draw_cluster_ids(key, part):
    return routing_plan(key)


def drawn(key, which):
    noise_key = jax.random.fold_in(key, 9300 + which)
    values = jnp.clip(jax.random.normal(noise_key, (TOKENS, HEADS, HD), jnp.float32), -6.0, 6.0)
    return values.reshape(TOKENS, HEADS * HD).astype(jnp.bfloat16)


def draw_query_rows(key, part):
    return drawn(key, 0)


def draw_key_rows(key, part):
    return drawn(key, 1)


def shard_levels(rng, dims, cuts, smallest, top_value):
    def one(position, parts):
        heights = jax.random.uniform(jax.random.fold_in(jax.random.fold_in(rng, 6), position), (parts,), jnp.float32, smallest / len(cuts), top_value / len(cuts))
        return jnp.repeat(jnp.exp(heights), dims[position] // parts).reshape((-1,) + (1,) * (len(dims) - position - 1))

    factor_of = one(*cuts[0])
    for cut in cuts[1:]:
        factor_of = factor_of * one(*cut)
    return factor_of


def centred(own_key, shape, width, bound, cuts=(), kind=jnp.bfloat16):
    array = jax.random.normal(own_key, shape, jnp.float32) * width
    if len(cuts) > 0:
        array = shard_levels(own_key, shape, cuts, -0.22, 0.18) * array
    return jnp.clip(array, min=-bound, max=bound).astype(kind)


def setup_inputs(seed: int = 0) -> dict:
    seeds = jax.random.split(jax.random.key(seed), 5)
    query_rows = draw_query_rows(jax.random.fold_in(seeds[4], 71), 0)
    key_rows = draw_key_rows(jax.random.fold_in(seeds[4], 71), 0)
    value_rows = centred(seeds[2], (TOKENS, HEADS * HD), 1.0, 6.0, ((0, 128),))
    cluster_ids = draw_cluster_ids(jax.random.fold_in(seeds[4], 71), 0)
    return {"query_rows": query_rows, "key_rows": key_rows, "value_rows": value_rows, "cluster_ids": cluster_ids}


NEG_FILL = -1.0e30


def head_output(query_head, key_head, value_head, labels):
    total_rows = query_head.shape[0]
    positions = jnp.arange(total_rows, dtype=jnp.int32)
    sort_order = jnp.argsort(labels * total_rows + positions).astype(jnp.int32)
    sorted_query = query_head[sort_order]
    sorted_key = key_head[sort_order]
    sorted_value = value_head[sort_order]
    sorted_label = labels[sort_order]
    previous = jnp.concatenate([jnp.full((1,), -1, jnp.int32), sorted_label[:-1]])
    region_start = lax.cummax(jnp.where(sorted_label != previous, positions, 0), axis=0)
    block_rows = 256
    first_rows = region_start.reshape(-1, block_rows)[:, 0]
    score_scale = HD ** -0.5

    def one_block(block_index):
        row_start = block_index * block_rows
        query_part = lax.dynamic_slice_in_dim(sorted_query, row_start, block_rows, 0)
        query_label = lax.dynamic_slice_in_dim(sorted_label, row_start, block_rows, 0)
        query_pos = row_start + jnp.arange(block_rows, dtype=jnp.int32)

        def key_block(key_index, state_now):
            run_max, run_sum, weighted = state_now
            key_start = key_index * block_rows
            key_part = lax.dynamic_slice_in_dim(sorted_key, key_start, block_rows, 0)
            value_part = lax.dynamic_slice_in_dim(sorted_value, key_start, block_rows, 0)
            key_label = lax.dynamic_slice_in_dim(sorted_label, key_start, block_rows, 0)
            key_pos = key_start + jnp.arange(block_rows, dtype=jnp.int32)
            scores = jnp.dot(query_part, key_part.T, preferred_element_type=jnp.float32) * score_scale
            allowed = (query_label[:, None] == key_label[None, :]) & (key_pos[None, :] <= query_pos[:, None])
            masked = jnp.where(allowed, scores, NEG_FILL)
            new_max = jnp.maximum(run_max, jnp.max(masked, axis=1))
            weights = jnp.where(allowed, jnp.exp(masked - new_max[:, None]), 0.0)
            factor = jnp.exp(run_max - new_max)
            run_sum = run_sum * factor + jnp.sum(weights, axis=1)
            weighted = weighted * factor[:, None] + jnp.dot(weights.astype(jnp.bfloat16), value_part, preferred_element_type=jnp.float32)
            return new_max, run_sum, weighted

        start_state = (jnp.full((block_rows,), NEG_FILL, jnp.float32), jnp.zeros((block_rows,), jnp.float32), jnp.zeros((block_rows, HD), jnp.float32))
        first_block = first_rows[block_index] // block_rows
        run_max, run_sum, weighted = lax.fori_loop(first_block, block_index + 1, key_block, start_state)
        return (weighted / run_sum[:, None]).astype(jnp.bfloat16)

    block_ids = jnp.arange(total_rows // block_rows, dtype=jnp.int32)
    sorted_out = lax.map(one_block, block_ids).reshape(total_rows, HD)
    return jnp.zeros_like(sorted_out).at[sort_order].set(sorted_out)


def reference(query_rows, key_rows, value_rows, cluster_ids):
    query_split = query_rows.reshape(TOKENS, HEADS, HD)
    key_split = key_rows.reshape(TOKENS, HEADS, HD)
    value_split = value_rows.reshape(TOKENS, HEADS, HD)
    outputs = []
    for head_pos in range(HEADS):
        outputs.append(head_output(query_split[:, head_pos], key_split[:, head_pos], value_split[:, head_pos], cluster_ids[head_pos]))
    return jnp.stack(outputs, axis=1).reshape(TOKENS, HEADS * HD)
```

```python
import functools

import jax
import jax.numpy as jnp
from jax import lax
from jax.experimental import pallas as pl
from jax.experimental.pallas import tpu as pltpu
from jax.sharding import PartitionSpec as P

CL_DEV = 8
COLD = 8
HOT = 24
HOT_PAD = 32
LANES = 128
NEG_FILL = -1e30
LOG2E = 1.4426950408889634
F32 = jnp.float32
BF16 = jnp.bfloat16
VMEM_LIMIT = 56 * 1024 * 1024


def pack_kernel(ids_ref, q_ref, k_ref, v_ref, send_ref, hot_kv_ref, hot_q_ref, cols_ref, x_ref):
    heads, tokens = ids_ref.shape
    devices = send_ref.shape[0]
    hd = q_ref.shape[1] // heads
    slots = devices * COLD
    step = 256
    ids = ids_ref[...]
    owner = ids // CL_DEV
    lid = ids - owner * CL_DEV
    upper = (
        lax.broadcasted_iota(jnp.int32, (step, step), 0)
        < lax.broadcasted_iota(jnp.int32, (step, step), 1)
    ).astype(BF16)
    dev_col = lax.broadcasted_iota(jnp.int32, (devices, step), 0)
    slot_rows = []
    for h in range(heads):
        carry = jnp.zeros((devices, 1), F32)
        ones, ranks = [], []
        for b in range(tokens // step):
            one = (owner[h : h + 1, b * step : (b + 1) * step] == dev_col).astype(F32)
            inside = jnp.dot(one.astype(BF16), upper, preferred_element_type=F32) + carry
            carry = carry + jnp.sum(one, axis=1, keepdims=True)
            ones.append(one)
            ranks.append(jnp.sum(one * inside, axis=0, keepdims=True))
        full = (carry > COLD).astype(F32)
        is_hot = jnp.concatenate(
            [jnp.sum(one * full, axis=0, keepdims=True) for one in ones], axis=1
        )
        rank = jnp.concatenate(ranks, axis=1).astype(jnp.int32)
        slot_rows.append(jnp.where(is_hot > 0.5, slots + rank, owner[h : h + 1] * COLD + rank))
    slot_all = jnp.concatenate(slot_rows, axis=0)
    pad = jnp.zeros((4, tokens), F32)
    table = jnp.concatenate(
        [(lid + 1).astype(F32), pad, slot_all.astype(F32), pad, jnp.zeros((LANES - 16, tokens), F32)],
        axis=0,
    )
    cols = jnp.transpose(table)
    cols_ref[...] = cols
    lane = lax.broadcasted_iota(jnp.int32, (tokens, LANES), 1)
    labels = jnp.zeros((slots, LANES), F32)
    hot_labels = jnp.zeros((HOT_PAD, LANES), F32)
    part = 256
    label_parts = [jnp.zeros((part, LANES), F32) for _ in range(slots // part)]
    for h in range(heads):
        x_ref[:, 0:hd] = q_ref[:, h * hd : (h + 1) * hd]
        x_ref[:, hd : 2 * hd] = k_ref[:, h * hd : (h + 1) * hd]
        x_ref[:, 2 * hd : 3 * hd] = v_ref[:, h * hd : (h + 1) * hd]
        x_ref[:, 3 * hd :] = jnp.where(lane == h, cols, 0.0).astype(BF16)
        rows = x_ref[...]
        slot_row = slot_all[h : h + 1]
        for c in range(slots // part):
            place = (
                slot_row == lax.broadcasted_iota(jnp.int32, (part, tokens), 0) + c * part
            ).astype(BF16)
            moved = jnp.dot(place, rows, preferred_element_type=F32)
            devs = slice(c * part // COLD, (c + 1) * part // COLD)
            for j in range(3):
                send_ref[devs, 3 * h + j] = (
                    moved[:, j * hd : (j + 1) * hd].reshape(part // COLD, COLD, hd).astype(BF16)
                )
            label_parts[c] = label_parts[c] + moved[:, 3 * hd :]
        place = (
            slot_row == lax.broadcasted_iota(jnp.int32, (HOT_PAD, tokens), 0) + slots
        ).astype(BF16)
        moved = jnp.dot(place, rows, preferred_element_type=F32)
        hot_q_ref[3 * h : 3 * h + 3] = moved[:HOT, :hd].reshape(3, COLD, hd).astype(BF16)
        hot_kv_ref[6 * h : 6 * h + 3] = moved[:HOT, hd : 2 * hd].reshape(3, COLD, hd).astype(BF16)
        hot_kv_ref[6 * h + 3 : 6 * h + 6] = (
            moved[:HOT, 2 * hd : 3 * hd].reshape(3, COLD, hd).astype(BF16)
        )
        hot_labels = hot_labels + moved[:, 3 * hd :]
    for c in range(slots // part):
        devs = slice(c * part // COLD, (c + 1) * part // COLD)
        send_ref[devs, 3 * heads] = (
            label_parts[c].reshape(part // COLD, COLD, LANES).astype(BF16)
        )
    hot_kv_ref[6 * heads :] = hot_labels[:HOT].reshape(3, COLD, LANES).astype(BF16)


def softmax_rows(scores, allowed, scale, values):
    masked = jnp.where(allowed, scores, NEG_FILL)
    top = jnp.max(masked, axis=1, keepdims=True)
    weights = jnp.exp2((masked - top) * scale)
    total = jnp.sum(weights, axis=1, keepdims=True)
    out = jnp.dot(weights.astype(BF16), values, preferred_element_type=F32)
    return out / total


NT = (((1,), (1,)), ((), ()))


def cold_kernel(got_ref, out_ref):
    devices, tiles, _, hd = got_ref.shape
    heads = tiles // 3
    slots = devices * COLD
    scale = hd ** (-0.5) * LOG2E
    labels = got_ref[:, 3 * heads].astype(F32).reshape(slots, hd)
    label_rows = jnp.transpose(labels)
    part = 256
    causal = lax.broadcasted_iota(jnp.int32, (part, part), 1) <= lax.broadcasted_iota(
        jnp.int32, (part, part), 0
    )
    for h in range(heads):
        q, k, v = (
            got_ref[:, 3 * h + j].astype(F32).reshape(slots, hd).astype(BF16) for j in range(3)
        )
        row = label_rows[h : h + 1]
        for c in range(slots // part):
            stop = (c + 1) * part
            col = labels[c * part : stop, h : h + 1]
            scores = lax.dot_general(
                q[c * part : stop], k[:stop], NT, preferred_element_type=F32
            )
            allowed = col == row[:, :stop]
            last = allowed[:, c * part :] & causal
            allowed = last if c == 0 else jnp.concatenate([allowed[:, : c * part], last], axis=1)
            out = softmax_rows(scores, allowed, scale, v[:stop])
            devs = slice(c * part // COLD, stop // COLD)
            out_ref[devs, h] = out.reshape(part // COLD, COLD, hd).astype(BF16)


def hot_kernel(me_ref, q_ref, own_ref, all_ref, out_ref):
    devices, tiles, _, hd = all_ref.shape
    heads = tiles // 6
    keys = devices * HOT
    scale = hd ** (-0.5) * LOG2E
    own_labels = own_ref[6 * heads :].astype(F32).reshape(HOT, hd)
    labels = all_ref[:, 6 * heads :].astype(F32).reshape(keys, hd)
    label_rows = jnp.transpose(labels)
    first = me_ref[0] * HOT
    before = lax.broadcasted_iota(jnp.int32, (HOT, keys), 1) <= first + lax.broadcasted_iota(
        jnp.int32, (HOT, keys), 0
    )
    for h in range(heads):
        q = q_ref[3 * h : 3 * h + 3].astype(F32).reshape(HOT, hd).astype(BF16)
        k = all_ref[:, 6 * h : 6 * h + 3].astype(F32).reshape(keys, hd).astype(BF16)
        v = all_ref[:, 6 * h + 3 : 6 * h + 6].astype(F32).reshape(keys, hd).astype(BF16)
        scores = lax.dot_general(q, k, NT, preferred_element_type=F32)
        allowed = (own_labels[:, h : h + 1] == label_rows[h : h + 1]) & before
        out = softmax_rows(scores, allowed, scale, v)
        out_ref[3 * h : 3 * h + 3] = out.reshape(3, COLD, hd)


def unpack_kernel(cols_ref, back_ref, hot_ref, out_ref):
    devices, heads, _, hd = back_ref.shape
    tokens = cols_ref.shape[0]
    slots = devices * COLD
    part = 256
    for h in range(heads):
        rows = back_ref[:, h].astype(F32).reshape(slots, hd).astype(BF16)
        hot = hot_ref[3 * h : 3 * h + 3].reshape(HOT, hd)
        hot = jnp.concatenate([hot, jnp.zeros((LANES - HOT, hd), F32)], axis=0).astype(BF16)
        for c in range(tokens // part):
            slot = cols_ref[c * part : (c + 1) * part, 8 + h : 9 + h].astype(jnp.int32)
            place = (slot == lax.broadcasted_iota(jnp.int32, (part, slots), 1)).astype(BF16)
            hot_place = (
                slot == lax.broadcasted_iota(jnp.int32, (part, LANES), 1) + slots
            ).astype(BF16)
            got = jnp.dot(place, rows, preferred_element_type=F32) + jnp.dot(
                hot_place, hot, preferred_element_type=F32
            )
            out_ref[c * part : (c + 1) * part, h * hd : (h + 1) * hd] = got.astype(BF16)


def vmem(count):
    return [pl.BlockSpec(memory_space=pltpu.VMEM)] * count


PARAMS = pltpu.CompilerParams(vmem_limit_bytes=VMEM_LIMIT)


def local(query_rows, key_rows, value_rows, cluster_ids):
    devices = lax.axis_size("grp") * lax.axis_size("ctx")
    heads, tokens = cluster_ids.shape
    hd = query_rows.shape[1] // heads
    axes = ("grp", "ctx")
    send, hot_kv, hot_q, cols = pl.pallas_call(
        pack_kernel,
        out_shape=(
            jax.ShapeDtypeStruct((devices, 3 * heads + 1, COLD, hd), BF16),
            jax.ShapeDtypeStruct((6 * heads + 3, COLD, hd), BF16),
            jax.ShapeDtypeStruct((3 * heads, COLD, hd), BF16),
            jax.ShapeDtypeStruct((tokens, LANES), F32),
        ),
        in_specs=vmem(4),
        out_specs=tuple(vmem(4)),
        scratch_shapes=[pltpu.VMEM((tokens, 3 * hd + LANES), BF16)],
        compiler_params=PARAMS,
        name="pack",
    )(cluster_ids, query_rows, key_rows, value_rows)
    hot_all = lax.all_gather(hot_kv, axes, axis=0, tiled=False)
    got = lax.all_to_all(send, axes, split_axis=0, concat_axis=0, tiled=True)
    me = lax.axis_index(axes).astype(jnp.int32).reshape(1)
    hot_out = pl.pallas_call(
        hot_kernel,
        out_shape=jax.ShapeDtypeStruct((3 * heads, COLD, hd), F32),
        in_specs=[pl.BlockSpec(memory_space=pltpu.SMEM)] + vmem(3),
        out_specs=vmem(1)[0],
        compiler_params=PARAMS,
        name="hot",
    )(me, hot_q, hot_kv, hot_all)
    answer = pl.pallas_call(
        cold_kernel,
        out_shape=jax.ShapeDtypeStruct((devices, heads, COLD, hd), BF16),
        in_specs=vmem(1),
        out_specs=vmem(1)[0],
        compiler_params=PARAMS,
        name="cold",
    )(got)
    back = lax.all_to_all(answer, axes, split_axis=0, concat_axis=0, tiled=True)
    return pl.pallas_call(
        unpack_kernel,
        out_shape=jax.ShapeDtypeStruct((tokens, heads * hd), BF16),
        in_specs=vmem(3),
        out_specs=vmem(1)[0],
        compiler_params=PARAMS,
        name="unpack",
    )(cols, back, hot_out)


def solution(mesh):
    return jax.shard_map(
        local,
        mesh=mesh,
        in_specs=(
            P(("grp", "ctx"), None),
            P(("grp", "ctx"), None),
            P(("grp", "ctx"), None),
            P(None, ("grp", "ctx")),
        ),
        out_specs=P(("grp", "ctx"), None),
        check_vma=False,
    )
```

```python
import jax
import jax.numpy as jnp
from jax import lax
from jax.experimental import pallas as pl
from jax.experimental.pallas import tpu as pltpu
from jax.sharding import PartitionSpec as P

CL_DEV = 8
COLD = 8
HOT = 24
HOT_PAD = 32
LANES = 128
NEG_FILL = -1e30
LOG2E = 1.4426950408889634
F32 = jnp.float32
BF16 = jnp.bfloat16
VMEM_LIMIT = 24 * 1024 * 1024


def pack_kernel(
    at_ref, ids_ref, q_ref, k_ref, v_ref, send_ref, h0_ref, h1_ref, h2_ref, h3_ref, cols_ref, x_ref, hot_ref
):
    heads, tokens = ids_ref.shape
    devices = send_ref.shape[0]
    hd = q_ref.shape[1] // heads
    slots = devices * COLD
    step = 256
    ids = ids_ref[...]
    owner = ids // CL_DEV
    lid = ids - owner * CL_DEV
    upper = (
        lax.broadcasted_iota(jnp.int32, (step, step), 0)
        < lax.broadcasted_iota(jnp.int32, (step, step), 1)
    ).astype(BF16)
    dev_col = lax.broadcasted_iota(jnp.int32, (devices, step), 0)
    slot_rows = []
    for h in range(heads):
        carry = jnp.zeros((devices, 1), F32)
        ones, ranks = [], []
        for b in range(tokens // step):
            one = (owner[h : h + 1, b * step : (b + 1) * step] == dev_col).astype(F32)
            inside = jnp.dot(one.astype(BF16), upper, preferred_element_type=F32) + carry
            carry = carry + jnp.sum(one, axis=1, keepdims=True)
            ones.append(one)
            ranks.append(jnp.sum(one * inside, axis=0, keepdims=True))
        full = (carry > COLD).astype(F32)
        is_hot = jnp.concatenate(
            [jnp.sum(one * full, axis=0, keepdims=True) for one in ones], axis=1
        )
        rank = jnp.concatenate(ranks, axis=1).astype(jnp.int32)
        slot_rows.append(jnp.where(is_hot > 0.5, slots + rank, owner[h : h + 1] * COLD + rank))
    slot_all = jnp.concatenate(slot_rows, axis=0)
    pad = jnp.zeros((4, tokens), F32)
    table = jnp.concatenate(
        [(lid + 1).astype(F32), pad, slot_all.astype(F32), pad, jnp.zeros((LANES - 16, tokens), F32)],
        axis=0,
    )
    cols = jnp.transpose(table)
    cols_ref[...] = cols
    lane = lax.broadcasted_iota(jnp.int32, (tokens, LANES), 1)
    part = 256
    label_parts = [jnp.zeros((part, LANES), F32) for _ in range(slots // part)]
    for h in range(heads):
        x_ref[:, 0:hd] = q_ref[:, h * hd : (h + 1) * hd]
        x_ref[:, hd : 2 * hd] = k_ref[:, h * hd : (h + 1) * hd]
        x_ref[:, 2 * hd : 3 * hd] = v_ref[:, h * hd : (h + 1) * hd]
        x_ref[:, 3 * hd :] = jnp.where(lane == h, cols, 0.0).astype(BF16)
        rows = x_ref[...]
        slot_row = slot_all[h : h + 1]
        for c in range(slots // part):
            place = (
                slot_row == lax.broadcasted_iota(jnp.int32, (part, tokens), 0) + c * part
            ).astype(BF16)
            moved = jnp.dot(place, rows, preferred_element_type=F32)
            devs = slice(c * part // COLD, (c + 1) * part // COLD)
            for j in range(3):
                send_ref[devs, 3 * h + j] = (
                    moved[:, j * hd : (j + 1) * hd].reshape(part // COLD, COLD, hd).astype(BF16)
                )
            label_parts[c] = label_parts[c] + moved[:, 3 * hd :]
        place = (
            slot_row == lax.broadcasted_iota(jnp.int32, (HOT_PAD, tokens), 0) + slots
        ).astype(BF16)
        moved = jnp.dot(place, rows, preferred_element_type=F32)
        for j in range(4):
            block = moved[:HOT, j * hd : (j + 1) * hd]
            if j == 3:
                block = jnp.broadcast_to(block[:, h : h + 1], (HOT, hd))
            hot_ref[h, 3 * j : 3 * j + 3] = block.reshape(3, COLD, hd).astype(BF16)
    for c in range(slots // part):
        devs = slice(c * part // COLD, (c + 1) * part // COLD)
        send_ref[devs, 3 * heads] = (
            label_parts[c].reshape(part // COLD, COLD, LANES).astype(BF16)
        )
    for d, ref in enumerate((h0_ref, h1_ref, h2_ref, h3_ref)):
        ref[...] = hot_ref[lax.rem(at_ref[0] + d, heads)]


def softmax_rows(scores, allowed, scale, values):
    masked = jnp.where(allowed, scores, NEG_FILL)
    top = jnp.max(masked, axis=1, keepdims=True)
    weights = jnp.exp2((masked - top) * scale)
    total = jnp.sum(weights, axis=1, keepdims=True)
    out = jnp.dot(weights.astype(BF16), values, preferred_element_type=F32)
    return out / total


NT = (((1,), (1,)), ((), ()))


def cold_kernel(got_ref, out_ref):
    devices, tiles, _, hd = got_ref.shape
    heads = tiles // 3
    slots = devices * COLD
    scale = hd ** (-0.5) * LOG2E
    labels = got_ref[:, 3 * heads].astype(F32).reshape(slots, hd)
    label_rows = jnp.transpose(labels)
    part = 256
    causal = lax.broadcasted_iota(jnp.int32, (part, part), 1) <= lax.broadcasted_iota(
        jnp.int32, (part, part), 0
    )
    for h in range(heads):
        q, k, v = (
            got_ref[:, 3 * h + j].astype(F32).reshape(slots, hd).astype(BF16) for j in range(3)
        )
        row = label_rows[h : h + 1]
        for c in range(slots // part):
            stop = (c + 1) * part
            col = labels[c * part : stop, h : h + 1]
            scores = lax.dot_general(
                q[c * part : stop], k[:stop], NT, preferred_element_type=F32
            )
            allowed = col == row[:, :stop]
            last = allowed[:, c * part :] & causal
            allowed = last if c == 0 else jnp.concatenate([allowed[:, : c * part], last], axis=1)
            out = softmax_rows(scores, allowed, scale, v[:stop])
            devs = slice(c * part // COLD, stop // COLD)
            out_ref[devs, h] = out.reshape(part // COLD, COLD, hd).astype(BF16)


def mid_kernel(at_ref, b0_ref, b1_ref, b2_ref, b3_ref, q_ref, kv_ref, all_ref):
    hd = q_ref.shape[-1]
    for d, ref in enumerate((b0_ref, b1_ref, b2_ref, b3_ref)):
        all_ref[lax.rem(at_ref[0] - d + 4, 4)] = ref[...].astype(F32)
    rows = 4 * HOT
    blocks = [all_ref[:, 3 * j : 3 * j + 3] for j in range(4)]
    labels = blocks[3].reshape(rows, hd)
    q_ref[0:12] = blocks[0].reshape(12, COLD, hd).astype(BF16)
    q_ref[12:24] = blocks[3].reshape(12, COLD, hd).astype(BF16)
    kv_ref[0:12] = blocks[1].reshape(12, COLD, hd).astype(BF16)
    kv_ref[12:24] = blocks[2].reshape(12, COLD, hd).astype(BF16)
    flat = jnp.transpose(jnp.concatenate([labels, jnp.zeros((LANES - rows, hd), F32)], axis=0))
    kv_ref[24] = flat[:COLD].astype(BF16)


def hot_kernel(at_ref, q_ref, near_ref, far_ref, o0_ref, o1_ref, o2_ref, o3_ref, k_ref, v_ref, o_ref):
    hd = q_ref.shape[-1]
    rows = 4 * HOT
    scale = hd ** (-0.5) * LOG2E
    y, x, core, z = (at_ref[i] for i in range(4))
    mine = (z * 2 + core) * 4 + x
    q = q_ref[0:12].astype(F32).reshape(rows, hd).astype(BF16)
    label_col = q_ref[12:24].astype(F32).reshape(rows, hd)[:, 0:1]
    zeros = jnp.zeros((LANES - rows, hd), F32)
    allowed = []
    for dc, ref in enumerate((near_ref, far_ref)):
        for dz in range(4):
            for dx in range(4):
                n = (dc * 4 + dz) * 4 + dx
                tile = 25 * (dz * 4 + dx)
                at = slice(n * LANES, (n + 1) * LANES)
                for dst_ref, first in ((k_ref, 0), (v_ref, 12)):
                    block = ref[tile + first : tile + first + 12].astype(F32).reshape(rows, hd)
                    dst_ref[at] = jnp.concatenate([block, zeros], axis=0).astype(BF16)
                label_row = ref[tile + 24].astype(F32)[0:1]
                theirs = (lax.rem(z + 4 - dz, 4) * 2 + lax.rem(core + dc, 2)) * 4 + lax.rem(x + 4 - dx, 4)
                label_row = label_row + jnp.where(theirs > mine, 64.0, 0.0)
                here = label_col == label_row
                if n == 0:
                    here = here & (
                        lax.broadcasted_iota(jnp.int32, (rows, LANES), 1)
                        <= lax.broadcasted_iota(jnp.int32, (rows, LANES), 0)
                    )
                allowed.append(here)
    scores = lax.dot_general(q, k_ref[...], NT, preferred_element_type=F32)
    out = softmax_rows(scores, jnp.concatenate(allowed, axis=1), scale, v_ref[...])
    o_ref[...] = out.reshape(4, 3, COLD, hd)
    for d, ref in enumerate((o0_ref, o1_ref, o2_ref, o3_ref)):
        ref[...] = o_ref[lax.rem(y + 4 - d, 4)].astype(BF16)


def unpack_kernel(at_ref, cols_ref, back_ref, o0_ref, o1_ref, o2_ref, o3_ref, out_ref, hot_ref):
    devices, heads, _, hd = back_ref.shape
    tokens = cols_ref.shape[0]
    slots = devices * COLD
    part = 256
    for d, ref in enumerate((o0_ref, o1_ref, o2_ref, o3_ref)):
        hot_ref[d] = ref[...].astype(F32)
    for h in range(heads):
        rows = back_ref[:, h].astype(F32).reshape(slots, hd).astype(BF16)
        hot = hot_ref[lax.rem(h + 4 - at_ref[0], 4)].reshape(HOT, hd)
        hot = jnp.concatenate([hot, jnp.zeros((LANES - HOT, hd), F32)], axis=0).astype(BF16)
        for c in range(tokens // part):
            slot = cols_ref[c * part : (c + 1) * part, 8 + h : 9 + h].astype(jnp.int32)
            place = (slot == lax.broadcasted_iota(jnp.int32, (part, slots), 1)).astype(BF16)
            hot_place = (
                slot == lax.broadcasted_iota(jnp.int32, (part, LANES), 1) + slots
            ).astype(BF16)
            got = jnp.dot(place, rows, preferred_element_type=F32) + jnp.dot(
                hot_place, hot, preferred_element_type=F32
            )
            out_ref[c * part : (c + 1) * part, h * hd : (h + 1) * hd] = got.astype(BF16)


def vmem(count):
    return [pl.BlockSpec(memory_space=pltpu.VMEM)] * count


SMEM = [pl.BlockSpec(memory_space=pltpu.SMEM)]
PARAMS = pltpu.CompilerParams(vmem_limit_bytes=VMEM_LIMIT)
AXES = ("z", "core", "x", "y")


def call(kernel, name, outs, scratch, scalars, *arrays):
    return pl.pallas_call(
        kernel,
        out_shape=tuple(jax.ShapeDtypeStruct(*out) for out in outs),
        in_specs=(SMEM if scalars is not None else []) + vmem(len(arrays)),
        out_specs=tuple(vmem(len(outs))),
        scratch_shapes=[pltpu.VMEM(*one) for one in scratch],
        compiler_params=PARAMS,
        name=name,
    )(*([scalars] if scalars is not None else []), *arrays)


def shift(block, axis, by):
    size = lax.axis_size(axis)
    return lax.ppermute(block, axis, [(i, (i + by) % size) for i in range(size)])


def local(query_rows, key_rows, value_rows, cluster_ids):
    devices = lax.axis_size(AXES)
    heads, tokens = cluster_ids.shape
    hd = query_rows.shape[1] // heads
    at = jnp.stack([lax.axis_index(a).astype(jnp.int32) for a in ("y", "x", "core", "z")])
    block = ((12, COLD, hd), BF16)
    send, h0, h1, h2, h3, cols = call(
        pack_kernel,
        "pack",
        [((devices, 3 * heads + 1, COLD, hd), BF16)] + [block] * 4 + [((tokens, LANES), F32)],
        [((tokens, 3 * hd + LANES), BF16), ((heads, 12, COLD, hd), BF16)],
        at, cluster_ids, query_rows, key_rows, value_rows,
    )
    got = lax.all_to_all(send, AXES, split_axis=0, concat_axis=0, tiled=True)
    near = [h0] + [shift(b, "y", d + 1) for d, b in enumerate((h1, h2, h3))]
    hot_q, kv = call(
        mid_kernel, "mid", [((24, COLD, hd), BF16), ((25, COLD, hd), BF16)], [((4, 12, COLD, hd), F32)],
        at, *near,
    )
    for axis in ("x", "z"):
        kv = jnp.concatenate([kv] + [shift(kv, axis, d) for d in (1, 2, 3)], axis=0)
    far = shift(kv, "core", 1)
    outs = call(
        hot_kernel, "hot", [((3, COLD, hd), BF16)] * 4,
        [((32 * LANES, hd), BF16), ((32 * LANES, hd), BF16), ((4, 3, COLD, hd), F32)],
        at, hot_q, kv, far,
    )
    hot_out = [outs[0]] + [shift(b, "y", 3 - d) for d, b in enumerate(outs[1:])]
    (answer,) = call(cold_kernel, "cold", [((devices, heads, COLD, hd), BF16)], [], None, got)
    back = lax.all_to_all(answer, AXES, split_axis=0, concat_axis=0, tiled=True)
    (result,) = call(
        unpack_kernel, "unpack", [((tokens, heads * hd), BF16)], [((4, 3, COLD, hd), F32)],
        at, cols, back, *hot_out,
    )
    return result


def solution(mesh):
    split = jax.sharding.Mesh(mesh.devices.reshape(4, 2, 4, 4), AXES)
    return jax.shard_map(
        local,
        mesh=split,
        in_specs=(P(AXES, None), P(AXES, None), P(AXES, None), P(None, AXES)),
        out_specs=P(AXES, None),
        check_vma=False,
    )
```

```python
import jax
import jax.numpy as jnp
from jax import lax
from jax.experimental import pallas as pl
from jax.experimental.pallas import tpu as pltpu
from jax.sharding import PartitionSpec as P

CL_DEV = 8
COLD = 8
HOT = 24
HOT_PAD = 32
LANES = 128
NEG_FILL = -1e30
LOG2E = 1.4426950408889634
F32 = jnp.float32
BF16 = jnp.bfloat16


def load_heads(q_hbm, k_hbm, v_hbm, x_ref, sems):
    heads = x_ref.shape[0]
    hd = q_hbm.shape[1] // heads
    copies = []
    for h in range(heads):
        copies.append([
            pltpu.make_async_copy(
                src.at[:, h * hd : (h + 1) * hd],
                x_ref.at[h, :, j * hd : (j + 1) * hd],
                sems.at[3 * h + j],
            )
            for j, src in enumerate((q_hbm, k_hbm, v_hbm))
        ])
        for one in copies[h]:
            one.start()
    return copies


def columns_of(table):
    tokens = table.shape[1]
    return jnp.transpose(
        jnp.concatenate([table, jnp.zeros((LANES - table.shape[0], tokens), F32)], axis=0)
    )


def rank_kernel(
    at_ref, ids_ref, q_hbm, k_hbm, v_hbm, table_ref, h0_ref, h1_ref, h2_ref, h3_ref, x_ref, hot_ref, sems
):
    heads, tokens = ids_ref.shape
    hd = q_hbm.shape[1] // heads
    devices = tokens // COLD
    slots = devices * COLD
    step = 256
    copies = load_heads(q_hbm, k_hbm, v_hbm, x_ref, sems)
    ids = ids_ref[...]
    owner = ids // CL_DEV
    lid = ids - owner * CL_DEV
    upper = (
        lax.broadcasted_iota(jnp.int32, (step, step), 0)
        < lax.broadcasted_iota(jnp.int32, (step, step), 1)
    ).astype(BF16)
    dev_col = lax.broadcasted_iota(jnp.int32, (devices, step), 0)
    slot_rows = []
    for h in range(heads):
        carry = jnp.zeros((devices, 1), F32)
        ones, ranks = [], []
        for b in range(tokens // step):
            one = (owner[h : h + 1, b * step : (b + 1) * step] == dev_col).astype(F32)
            inside = jnp.dot(one.astype(BF16), upper, preferred_element_type=F32) + carry
            carry = carry + jnp.sum(one, axis=1, keepdims=True)
            ones.append(one)
            ranks.append(jnp.sum(one * inside, axis=0, keepdims=True))
        full = (carry > COLD).astype(F32)
        is_hot = jnp.concatenate(
            [jnp.sum(one * full, axis=0, keepdims=True) for one in ones], axis=1
        )
        rank = jnp.concatenate(ranks, axis=1).astype(jnp.int32)
        slot_rows.append(jnp.where(is_hot > 0.5, slots + rank, owner[h : h + 1] * COLD + rank))
    slot_all = jnp.concatenate(slot_rows, axis=0)
    table = jnp.concatenate([slot_all.astype(F32), (lid + 1).astype(F32)], axis=0)
    table_ref[...] = table
    label_cols = columns_of(table).astype(BF16)
    for h in range(heads):
        place = (
            slot_all[h : h + 1] == lax.broadcasted_iota(jnp.int32, (HOT_PAD, tokens), 0) + slots
        ).astype(BF16)
        tags = jnp.dot(place, label_cols, preferred_element_type=F32)
        tags = jnp.broadcast_to(tags[:HOT, heads + h : heads + h + 1], (HOT, hd))
        for one in copies[h]:
            one.wait()
        moved = jnp.dot(place, x_ref[h], preferred_element_type=F32)
        for j in range(3):
            hot_ref[h, 3 * j : 3 * j + 3] = (
                moved[:HOT, j * hd : (j + 1) * hd].reshape(3, COLD, hd).astype(BF16)
            )
        hot_ref[h, 9:12] = tags.reshape(3, COLD, hd).astype(BF16)
    for d, ref in enumerate((h0_ref, h1_ref, h2_ref, h3_ref)):
        ref[...] = hot_ref[lax.rem(at_ref[0] + d, heads)]


def pack_kernel(table_ref, q_hbm, k_hbm, v_hbm, send_hbm, x_ref, e_ref, send_ref, sems, out_sems):
    heads = x_ref.shape[0]
    tokens = table_ref.shape[1]
    hd = q_hbm.shape[1] // heads
    devices = send_ref.shape[0]
    slots = devices * COLD
    part = 256
    copies = load_heads(q_hbm, k_hbm, v_hbm, x_ref, sems)
    cols = columns_of(table_ref[...])
    lane = lax.broadcasted_iota(jnp.int32, (tokens, LANES), 1)
    for h in range(heads):
        e_ref[h] = jnp.where(lane == heads + h, cols, 0.0).astype(BF16)
    label_parts = [jnp.zeros((part, LANES), F32) for _ in range(slots // part)]
    sent = []
    for h in range(heads):
        slot_row = table_ref[h : h + 1].astype(jnp.int32)
        for one in copies[h]:
            one.wait()
        rows = jnp.concatenate([x_ref[h], e_ref[h]], axis=1)
        for c in range(slots // part):
            place = (
                slot_row == lax.broadcasted_iota(jnp.int32, (part, tokens), 0) + c * part
            ).astype(BF16)
            moved = jnp.dot(place, rows, preferred_element_type=F32)
            devs = slice(c * part // COLD, (c + 1) * part // COLD)
            for j in range(3):
                send_ref[devs, 3 * h + j] = (
                    moved[:, j * hd : (j + 1) * hd].reshape(part // COLD, COLD, hd).astype(BF16)
                )
            label_parts[c] = label_parts[c] + moved[:, 3 * hd :]
            if h == heads - 1:
                send_ref[devs, 3 * heads] = (
                    label_parts[c].reshape(part // COLD, COLD, LANES).astype(BF16)
                )
        last = 3 * h + 3 + (h == heads - 1)
        out = pltpu.make_async_copy(
            send_ref.at[:, 3 * h : last], send_hbm.at[:, 3 * h : last], out_sems.at[h]
        )
        out.start()
        sent.append(out)
    for out in sent:
        out.wait()


def softmax_rows(scores, allowed, scale, values):
    masked = jnp.where(allowed, scores, NEG_FILL)
    top = jnp.max(masked, axis=1, keepdims=True)
    weights = jnp.exp2((masked - top) * scale)
    total = jnp.sum(weights, axis=1, keepdims=True)
    out = jnp.dot(weights.astype(BF16), values, preferred_element_type=F32)
    return out / total


NT = (((1,), (1,)), ((), ()))


def cold_kernel(got_hbm, out_hbm, got_ref, out_ref, sems, out_sems):
    devices, tiles, _, hd = got_ref.shape
    heads = tiles // 3
    slots = devices * COLD
    scale = hd ** (-0.5) * LOG2E
    ranges = [slice(3 * heads, 3 * heads + 1)] + [slice(3 * h, 3 * h + 3) for h in range(heads)]
    loads = [
        pltpu.make_async_copy(got_hbm.at[:, r], got_ref.at[:, r], sems.at[i])
        for i, r in enumerate(ranges)
    ]
    for load in loads:
        load.start()
    loads[0].wait()
    labels = got_ref[:, 3 * heads].astype(F32).reshape(slots, hd)
    label_rows = jnp.transpose(labels)
    part = 256
    causal = lax.broadcasted_iota(jnp.int32, (part, part), 1) <= lax.broadcasted_iota(
        jnp.int32, (part, part), 0
    )
    sent = []
    for h in range(heads):
        loads[1 + h].wait()
        q, k, v = (
            got_ref[:, 3 * h + j].astype(F32).reshape(slots, hd).astype(BF16) for j in range(3)
        )
        row = label_rows[heads + h : heads + h + 1]
        for c in range(slots // part):
            stop = (c + 1) * part
            col = labels[c * part : stop, heads + h : heads + h + 1]
            scores = lax.dot_general(
                q[c * part : stop], k[:stop], NT, preferred_element_type=F32
            )
            allowed = col == row[:, :stop]
            last = allowed[:, c * part :] & causal
            allowed = last if c == 0 else jnp.concatenate([allowed[:, : c * part], last], axis=1)
            out = softmax_rows(scores, allowed, scale, v[:stop])
            devs = slice(c * part // COLD, stop // COLD)
            out_ref[devs, h] = out.reshape(part // COLD, COLD, hd).astype(BF16)
        out = pltpu.make_async_copy(out_ref.at[:, h], out_hbm.at[:, h], out_sems.at[h])
        out.start()
        sent.append(out)
    for out in sent:
        out.wait()


def mid_kernel(at_ref, b0_ref, b1_ref, b2_ref, b3_ref, q_ref, kv_ref, all_ref):
    hd = q_ref.shape[-1]
    for d, ref in enumerate((b0_ref, b1_ref, b2_ref, b3_ref)):
        all_ref[lax.rem(at_ref[0] - d + 4, 4)] = ref[...].astype(F32)
    rows = 4 * HOT
    blocks = [all_ref[:, 3 * j : 3 * j + 3] for j in range(4)]
    labels = blocks[3].reshape(rows, hd)
    q_ref[0:12] = blocks[0].reshape(12, COLD, hd).astype(BF16)
    q_ref[12:24] = blocks[3].reshape(12, COLD, hd).astype(BF16)
    kv_ref[0:12] = blocks[1].reshape(12, COLD, hd).astype(BF16)
    kv_ref[12:24] = blocks[2].reshape(12, COLD, hd).astype(BF16)
    flat = jnp.transpose(jnp.concatenate([labels, jnp.zeros((LANES - rows, hd), F32)], axis=0))
    kv_ref[24] = flat[:COLD].astype(BF16)


def hot_kernel(at_ref, q_ref, near_ref, far_ref, o0_ref, o1_ref, o2_ref, o3_ref, k_ref, v_ref, o_ref):
    hd = q_ref.shape[-1]
    rows = 4 * HOT
    scale = hd ** (-0.5) * LOG2E
    y, x, core, z = (at_ref[i] for i in range(4))
    mine = (z * 2 + core) * 4 + x
    q = q_ref[0:12].astype(F32).reshape(rows, hd).astype(BF16)
    label_col = q_ref[12:24].astype(F32).reshape(rows, hd)[:, 0:1]
    zeros = jnp.zeros((LANES - rows, hd), F32)
    allowed = []
    for dc, ref in enumerate((near_ref, far_ref)):
        for dz in range(4):
            for dx in range(4):
                n = (dc * 4 + dz) * 4 + dx
                tile = 25 * (dz * 4 + dx)
                at = slice(n * LANES, (n + 1) * LANES)
                for dst_ref, first in ((k_ref, 0), (v_ref, 12)):
                    block = ref[tile + first : tile + first + 12].astype(F32).reshape(rows, hd)
                    dst_ref[at] = jnp.concatenate([block, zeros], axis=0).astype(BF16)
                label_row = ref[tile + 24].astype(F32)[0:1]
                theirs = (lax.rem(z + 4 - dz, 4) * 2 + lax.rem(core + dc, 2)) * 4 + lax.rem(x + 4 - dx, 4)
                label_row = label_row + jnp.where(theirs > mine, 64.0, 0.0)
                here = label_col == label_row
                if n == 0:
                    here = here & (
                        lax.broadcasted_iota(jnp.int32, (rows, LANES), 1)
                        <= lax.broadcasted_iota(jnp.int32, (rows, LANES), 0)
                    )
                allowed.append(here)
    scores = lax.dot_general(q, k_ref[...], NT, preferred_element_type=F32)
    out = softmax_rows(scores, jnp.concatenate(allowed, axis=1), scale, v_ref[...])
    o_ref[...] = out.reshape(4, 3, COLD, hd)
    for d, ref in enumerate((o0_ref, o1_ref, o2_ref, o3_ref)):
        ref[...] = o_ref[lax.rem(y + 4 - d, 4)].astype(BF16)


def unpack_kernel(at_ref, table_ref, back_ref, o0_ref, o1_ref, o2_ref, o3_ref, out_ref, hot_ref):
    devices, heads, _, hd = back_ref.shape
    tokens = table_ref.shape[1]
    cols = columns_of(table_ref[...])
    slots = devices * COLD
    part = 256
    for d, ref in enumerate((o0_ref, o1_ref, o2_ref, o3_ref)):
        hot_ref[d] = ref[...].astype(F32)
    for h in range(heads):
        rows = back_ref[:, h].astype(F32).reshape(slots, hd).astype(BF16)
        hot = hot_ref[lax.rem(h + 4 - at_ref[0], 4)].reshape(HOT, hd)
        hot = jnp.concatenate([hot, jnp.zeros((LANES - HOT, hd), F32)], axis=0).astype(BF16)
        for c in range(tokens // part):
            slot = cols[c * part : (c + 1) * part, h : h + 1].astype(jnp.int32)
            place = (slot == lax.broadcasted_iota(jnp.int32, (part, slots), 1)).astype(BF16)
            hot_place = (
                slot == lax.broadcasted_iota(jnp.int32, (part, LANES), 1) + slots
            ).astype(BF16)
            got = jnp.dot(place, rows, preferred_element_type=F32) + jnp.dot(
                hot_place, hot, preferred_element_type=F32
            )
            out_ref[c * part : (c + 1) * part, h * hd : (h + 1) * hd] = got.astype(BF16)


SMEM = pl.BlockSpec(memory_space=pltpu.SMEM)
VMEM = pl.BlockSpec(memory_space=pltpu.VMEM)
HBM = pl.BlockSpec(memory_space=pltpu.HBM)
AXES = ("z", "core", "x", "y")
MIB = 1024 * 1024


def call(kernel, name, limit, ins, outs, scratch, *arrays):
    return pl.pallas_call(
        kernel,
        out_shape=tuple(jax.ShapeDtypeStruct(*out[1:]) for out in outs),
        in_specs=ins,
        out_specs=tuple(out[0] for out in outs),
        scratch_shapes=scratch,
        compiler_params=pltpu.CompilerParams(vmem_limit_bytes=limit * MIB),
        name=name,
    )(*arrays)


def shift(block, axis, by):
    size = lax.axis_size(axis)
    return lax.ppermute(block, axis, [(i, (i + by) % size) for i in range(size)])


def local(query_rows, key_rows, value_rows, cluster_ids):
    devices = lax.axis_size(AXES)
    heads, tokens = cluster_ids.shape
    hd = query_rows.shape[1] // heads
    at = jnp.stack([lax.axis_index(a).astype(jnp.int32) for a in ("y", "x", "core", "z")])
    tile = (COLD, hd)
    x_scratch = pltpu.VMEM((heads, tokens, 3 * hd), BF16)
    x_sems = pltpu.SemaphoreType.DMA((3 * heads,))
    table, h0, h1, h2, h3 = call(
        rank_kernel, "rank", 58, [SMEM, VMEM, HBM, HBM, HBM],
        [(VMEM, (2 * heads, tokens), F32)] + [(VMEM, (12, *tile), BF16)] * 4,
        [x_scratch, pltpu.VMEM((heads, 12, *tile), BF16), x_sems],
        at, cluster_ids, query_rows, key_rows, value_rows,
    )
    near = [h0] + [shift(b, "y", d + 1) for d, b in enumerate((h1, h2, h3))]
    (send,) = call(
        pack_kernel, "pack", 58, [VMEM, HBM, HBM, HBM],
        [(HBM, (devices, 3 * heads + 1, *tile), BF16)],
        [
            x_scratch, pltpu.VMEM((heads, tokens, LANES), BF16),
            pltpu.VMEM((devices, 3 * heads + 1, *tile), BF16), x_sems,
            pltpu.SemaphoreType.DMA((heads,)),
        ],
        table, query_rows, key_rows, value_rows,
    )
    send, near = lax.optimization_barrier((send, near))
    got = lax.all_to_all(send, AXES, split_axis=0, concat_axis=0, tiled=True)
    hot_q, kv = call(
        mid_kernel, "mid", 24, [SMEM] + [VMEM] * 4,
        [(VMEM, (24, *tile), BF16), (VMEM, (25, *tile), BF16)],
        [pltpu.VMEM((4, 12, *tile), F32)],
        at, *near,
    )
    kv = jnp.concatenate([kv] + [shift(kv, "x", d) for d in (1, 2, 3)], axis=0)
    along_z = [kv] + [shift(kv, "z", d) for d in (1, 2, 3)]
    (answer,) = call(
        cold_kernel, "cold", 58, [HBM], [(HBM, (devices, heads, *tile), BF16)],
        [
            pltpu.VMEM((devices, 3 * heads + 1, *tile), BF16), pltpu.VMEM((devices, heads, *tile), BF16),
            pltpu.SemaphoreType.DMA((heads + 1,)), pltpu.SemaphoreType.DMA((heads,)),
        ],
        got,
    )
    along_z, _ = lax.optimization_barrier((along_z, answer))
    kv = jnp.concatenate(along_z, axis=0)
    far = shift(kv, "core", 1)
    outs = call(
        hot_kernel, "hot", 24, [SMEM] + [VMEM] * 3, [(VMEM, (3, *tile), BF16)] * 4,
        [
            pltpu.VMEM((32 * LANES, hd), BF16), pltpu.VMEM((32 * LANES, hd), BF16),
            pltpu.VMEM((4, 3, *tile), F32),
        ],
        at, hot_q, kv, far,
    )
    hot_out = [outs[0]] + [shift(b, "y", 3 - d) for d, b in enumerate(outs[1:])]
    back = lax.all_to_all(answer, AXES, split_axis=0, concat_axis=0, tiled=True)
    (result,) = call(
        unpack_kernel, "unpack", 24, [SMEM] + [VMEM] * 6, [(VMEM, (tokens, heads * hd), BF16)],
        [pltpu.VMEM((4, 3, *tile), F32)],
        at, table, back, *hot_out,
    )
    return result


def solution(mesh):
    split = jax.sharding.Mesh(mesh.devices.reshape(4, 2, 4, 4), AXES)
    return jax.shard_map(
        local,
        mesh=split,
        in_specs=(P(AXES, None), P(AXES, None), P(AXES, None), P(None, AXES)),
        out_specs=P(AXES, None),
        check_vma=False,
    )
```

```python
import jax
import jax.numpy as jnp
from jax import lax
from jax.experimental import pallas as pl
from jax.experimental.pallas import tpu as pltpu
from jax.sharding import PartitionSpec as P

CL_DEV = 8
COLD = 8
HOT = 24
HOT_PAD = 32
LANES = 128
NEG_FILL = -1e30
TAGS = 16
MARK = 128.0
LOG2E = 1.4426950408889634
F32 = jnp.float32
BF16 = jnp.bfloat16


def load_heads(q_hbm, k_hbm, v_hbm, x_ref, sems):
    heads = x_ref.shape[0]
    hd = q_hbm.shape[1] // heads
    copies = []
    for h in range(heads):
        copies.append([
            pltpu.make_async_copy(
                src.at[:, h * hd : (h + 1) * hd],
                x_ref.at[h, :, j * hd : (j + 1) * hd],
                sems.at[3 * h + j],
            )
            for j, src in enumerate((q_hbm, k_hbm, v_hbm))
        ])
        for one in copies[h]:
            one.start()
    return copies


def columns_of(table):
    tokens = table.shape[1]
    return jnp.transpose(
        jnp.concatenate([table, jnp.zeros((LANES - table.shape[0], tokens), F32)], axis=0)
    )


def rank_kernel(
    ids_ref, q_hbm, k_hbm, v_hbm, table_ref, h0_ref, h1_ref, h2_ref, h3_ref, x_ref, hot_ref, sems
):
    heads, tokens = ids_ref.shape
    hd = q_hbm.shape[1] // heads
    devices = tokens // COLD
    slots = devices * COLD
    step = 256
    copies = load_heads(q_hbm, k_hbm, v_hbm, x_ref, sems)
    ids = ids_ref[...]
    owner = ids // CL_DEV
    lid = ids - owner * CL_DEV
    upper = (
        lax.broadcasted_iota(jnp.int32, (step, step), 0)
        < lax.broadcasted_iota(jnp.int32, (step, step), 1)
    ).astype(BF16)
    dev_col = lax.broadcasted_iota(jnp.int32, (devices, step), 0)
    slot_rows = []
    for h in range(heads):
        carry = jnp.zeros((devices, 1), F32)
        ones, ranks = [], []
        for b in range(tokens // step):
            one = (owner[h : h + 1, b * step : (b + 1) * step] == dev_col).astype(F32)
            inside = jnp.dot(one.astype(BF16), upper, preferred_element_type=F32) + carry
            carry = carry + jnp.sum(one, axis=1, keepdims=True)
            ones.append(one)
            ranks.append(jnp.sum(one * inside, axis=0, keepdims=True))
        full = (carry > COLD).astype(F32)
        is_hot = jnp.concatenate(
            [jnp.sum(one * full, axis=0, keepdims=True) for one in ones], axis=1
        )
        rank = jnp.concatenate(ranks, axis=1).astype(jnp.int32)
        slot_rows.append(jnp.where(is_hot > 0.5, slots + rank, owner[h : h + 1] * COLD + rank))
    slot_all = jnp.concatenate(slot_rows, axis=0)
    table = jnp.concatenate([slot_all.astype(F32), (lid + 1).astype(F32)], axis=0)
    table_ref[...] = table
    label_cols = columns_of(table).astype(BF16)
    for h in range(heads):
        place = (
            slot_all[h : h + 1] == lax.broadcasted_iota(jnp.int32, (HOT_PAD, tokens), 0) + slots
        ).astype(BF16)
        tags = jnp.dot(place, label_cols, preferred_element_type=F32)
        tags = jnp.broadcast_to(tags[:HOT, heads + h : heads + h + 1], (HOT, hd))
        for one in copies[h]:
            one.wait()
        moved = jnp.dot(place, x_ref[h], preferred_element_type=F32)
        for j in range(3):
            hot_ref[h, 3 * j : 3 * j + 3] = (
                moved[:HOT, j * hd : (j + 1) * hd].reshape(3, COLD, hd).astype(BF16)
            )
        hot_ref[h, 9:12] = tags.reshape(3, COLD, hd).astype(BF16)
    y = lax.axis_index("y")
    for d, ref in enumerate((h0_ref, h1_ref, h2_ref, h3_ref)):
        ref[...] = hot_ref[lax.rem(y + d, heads)]


def pack_kernel(table_ref, q_hbm, k_hbm, v_hbm, send_hbm, x_ref, e_ref, send_ref, sems, out_sems):
    heads = x_ref.shape[0]
    tokens = table_ref.shape[1]
    hd = q_hbm.shape[1] // heads
    devices = send_ref.shape[0]
    slots = devices * COLD
    part = 256
    copies = load_heads(q_hbm, k_hbm, v_hbm, x_ref, sems)
    tag = lax.broadcasted_iota(jnp.int32, (TAGS, tokens), 0) + 1
    marks = [
        jnp.where(table_ref[heads + h : heads + h + 1].astype(jnp.int32) == tag, MARK, 0.0)
        for h in range(heads)
    ]
    cols = columns_of(jnp.concatenate(marks, axis=0))
    lane = lax.broadcasted_iota(jnp.int32, (tokens, LANES), 1) // TAGS
    for h in range(heads):
        e_ref[h] = jnp.where(lane == h, cols, 0.0).astype(BF16)
    label_parts = [jnp.zeros((part, LANES), F32) for _ in range(slots // part)]
    sent = []
    for h in range(heads):
        slot_row = table_ref[h : h + 1].astype(jnp.int32)
        for one in copies[h]:
            one.wait()
        rows = jnp.concatenate([x_ref[h], e_ref[h]], axis=1)
        for c in range(slots // part):
            place = (
                slot_row == lax.broadcasted_iota(jnp.int32, (part, tokens), 0) + c * part
            ).astype(BF16)
            moved = jnp.dot(place, rows, preferred_element_type=F32)
            devs = slice(c * part // COLD, (c + 1) * part // COLD)
            for j in range(3):
                send_ref[devs, 3 * h + j] = (
                    moved[:, j * hd : (j + 1) * hd].reshape(part // COLD, COLD, hd).astype(BF16)
                )
            label_parts[c] = label_parts[c] + moved[:, 3 * hd :]
            if h == heads - 1:
                send_ref[devs, 3 * heads] = (
                    label_parts[c].reshape(part // COLD, COLD, LANES).astype(BF16)
                )
        last = 3 * h + 3 + (h == heads - 1)
        out = pltpu.make_async_copy(
            send_ref.at[:, 3 * h : last], send_hbm.at[:, 3 * h : last], out_sems.at[h]
        )
        out.start()
        sent.append(out)
    for out in sent:
        out.wait()


def softmax_rows(scores, allowed, scale, values):
    masked = jnp.where(allowed, scores, NEG_FILL)
    top = jnp.max(masked, axis=1, keepdims=True)
    weights = jnp.exp2((masked - top) * scale)
    total = jnp.sum(weights, axis=1, keepdims=True)
    out = jnp.dot(weights.astype(BF16), values, preferred_element_type=F32)
    return out / total


NT = (((1,), (1,)), ((), ()))


def cold_kernel(got_hbm, out_hbm, got_ref, out_ref, sems, out_sems):
    devices, tiles, _, hd = got_ref.shape
    heads = tiles // 3
    slots = devices * COLD
    scale = hd ** (-0.5) * LOG2E
    ranges = [slice(3 * heads, 3 * heads + 1)] + [slice(3 * h, 3 * h + 3) for h in range(heads)]
    loads = [
        pltpu.make_async_copy(got_hbm.at[:, r], got_ref.at[:, r], sems.at[i])
        for i, r in enumerate(ranges)
    ]
    for load in loads:
        load.start()
    loads[0].wait()
    marks = got_ref[:, 3 * heads].astype(F32).reshape(slots, hd)
    lane = lax.broadcasted_iota(jnp.int32, (slots, hd), 1) // TAGS
    key_marks = marks.astype(BF16)
    part = 256
    causal = lax.broadcasted_iota(jnp.int32, (part, part), 1) <= lax.broadcasted_iota(
        jnp.int32, (part, part), 0
    )
    ones = jnp.ones((slots, hd), BF16)
    sent = []
    for h in range(heads):
        query_marks = jnp.where(lane == h, marks, 0.0).astype(BF16)
        loads[1 + h].wait()
        q, k, v = (
            got_ref[:, 3 * h + j].astype(F32).reshape(slots, hd).astype(BF16) for j in range(3)
        )
        q = jnp.concatenate([q, query_marks], axis=1)
        k = jnp.concatenate([k, key_marks], axis=1)
        v = jnp.concatenate([v, ones], axis=1)
        for c in range(slots // part):
            stop = (c + 1) * part
            scores = lax.dot_general(
                q[c * part : stop], k[:stop], NT, preferred_element_type=F32
            )
            last = jnp.where(causal, scores[:, c * part :], NEG_FILL)
            if c > 0:
                last = jnp.concatenate([scores[:, : c * part], last], axis=1)
            top = jnp.max(last, axis=1, keepdims=True)
            weights = jnp.exp2(last * scale - top * scale).astype(BF16)
            out = jnp.dot(weights, v[:stop], preferred_element_type=F32)
            out = out[:, :hd] / out[:, hd:]
            devs = slice(c * part // COLD, stop // COLD)
            out_ref[devs, h] = out.reshape(part // COLD, COLD, hd).astype(BF16)
        out = pltpu.make_async_copy(out_ref.at[:, h], out_hbm.at[:, h], out_sems.at[h])
        out.start()
        sent.append(out)
    for out in sent:
        out.wait()


def mid_kernel(b0_ref, b1_ref, b2_ref, b3_ref, q_ref, kv_ref, all_ref):
    hd = q_ref.shape[-1]
    y = lax.axis_index("y")
    for d, ref in enumerate((b0_ref, b1_ref, b2_ref, b3_ref)):
        all_ref[lax.rem(y + 4 - d, 4)] = ref[...].astype(F32)
    rows = 4 * HOT
    blocks = [all_ref[:, 3 * j : 3 * j + 3] for j in range(4)]
    labels = blocks[3].reshape(rows, hd)
    q_ref[0:12] = blocks[0].reshape(12, COLD, hd).astype(BF16)
    q_ref[12:24] = blocks[3].reshape(12, COLD, hd).astype(BF16)
    kv_ref[0:12] = blocks[1].reshape(12, COLD, hd).astype(BF16)
    kv_ref[12:24] = blocks[2].reshape(12, COLD, hd).astype(BF16)
    flat = jnp.transpose(jnp.concatenate([labels, jnp.zeros((LANES - rows, hd), F32)], axis=0))
    kv_ref[24] = flat[:COLD].astype(BF16)


def hot_kernel(q_ref, near_ref, far_ref, o0_ref, o1_ref, o2_ref, o3_ref, k_ref, v_ref, o_ref):
    hd = q_ref.shape[-1]
    rows = 4 * HOT
    scale = hd ** (-0.5) * LOG2E
    y, x, core, z = (lax.axis_index(a) for a in ("y", "x", "core", "z"))
    mine = (z * 2 + core) * 4 + x
    q = q_ref[0:12].astype(F32).reshape(rows, hd).astype(BF16)
    label_col = q_ref[12:24].astype(F32).reshape(rows, hd)[:, 0:1]
    zeros = jnp.zeros((LANES - rows, hd), F32)
    allowed = []
    for dc, ref in enumerate((near_ref, far_ref)):
        for dz in range(4):
            for dx in range(4):
                n = (dc * 4 + dz) * 4 + dx
                tile = 25 * (dz * 4 + dx)
                at = slice(n * LANES, (n + 1) * LANES)
                for dst_ref, first in ((k_ref, 0), (v_ref, 12)):
                    block = ref[tile + first : tile + first + 12].astype(F32).reshape(rows, hd)
                    dst_ref[at] = jnp.concatenate([block, zeros], axis=0).astype(BF16)
                label_row = ref[tile + 24].astype(F32)[0:1]
                theirs = (lax.rem(z + 4 - dz, 4) * 2 + lax.rem(core + dc, 2)) * 4 + lax.rem(x + 4 - dx, 4)
                label_row = label_row + jnp.where(theirs > mine, 64.0, 0.0)
                here = label_col == label_row
                if n == 0:
                    here = here & (
                        lax.broadcasted_iota(jnp.int32, (rows, LANES), 1)
                        <= lax.broadcasted_iota(jnp.int32, (rows, LANES), 0)
                    )
                allowed.append(here)
    scores = lax.dot_general(q, k_ref[...], NT, preferred_element_type=F32)
    out = softmax_rows(scores, jnp.concatenate(allowed, axis=1), scale, v_ref[...])
    o_ref[...] = out.reshape(4, 3, COLD, hd)
    for d, ref in enumerate((o0_ref, o1_ref, o2_ref, o3_ref)):
        ref[...] = o_ref[lax.rem(y + 4 - d, 4)].astype(BF16)


def unpack_kernel(table_ref, back_ref, o0_ref, o1_ref, o2_ref, o3_ref, out_ref, hot_ref):
    devices, heads, _, hd = back_ref.shape
    tokens = table_ref.shape[1]
    cols = columns_of(table_ref[...])
    slots = devices * COLD
    part = 256
    for d, ref in enumerate((o0_ref, o1_ref, o2_ref, o3_ref)):
        hot_ref[d] = ref[...].astype(F32)
    for h in range(heads):
        rows = back_ref[:, h].astype(F32).reshape(slots, hd).astype(BF16)
        hot = hot_ref[lax.rem(h + 4 - lax.axis_index("y"), 4)].reshape(HOT, hd)
        hot = jnp.concatenate([hot, jnp.zeros((LANES - HOT, hd), F32)], axis=0).astype(BF16)
        for c in range(tokens // part):
            slot = cols[c * part : (c + 1) * part, h : h + 1].astype(jnp.int32)
            place = (slot == lax.broadcasted_iota(jnp.int32, (part, slots), 1)).astype(BF16)
            hot_place = (
                slot == lax.broadcasted_iota(jnp.int32, (part, LANES), 1) + slots
            ).astype(BF16)
            got = jnp.dot(place, rows, preferred_element_type=F32) + jnp.dot(
                hot_place, hot, preferred_element_type=F32
            )
            out_ref[c * part : (c + 1) * part, h * hd : (h + 1) * hd] = got.astype(BF16)


VMEM = pl.BlockSpec(memory_space=pltpu.VMEM)
HBM = pl.BlockSpec(memory_space=pltpu.HBM)
AXES = ("z", "core", "x", "y")
MIB = 1024 * 1024


def call(kernel, name, limit, ins, outs, scratch, *arrays):
    return pl.pallas_call(
        kernel,
        out_shape=tuple(jax.ShapeDtypeStruct(*out[1:]) for out in outs),
        in_specs=ins,
        out_specs=tuple(out[0] for out in outs),
        scratch_shapes=scratch,
        compiler_params=pltpu.CompilerParams(vmem_limit_bytes=limit * MIB),
        name=name,
    )(*arrays)


def shift(block, axis, by):
    size = lax.axis_size(axis)
    return lax.ppermute(block, axis, [(i, (i + by) % size) for i in range(size)])


def local(query_rows, key_rows, value_rows, cluster_ids):
    devices = lax.axis_size(AXES)
    heads, tokens = cluster_ids.shape
    hd = query_rows.shape[1] // heads
    tile = (COLD, hd)
    x_scratch = pltpu.VMEM((heads, tokens, 3 * hd), BF16)
    x_sems = pltpu.SemaphoreType.DMA((3 * heads,))
    table, h0, h1, h2, h3 = call(
        rank_kernel, "rank", 58, [VMEM, HBM, HBM, HBM],
        [(VMEM, (2 * heads, tokens), F32)] + [(VMEM, (12, *tile), BF16)] * 4,
        [x_scratch, pltpu.VMEM((heads, 12, *tile), BF16), x_sems],
        cluster_ids, query_rows, key_rows, value_rows,
    )
    near = [h0] + [shift(b, "y", d + 1) for d, b in enumerate((h1, h2, h3))]
    (send,) = call(
        pack_kernel, "pack", 58, [VMEM, HBM, HBM, HBM],
        [(HBM, (devices, 3 * heads + 1, *tile), BF16)],
        [
            x_scratch, pltpu.VMEM((heads, tokens, LANES), BF16),
            pltpu.VMEM((devices, 3 * heads + 1, *tile), BF16), x_sems,
            pltpu.SemaphoreType.DMA((heads,)),
        ],
        table, query_rows, key_rows, value_rows,
    )
    send, near = lax.optimization_barrier((send, near))
    got = lax.all_to_all(send, AXES, split_axis=0, concat_axis=0, tiled=True)
    hot_q, kv = call(
        mid_kernel, "mid", 24, [VMEM] * 4,
        [(VMEM, (24, *tile), BF16), (VMEM, (25, *tile), BF16)],
        [pltpu.VMEM((4, 12, *tile), F32)],
        *near,
    )
    kv = jnp.concatenate([kv] + [shift(kv, "x", d) for d in (1, 2, 3)], axis=0)
    blocks = [kv] + [shift(kv, "z", d) for d in (1, 2, 3)]
    (answer,) = call(
        cold_kernel, "cold", 58, [HBM], [(HBM, (devices, heads, *tile), BF16)],
        [
            pltpu.VMEM((devices, 3 * heads + 1, *tile), BF16), pltpu.VMEM((devices, heads, *tile), BF16),
            pltpu.SemaphoreType.DMA((heads + 1,)), pltpu.SemaphoreType.DMA((heads,)),
        ],
        got,
    )
    blocks, _ = lax.optimization_barrier((blocks, answer))
    kv = jnp.concatenate(blocks, axis=0)
    far = shift(kv, "core", 1)
    outs = call(
        hot_kernel, "hot", 24, [VMEM] * 3, [(VMEM, (3, *tile), BF16)] * 4,
        [
            pltpu.VMEM((32 * LANES, hd), BF16), pltpu.VMEM((32 * LANES, hd), BF16),
            pltpu.VMEM((4, 3, *tile), F32),
        ],
        hot_q, kv, far,
    )
    hot_out = [outs[0]] + [shift(b, "y", 3 - d) for d, b in enumerate(outs[1:])]
    back = lax.all_to_all(answer, AXES, split_axis=0, concat_axis=0, tiled=True)
    (result,) = call(
        unpack_kernel, "unpack", 24, [VMEM] * 6, [(VMEM, (tokens, heads * hd), BF16)],
        [pltpu.VMEM((4, 3, *tile), F32)],
        table, back, *hot_out,
    )
    return result


def solution(mesh):
    split = jax.sharding.Mesh(mesh.devices.reshape(4, 2, 4, 4), AXES)
    return jax.shard_map(
        local,
        mesh=split,
        in_specs=(P(AXES, None), P(AXES, None), P(AXES, None), P(None, AXES)),
        out_specs=P(AXES, None),
        check_vma=False,
    )
```

```python
import jax
import jax.numpy as jnp
from jax import lax
from jax.experimental import pallas as pl
from jax.experimental.pallas import tpu as pltpu
from jax.sharding import PartitionSpec as P

CL_DEV = 8
COLD = 8
HOT = 24
HOT_PAD = 32
LANES = 128
NEG_FILL = -1e30
SHARE = 3
HOT_LANE = 64
LOG2E = 1.4426950408889634
F32 = jnp.float32
BF16 = jnp.bfloat16


def iota(shape, dim):
    return lax.broadcasted_iota(jnp.int32, shape, dim)


def columns_of(table):
    tokens = table.shape[1]
    return jnp.transpose(
        jnp.concatenate([table, jnp.zeros((LANES - table.shape[0], tokens), F32)], axis=0)
    )


def pack_kernel(
    ids_ref, q_hbm, k_hbm, v_hbm,
    table_ref, h0_ref, h1_ref, h2_ref, h3_ref, send_hbm,
    q_ref, k_ref, v_ref, x_ref, hot_ref, send_ref, sems, out_sems,
):
    heads, tokens = ids_ref.shape
    hd = q_ref.shape[1] // heads
    devices = send_ref.shape[0]
    slots = devices * COLD
    step = 256
    loads = [
        pltpu.make_async_copy(src, dst, sems.at[j])
        for j, (src, dst) in enumerate(((q_hbm, q_ref), (k_hbm, k_ref), (v_hbm, v_ref)))
    ]
    for load in loads:
        load.start()
    ids = ids_ref[...]
    owner = ids // CL_DEV
    tags = (ids - owner * CL_DEV + 1).astype(F32)
    upper = (iota((step, step), 0) < iota((step, step), 1)).astype(BF16)
    dev_col = iota((devices, step), 0)
    slot_rows, hot_ranks = [], []
    labels = jnp.zeros((devices, LANES), F32)
    for h in range(heads):
        carry = jnp.zeros((devices, 1), F32)
        ones, ranks = [], []
        for b in range(tokens // step):
            one = (owner[h : h + 1, b * step : (b + 1) * step] == dev_col).astype(F32)
            inside = jnp.dot(one.astype(BF16), upper, preferred_element_type=F32) + carry
            carry = carry + jnp.sum(one, axis=1, keepdims=True)
            ones.append(one)
            ranks.append(jnp.sum(one * inside, axis=0, keepdims=True))
        full = (carry > COLD).astype(F32)
        for b, one in enumerate(ones):
            ranks[b] = jnp.where(
                jnp.sum(one * full, axis=0, keepdims=True) > 0.5, ranks[b] + slots, ranks[b]
            )
            lane = jnp.where(ranks[b] < COLD, ranks[b] + COLD * h, -1.0).astype(jnp.int32)
            tag = jnp.where(
                lane == iota((LANES, step), 0), tags[h : h + 1, b * step : (b + 1) * step], 0.0
            )
            labels = labels + lax.dot_general(
                one.astype(BF16), tag.astype(BF16), NT, preferred_element_type=F32
            )
        rank = jnp.concatenate(ranks, axis=1).astype(jnp.int32)
        slot_rows.append(jnp.where(rank >= slots, rank, owner[h : h + 1] * COLD + rank))
        hot_ranks.append(jnp.where(rank >= slots, rank - slots, -SHARE))
    slot_all = jnp.concatenate(slot_rows, axis=0)
    table_ref[...] = jnp.concatenate([slot_all.astype(F32), tags], axis=0)
    shares = HOT // SHARE
    rows = shares * COLD
    row = iota((rows, 1), 0)
    row_share, row_at = row // COLD, row % COLD
    want_k = jnp.where(row_at < SHARE, SHARE * row_share + row_at, -9)
    want_v = jnp.where(
        (row_at >= SHARE) & (row_at < 2 * SHARE), SHARE * (row_share - 1) + row_at, -9
    )
    want_tag = jnp.where(row_at == 2 * SHARE, row_share, -9)
    for load in loads:
        load.wait()
    hot_tiles = []
    for h in range(heads):
        cols = slice(h * hd, (h + 1) * hd)
        for j, ref in enumerate((q_ref, k_ref, v_ref)):
            x_ref[h, :, j * hd : (j + 1) * hd] = ref[:, cols]
        hot = hot_ranks[h]
        tag_rows = jnp.broadcast_to(tags[h : h + 1], (LANES, tokens))
        share = (hot + SHARE) // SHARE - 1
        lane_tag = jnp.where(iota((LANES, tokens), 0) == HOT_LANE + hot - SHARE * share, tag_rows, 0.0)
        tiles = lax.dot_general(
            (share == want_tag).astype(BF16), lane_tag.astype(BF16), NT, preferred_element_type=F32
        )
        tiles = tiles + jnp.dot((hot == want_k).astype(BF16), k_ref[:, cols], preferred_element_type=F32)
        tiles = tiles + jnp.dot((hot == want_v).astype(BF16), v_ref[:, cols], preferred_element_type=F32)
        hot_tiles.append(tiles)
        place = (hot == iota((HOT_PAD, tokens), 0)).astype(BF16)
        asked = jnp.dot(place, q_ref[:, cols], preferred_element_type=F32)
        asked_tags = lax.dot_general(place, tag_rows.astype(BF16), NT, preferred_element_type=F32)
        hot_ref[h, 0:3] = asked[:HOT].reshape(3, COLD, hd).astype(BF16)
        hot_ref[h, 3:6] = asked_tags[:HOT].reshape(3, COLD, hd).astype(BF16)
    y = lax.axis_index("y")
    for d, ref in enumerate((h0_ref, h1_ref, h2_ref, h3_ref)):
        ref[...] = hot_ref[lax.rem(y + d, heads)]
    part = 256
    sub = iota((COLD, LANES), 0)
    sent = []
    for c in range(slots // part):
        first, stop = c * part // COLD, (c + 1) * part // COLD
        for h in range(heads):
            place = (slot_all[h : h + 1] == iota((part, tokens), 0) + c * part).astype(BF16)
            moved = jnp.dot(place, x_ref[h], preferred_element_type=F32)
            for j in range(3):
                send_ref[first:stop, 3 * h + j] = (
                    moved[:, j * hd : (j + 1) * hd].reshape(stop - first, COLD, hd).astype(BF16)
                )
        for dev in range(first, stop):
            share, head = dev // 16, dev % heads
            tile = hot_tiles[head][share * COLD : (share + 1) * COLD]
            tile = jnp.where(sub == 2 * SHARE, tile + labels[dev : dev + 1], tile)
            send_ref[dev, 3 * heads] = tile.astype(BF16)
        out = pltpu.make_async_copy(
            send_ref.at[first:stop], send_hbm.at[first:stop], out_sems.at[c]
        )
        out.start()
        sent.append(out)
    for out in sent:
        out.wait()


def softmax_rows(scores, allowed, scale, values):
    masked = jnp.where(allowed, scores, NEG_FILL)
    top = jnp.max(masked, axis=1, keepdims=True)
    weights = jnp.exp2((masked - top) * scale)
    total = jnp.sum(weights, axis=1, keepdims=True)
    out = jnp.dot(weights.astype(BF16), values, preferred_element_type=F32)
    return out / total


NT = (((1,), (1,)), ((), ()))


def cold_kernel(got_ref, out_ref):
    devices, tiles, _, hd = got_ref.shape
    heads = tiles // 3
    slots = devices * COLD
    scale = hd ** (-0.5) * LOG2E
    extra = got_ref[:, 3 * heads].astype(F32)
    spread = jnp.broadcast_to(
        extra[:, 2 * SHARE : 2 * SHARE + 1], (devices, COLD, LANES)
    ).reshape(slots, LANES)
    pick = iota((slots, LANES), 1) - iota((slots, LANES), 0) % COLD
    ones = jnp.ones((LANES, LANES), BF16)
    part = 256
    causal = iota((part, part), 1) <= iota((part, part), 0)
    for h in range(heads):
        tags = jnp.where(pick == COLD * h, spread, 0.0).astype(BF16)
        label_cols = jnp.dot(tags, ones, preferred_element_type=F32)
        label_rows = lax.dot_general(ones[:COLD], tags, NT, preferred_element_type=F32)
        q, k, v = (
            got_ref[:, 3 * h + j].astype(F32).reshape(slots, hd).astype(BF16) for j in range(3)
        )
        for c in range(slots // part):
            stop = (c + 1) * part
            scores = lax.dot_general(
                q[c * part : stop], k[:stop], NT, preferred_element_type=F32
            )
            allowed = label_cols[c * part : stop, :1] == label_rows[:1, :stop]
            last = allowed[:, c * part :] & causal
            allowed = last if c == 0 else jnp.concatenate([allowed[:, : c * part], last], axis=1)
            out = softmax_rows(scores, allowed, scale, v[:stop])
            devs = slice(c * part // COLD, stop // COLD)
            out_ref[devs, h] = out.reshape(part // COLD, COLD, hd).astype(BF16)


def mid_kernel(got_ref, kv_ref):
    devices, tiles, _, hd = got_ref.shape
    slots = devices * COLD
    keys = devices * SHARE
    extra = got_ref[:, tiles - 1].astype(F32).reshape(slots, hd).astype(BF16)
    n = iota((keys, 1), 0)
    source, at = n // SHARE, n % SHARE
    col = iota((keys, slots), 1)

    def rows_at(offset):
        place = (col == source * COLD + offset).astype(BF16)
        return jnp.dot(place, extra, preferred_element_type=F32)

    kv_ref[0:48] = rows_at(at).reshape(48, COLD, hd).astype(BF16)
    kv_ref[48:96] = rows_at(at + SHARE).reshape(48, COLD, hd).astype(BF16)
    tags = jnp.where(iota((keys, hd), 1) == HOT_LANE + at, rows_at(2 * SHARE), 0.0).astype(BF16)
    flat = lax.dot_general(jnp.ones((COLD, hd), BF16), tags, NT, preferred_element_type=F32)
    label = [flat[0:1, j * LANES : (j + 1) * LANES] for j in range(keys // LANES)]
    label.append(jnp.zeros((COLD - len(label), LANES), F32))
    kv_ref[96] = jnp.concatenate(label, axis=0).astype(BF16)


def hot_kernel(
    b0_ref, b1_ref, b2_ref, b3_ref, n0_ref, n1_ref, n2_ref, n3_ref, f0_ref, f1_ref, f2_ref, f3_ref,
    o0_ref, o1_ref, o2_ref, o3_ref, all_ref, k_ref, v_ref, o_ref,
):
    hd = b0_ref.shape[-1]
    rows = 4 * HOT
    keys = k_ref.shape[0] // 8
    scale = hd ** (-0.5) * LOG2E
    y, x, core, z = (lax.axis_index(a) for a in ("y", "x", "core", "z"))
    for d, ref in enumerate((b0_ref, b1_ref, b2_ref, b3_ref)):
        all_ref[lax.rem(y + 4 - d, 4)] = ref[...].astype(F32)
    q = all_ref[:, 0:3].reshape(rows, hd).astype(BF16)
    label_col = all_ref[:, 3:6].reshape(rows, hd)[:, 0:1]
    row = iota((rows, 1), 0)
    asked_at = (((z * 2 + core) * 16 + x * 4) * HOT + row).astype(F32)
    n = iota((1, keys), 1)
    key_at = (n // SHARE) * HOT + n % SHARE
    allowed = []
    blocks = ((n0_ref, n1_ref, n2_ref, n3_ref), (f0_ref, f1_ref, f2_ref, f3_ref))
    for dc in range(2):
        for dz in range(4):
            ref = blocks[dc][dz]
            at = slice((dc * 4 + dz) * keys, (dc * 4 + dz + 1) * keys)
            k_ref[at] = ref[0:48].astype(F32).reshape(keys, hd).astype(BF16)
            v_ref[at] = ref[48:96].astype(F32).reshape(keys, hd).astype(BF16)
            tile = ref[96].astype(F32)
            label = jnp.concatenate([tile[j : j + 1] for j in range(keys // LANES)], axis=1)
            share = lax.rem(z + 4 - dz, 4) * 2 + lax.rem(core + dc, 2)
            there = (key_at + SHARE * share).astype(F32)
            allowed.append((label_col == label) & (there <= asked_at))
    scores = lax.dot_general(q, k_ref[...], NT, preferred_element_type=F32)
    out = softmax_rows(scores, jnp.concatenate(allowed, axis=1), scale, v_ref[...])
    o_ref[...] = out.reshape(4, 3, COLD, hd)
    for d, ref in enumerate((o0_ref, o1_ref, o2_ref, o3_ref)):
        ref[...] = o_ref[lax.rem(y + 4 - d, 4)].astype(BF16)


def unpack_kernel(table_ref, back_ref, o0_ref, o1_ref, o2_ref, o3_ref, out_ref, hot_ref):
    devices, heads, _, hd = back_ref.shape
    tokens = table_ref.shape[1]
    cols = columns_of(table_ref[...])
    slots = devices * COLD
    part = 256
    for d, ref in enumerate((o0_ref, o1_ref, o2_ref, o3_ref)):
        hot_ref[d] = ref[...].astype(F32)
    for h in range(heads):
        rows = back_ref[:, h].astype(F32).reshape(slots, hd).astype(BF16)
        hot = hot_ref[lax.rem(h + 4 - lax.axis_index("y"), 4)].reshape(HOT, hd)
        hot = jnp.concatenate([hot, jnp.zeros((LANES - HOT, hd), F32)], axis=0).astype(BF16)
        for c in range(tokens // part):
            slot = cols[c * part : (c + 1) * part, h : h + 1].astype(jnp.int32)
            place = (slot == lax.broadcasted_iota(jnp.int32, (part, slots), 1)).astype(BF16)
            hot_place = (
                slot == lax.broadcasted_iota(jnp.int32, (part, LANES), 1) + slots
            ).astype(BF16)
            got = jnp.dot(place, rows, preferred_element_type=F32) + jnp.dot(
                hot_place, hot, preferred_element_type=F32
            )
            out_ref[c * part : (c + 1) * part, h * hd : (h + 1) * hd] = got.astype(BF16)


VMEM = pl.BlockSpec(memory_space=pltpu.VMEM)
HBM = pl.BlockSpec(memory_space=pl.ANY)
AXES = ("z", "core", "x", "y")
MIB = 1024 * 1024


def call(kernel, name, limit, ins, outs, scratch, *arrays):
    return pl.pallas_call(
        kernel,
        out_shape=tuple(jax.ShapeDtypeStruct(*out[1:]) for out in outs),
        in_specs=ins,
        out_specs=tuple(out[0] for out in outs),
        scratch_shapes=scratch,
        compiler_params=pltpu.CompilerParams(vmem_limit_bytes=limit * MIB),
        name=name,
    )(*arrays)


def shift(block, axis, by):
    size = lax.axis_size(axis)
    return lax.ppermute(block, axis, [(i, (i + by) % size) for i in range(size)])


def local(query_rows, key_rows, value_rows, cluster_ids):
    devices = lax.axis_size(AXES)
    heads, tokens = cluster_ids.shape
    hd = query_rows.shape[1] // heads
    tile = (COLD, hd)
    rows = pltpu.VMEM((tokens, heads * hd), BF16)
    payload = (devices, 3 * heads + 1, *tile)
    table, h0, h1, h2, h3, send = call(
        pack_kernel, "pack", 58, [VMEM, HBM, HBM, HBM],
        [(VMEM, (2 * heads, tokens), F32)] + [(VMEM, (6, *tile), BF16)] * 4 + [(HBM, payload, BF16)],
        [
            rows, rows, rows, pltpu.VMEM((heads, tokens, 3 * hd), BF16),
            pltpu.VMEM((heads, 6, *tile), BF16), pltpu.VMEM(payload, BF16),
            pltpu.SemaphoreType.DMA((3,)), pltpu.SemaphoreType.DMA((4,)),
        ],
        cluster_ids, query_rows, key_rows, value_rows,
    )
    got = lax.all_to_all(send, AXES, split_axis=0, concat_axis=0, tiled=True)
    asked = [h0] + [shift(b, "y", d + 1) for d, b in enumerate((h1, h2, h3))]
    got, asked = lax.optimization_barrier((got, asked))
    (kv,) = call(mid_kernel, "mid", 24, [VMEM], [(VMEM, (97, *tile), BF16)], [], got)
    got, kv = lax.optimization_barrier((got, kv))
    near = [kv] + [shift(kv, "z", d) for d in (1, 2, 3)]
    (answer,) = call(
        cold_kernel, "cold", 24, [VMEM], [(VMEM, (devices, heads, *tile), BF16)], [], got
    )
    near, answer = lax.optimization_barrier((near, answer))
    far = [shift(b, "core", 1) for b in near]
    outs = call(
        hot_kernel, "hot", 24, [VMEM] * 12, [(VMEM, (3, *tile), BF16)] * 4,
        [
            pltpu.VMEM((4, 6, *tile), F32), pltpu.VMEM((devices * HOT, hd), BF16),
            pltpu.VMEM((devices * HOT, hd), BF16), pltpu.VMEM((4, 3, *tile), F32),
        ],
        *asked, *near, *far,
    )
    hot_out = [outs[0]] + [shift(b, "y", 3 - d) for d, b in enumerate(outs[1:])]
    back = lax.all_to_all(answer, AXES, split_axis=0, concat_axis=0, tiled=True)
    (result,) = call(
        unpack_kernel, "unpack", 24, [VMEM] * 6, [(VMEM, (tokens, heads * hd), BF16)],
        [pltpu.VMEM((4, 3, *tile), F32)],
        table, back, *hot_out,
    )
    return result


def solution(mesh):
    split = jax.sharding.Mesh(mesh.devices.reshape(4, 2, 4, 4), AXES)
    return jax.shard_map(
        local,
        mesh=split,
        in_specs=(P(AXES, None), P(AXES, None), P(AXES, None), P(None, AXES)),
        out_specs=P(AXES, None),
        check_vma=False,
    )
```

```python
import jax
import jax.numpy as jnp
from jax import lax
from jax.experimental import pallas as pl
from jax.experimental.pallas import tpu as pltpu
from jax.sharding import PartitionSpec as P

CL_DEV = 8
COLD = 8
HOT = 24
HOT_PAD = 32
LANES = 128
NEG_FILL = -1e30
SHARE = 3
HOT_LANE = 32
MARK_Q = 104.0
MARK_K = 100.0
LOG2E = 1.4426950408889634
F32 = jnp.float32
BF16 = jnp.bfloat16


def iota(shape, dim):
    return lax.broadcasted_iota(jnp.int32, shape, dim)


def columns_of(table):
    tokens = table.shape[1]
    return jnp.transpose(
        jnp.concatenate([table, jnp.zeros((LANES - table.shape[0], tokens), F32)], axis=0)
    )


def pack_kernel(
    ids_ref, q_hbm, k_hbm, v_hbm,
    table_ref, h0_ref, h1_ref, h2_ref, h3_ref, send_hbm,
    q_ref, k_ref, v_ref, x_ref, hot_ref, send_ref, sems, out_sems,
):
    heads, tokens = ids_ref.shape
    hd = q_ref.shape[1] // heads
    devices = send_ref.shape[0]
    slots = devices * COLD
    step = 256
    loads = [
        pltpu.make_async_copy(src, dst, sems.at[j])
        for j, (src, dst) in enumerate(((q_hbm, q_ref), (k_hbm, k_ref), (v_hbm, v_ref)))
    ]
    for load in loads:
        load.start()
    ids = ids_ref[...]
    owner = ids // CL_DEV
    tags = (ids - owner * CL_DEV + 1).astype(F32)
    upper = (iota((step, step), 0) < iota((step, step), 1)).astype(BF16)
    dev_col = iota((devices, step), 0)
    slot_rows = []
    labels = jnp.zeros((devices, LANES), F32)
    for h in range(heads):
        carry = jnp.zeros((devices, 1), F32)
        ones, ranks = [], []
        for b in range(tokens // step):
            one = (owner[h : h + 1, b * step : (b + 1) * step] == dev_col).astype(F32)
            inside = jnp.dot(one.astype(BF16), upper, preferred_element_type=F32) + carry
            carry = carry + jnp.sum(one, axis=1, keepdims=True)
            ones.append(one)
            ranks.append(jnp.sum(one * inside, axis=0, keepdims=True))
        full = (carry > COLD).astype(F32)
        for b, one in enumerate(ones):
            ranks[b] = jnp.where(
                jnp.sum(one * full, axis=0, keepdims=True) > 0.5, ranks[b] + slots, ranks[b]
            )
            lane = jnp.where(
                ranks[b] < COLD, ranks[b] + COLD * h, ranks[b] + (HOT_LANE + HOT * h - slots)
            ).astype(jnp.int32)
            tag = jnp.where(
                lane == iota((LANES, step), 0), tags[h : h + 1, b * step : (b + 1) * step], 0.0
            )
            labels = labels + lax.dot_general(
                one.astype(BF16), tag.astype(BF16), NT, preferred_element_type=F32
            )
        rank = jnp.concatenate(ranks, axis=1).astype(jnp.int32)
        slot_rows.append(jnp.where(rank >= slots, rank, owner[h : h + 1] * COLD + rank))
    slot_all = jnp.concatenate(slot_rows, axis=0)
    table_ref[...] = jnp.concatenate([slot_all.astype(F32), tags], axis=0)
    asked_tags = jnp.sum(labels, axis=0, keepdims=True)
    cold_lane = iota((1, LANES), 1) < HOT_LANE
    for h in range(heads):
        own = iota((HOT, LANES), 1) == iota((HOT, LANES), 0) + (HOT_LANE + HOT * h)
        tag = jnp.sum(jnp.where(own, asked_tags, 0.0), axis=1, keepdims=True)
        hot_ref[h, 3:6] = jnp.broadcast_to(tag, (HOT, hd)).reshape(3, COLD, hd).astype(BF16)
    rows = HOT // SHARE * COLD
    row = iota((rows + HOT_PAD, 1), 0)
    row_share, row_at = row // COLD, row % COLD
    want = jnp.where(row_at < SHARE, SHARE * row_share + row_at, SHARE * (row_share - 1) + row_at)
    want = jnp.where(row_at < 2 * SHARE, want, -9)
    want = jnp.where(row < rows, want, row - rows) + slots
    tile_at = iota((rows, hd), 0) % COLD
    for load in loads:
        load.wait()
    hot_tiles = []
    for h in range(heads):
        for j, ref in enumerate((q_ref, k_ref, v_ref)):
            x_ref[h, :, j * hd : (j + 1) * hd] = ref[:, h * hd : (h + 1) * hd]
        moved = jnp.dot(
            (slot_all[h : h + 1] == want).astype(BF16), x_ref[h], preferred_element_type=F32
        )
        tiles = jnp.where(tile_at < SHARE, moved[:rows, hd : 2 * hd], moved[:rows, 2 * hd :])
        tiles = jnp.where(tile_at == COLD - 1, asked_tags, tiles)
        hot_tiles.append(tiles)
        hot_ref[h, 0:3] = moved[rows : rows + HOT, :hd].reshape(3, COLD, hd).astype(BF16)
    y = lax.axis_index("y")
    for d, ref in enumerate((h0_ref, h1_ref, h2_ref, h3_ref)):
        ref[...] = hot_ref[lax.rem(y + d, heads)]
    labels = jnp.where(cold_lane, labels, 0.0)
    part = 256
    sub = iota((COLD, LANES), 0)
    sent = []
    for c in range(slots // part):
        first, stop = c * part // COLD, (c + 1) * part // COLD
        for h in range(heads):
            place = (slot_all[h : h + 1] == iota((part, tokens), 0) + c * part).astype(BF16)
            moved = jnp.dot(place, x_ref[h], preferred_element_type=F32)
            for j in range(3):
                send_ref[first:stop, 3 * h + j] = (
                    moved[:, j * hd : (j + 1) * hd].reshape(stop - first, COLD, hd).astype(BF16)
                )
        for dev in range(first, stop):
            share, head = dev // 16, dev % heads
            tile = hot_tiles[head][share * COLD : (share + 1) * COLD]
            tile = jnp.where(sub == 2 * SHARE, labels[dev : dev + 1], tile)
            send_ref[dev, 3 * heads] = tile.astype(BF16)
        out = pltpu.make_async_copy(
            send_ref.at[first:stop], send_hbm.at[first:stop], out_sems.at[c]
        )
        out.start()
        sent.append(out)
    for out in sent:
        out.wait()


def softmax_rows(scores, allowed, scale, values):
    masked = jnp.where(allowed, scores, NEG_FILL)
    top = jnp.max(masked, axis=1, keepdims=True)
    weights = jnp.exp2((masked - top) * scale)
    total = jnp.sum(weights, axis=1, keepdims=True)
    out = jnp.dot(weights.astype(BF16), values, preferred_element_type=F32)
    return out / total


NT = (((1,), (1,)), ((), ()))


def cold_kernel(got_ref, out_ref):
    devices, tiles, _, hd = got_ref.shape
    heads = tiles // 3
    slots = devices * COLD
    scale = hd ** (-0.5) * LOG2E
    extra = got_ref[:, 3 * heads].astype(F32)
    spread = jnp.broadcast_to(
        extra[:, 2 * SHARE : 2 * SHARE + 1], (devices, COLD, LANES)
    ).reshape(slots, LANES)
    pick = iota((slots, LANES), 1) - iota((slots, LANES), 0) % COLD
    ones = jnp.ones((LANES, LANES), BF16)
    part = 512
    causal = iota((part, part), 1) <= iota((part, part), 0)
    for h in range(heads):
        tags = jnp.where(pick == COLD * h, spread, 0.0).astype(BF16)
        label_cols = jnp.dot(tags, ones, preferred_element_type=F32)
        q, k, v = (
            got_ref[:, 3 * h + j].astype(F32).reshape(slots, hd).astype(BF16) for j in range(3)
        )
        marked = label_cols == (iota((slots, LANES), 1) + 1).astype(F32)
        q = jnp.concatenate([q, jnp.where(marked, MARK_Q, 0.0).astype(BF16)], axis=1)
        k = jnp.concatenate([k, jnp.where(marked, MARK_K, 0.0).astype(BF16)], axis=1)
        for c in range(slots // part):
            stop = (c + 1) * part
            scores = lax.dot_general(
                q[c * part : stop], k[:stop], NT, preferred_element_type=F32
            )
            last = jnp.where(causal, scores[:, c * part :], NEG_FILL)
            if c > 0:
                last = jnp.concatenate([scores[:, : c * part], last], axis=1)
            top = jnp.max(last, axis=1, keepdims=True)
            weights = jnp.exp2((last - top) * scale)
            total = jnp.sum(weights, axis=1, keepdims=True)
            out = jnp.dot(weights.astype(BF16), v[:stop], preferred_element_type=F32) / total
            devs = slice(c * part // COLD, stop // COLD)
            out_ref[devs, h] = out.reshape(part // COLD, COLD, hd).astype(BF16)


def mid_kernel(got_ref, kv_ref):
    devices, tiles, _, hd = got_ref.shape
    slots = devices * COLD
    keys = devices * SHARE
    extra = got_ref[:, tiles - 1].astype(F32).reshape(slots, hd).astype(BF16)
    n = iota((keys, 1), 0)
    source, at = n // SHARE, n % SHARE
    col = iota((keys, slots), 1)

    def rows_at(offset):
        place = (col == source * COLD + offset).astype(BF16)
        return jnp.dot(place, extra, preferred_element_type=F32)

    kv_ref[0:48] = rows_at(at).reshape(48, COLD, hd).astype(BF16)
    kv_ref[48:96] = rows_at(at + SHARE).reshape(48, COLD, hd).astype(BF16)
    y, core, z = (lax.axis_index(a) for a in ("y", "core", "z"))
    lane = HOT_LANE + HOT * y + SHARE * (z * 2 + core) + at
    tags = jnp.where(iota((keys, hd), 1) == lane, rows_at(COLD - 1), 0.0).astype(BF16)
    flat = lax.dot_general(jnp.ones((COLD, hd), BF16), tags, NT, preferred_element_type=F32)
    label = [flat[0:1, j * LANES : (j + 1) * LANES] for j in range(keys // LANES)]
    label.append(jnp.zeros((COLD - len(label), LANES), F32))
    kv_ref[96] = jnp.concatenate(label, axis=0).astype(BF16)


def hot_kernel(
    b0_ref, b1_ref, b2_ref, b3_ref, near_ref, far_ref,
    o0_ref, o1_ref, o2_ref, o3_ref, all_ref, k_ref, v_ref, o_ref,
):
    hd = b0_ref.shape[-1]
    rows = 4 * HOT
    keys = k_ref.shape[0] // 8
    scale = hd ** (-0.5) * LOG2E
    y, x, core, z = (lax.axis_index(a) for a in ("y", "x", "core", "z"))
    for d, ref in enumerate((b0_ref, b1_ref, b2_ref, b3_ref)):
        all_ref[lax.rem(y + 4 - d, 4)] = ref[...].astype(F32)
    q = all_ref[:, 0:3].reshape(rows, hd).astype(BF16)
    label_col = all_ref[:, 3:6].reshape(rows, hd)[:, 0:1]
    row = iota((rows, 1), 0)
    asked_at = (((z * 2 + core) * 16 + x * 4) * HOT + row).astype(F32)
    n = iota((1, keys), 1)
    key_at = (n // SHARE) * HOT + n % SHARE
    allowed = []
    for dc, ref in enumerate((near_ref, far_ref)):
        for dz in range(4):
            tile = 97 * dz
            at = slice((dc * 4 + dz) * keys, (dc * 4 + dz + 1) * keys)
            k_ref[at] = ref[tile : tile + 48].astype(F32).reshape(keys, hd).astype(BF16)
            v_ref[at] = ref[tile + 48 : tile + 96].astype(F32).reshape(keys, hd).astype(BF16)
            tags = ref[tile + 96].astype(F32)
            label = jnp.concatenate([tags[j : j + 1] for j in range(keys // LANES)], axis=1)
            share = lax.rem(z + 4 - dz, 4) * 2 + lax.rem(core + dc, 2)
            there = (key_at + SHARE * share).astype(F32)
            allowed.append((label_col == label) & (there <= asked_at))
    scores = lax.dot_general(q, k_ref[...], NT, preferred_element_type=F32)
    out = softmax_rows(scores, jnp.concatenate(allowed, axis=1), scale, v_ref[...])
    o_ref[...] = out.reshape(4, 3, COLD, hd)
    for d, ref in enumerate((o0_ref, o1_ref, o2_ref, o3_ref)):
        ref[...] = o_ref[lax.rem(y + 4 - d, 4)].astype(BF16)


def unpack_kernel(table_ref, back_ref, o0_ref, o1_ref, o2_ref, o3_ref, out_ref, hot_ref):
    devices, heads, _, hd = back_ref.shape
    tokens = table_ref.shape[1]
    cols = columns_of(table_ref[...])
    slots = devices * COLD
    part = 256
    for d, ref in enumerate((o0_ref, o1_ref, o2_ref, o3_ref)):
        hot_ref[d] = ref[...].astype(F32)
    for h in range(heads):
        rows = back_ref[:, h].astype(F32).reshape(slots, hd).astype(BF16)
        hot = hot_ref[lax.rem(h + 4 - lax.axis_index("y"), 4)].reshape(HOT, hd)
        hot = jnp.concatenate([hot, jnp.zeros((LANES - HOT, hd), F32)], axis=0).astype(BF16)
        for c in range(tokens // part):
            slot = cols[c * part : (c + 1) * part, h : h + 1].astype(jnp.int32)
            place = (slot == lax.broadcasted_iota(jnp.int32, (part, slots), 1)).astype(BF16)
            hot_place = (
                slot == lax.broadcasted_iota(jnp.int32, (part, LANES), 1) + slots
            ).astype(BF16)
            got = jnp.dot(place, rows, preferred_element_type=F32) + jnp.dot(
                hot_place, hot, preferred_element_type=F32
            )
            out_ref[c * part : (c + 1) * part, h * hd : (h + 1) * hd] = got.astype(BF16)


VMEM = pl.BlockSpec(memory_space=pltpu.VMEM)
HBM = pl.BlockSpec(memory_space=pl.ANY)
AXES = ("z", "core", "x", "y")
MIB = 1024 * 1024


def call(kernel, name, limit, ins, outs, scratch, *arrays):
    return pl.pallas_call(
        kernel,
        out_shape=tuple(jax.ShapeDtypeStruct(*out[1:]) for out in outs),
        in_specs=ins,
        out_specs=tuple(out[0] for out in outs),
        scratch_shapes=scratch,
        compiler_params=pltpu.CompilerParams(vmem_limit_bytes=limit * MIB),
        name=name,
    )(*arrays)


def shift(block, axis, by):
    size = lax.axis_size(axis)
    return lax.ppermute(block, axis, [(i, (i + by) % size) for i in range(size)])


def local(query_rows, key_rows, value_rows, cluster_ids):
    devices = lax.axis_size(AXES)
    heads, tokens = cluster_ids.shape
    hd = query_rows.shape[1] // heads
    tile = (COLD, hd)
    rows = pltpu.VMEM((tokens, heads * hd), BF16)
    payload = (devices, 3 * heads + 1, *tile)
    table, h0, h1, h2, h3, send = call(
        pack_kernel, "pack", 58, [VMEM, HBM, HBM, HBM],
        [(VMEM, (2 * heads, tokens), F32)] + [(VMEM, (6, *tile), BF16)] * 4 + [(HBM, payload, BF16)],
        [
            rows, rows, rows, pltpu.VMEM((heads, tokens, 3 * hd), BF16),
            pltpu.VMEM((heads, 6, *tile), BF16), pltpu.VMEM(payload, BF16),
            pltpu.SemaphoreType.DMA((3,)), pltpu.SemaphoreType.DMA((4,)),
        ],
        cluster_ids, query_rows, key_rows, value_rows,
    )
    got = lax.all_to_all(send, AXES, split_axis=0, concat_axis=0, tiled=True)
    asked = [h0] + [shift(b, "y", d + 1) for d, b in enumerate((h1, h2, h3))]
    got, asked = lax.optimization_barrier((got, asked))
    (kv,) = call(mid_kernel, "mid", 24, [VMEM], [(VMEM, (97, *tile), BF16)], [], got)
    got, kv = lax.optimization_barrier((got, kv))
    near = [kv] + [shift(kv, "z", d) for d in (1, 2, 3)]
    (answer,) = call(
        cold_kernel, "cold", 24, [VMEM], [(VMEM, (devices, heads, *tile), BF16)], [], got
    )
    near, answer = lax.optimization_barrier((near, answer))
    near = jnp.concatenate(near, axis=0)
    far = shift(near, "core", 1)
    outs = call(
        hot_kernel, "hot", 24, [VMEM] * 6, [(VMEM, (3, *tile), BF16)] * 4,
        [
            pltpu.VMEM((4, 6, *tile), F32), pltpu.VMEM((devices * HOT, hd), BF16),
            pltpu.VMEM((devices * HOT, hd), BF16), pltpu.VMEM((4, 3, *tile), F32),
        ],
        *asked, near, far,
    )
    hot_out = [outs[0]] + [shift(b, "y", 3 - d) for d, b in enumerate(outs[1:])]
    back = lax.all_to_all(answer, AXES, split_axis=0, concat_axis=0, tiled=True)
    (result,) = call(
        unpack_kernel, "unpack", 24, [VMEM] * 6, [(VMEM, (tokens, heads * hd), BF16)],
        [pltpu.VMEM((4, 3, *tile), F32)],
        table, back, *hot_out,
    )
    return result


def solution(mesh):
    split = jax.sharding.Mesh(mesh.devices.reshape(4, 2, 4, 4), AXES)
    return jax.shard_map(
        local,
        mesh=split,
        in_specs=(P(AXES, None), P(AXES, None), P(AXES, None), P(None, AXES)),
        out_specs=P(AXES, None),
        check_vma=False,
    )
```

```python
import jax
import jax.numpy as jnp
from jax import lax
from jax.experimental import pallas as pl
from jax.experimental.pallas import tpu as pltpu
from jax.sharding import PartitionSpec as P

CL_DEV = 8
COLD = 8
HOT = 24
HOT_PAD = 32
LANES = 128
NEG_FILL = -1e30
SHARE = 3
HOT_LANE = 32
MARK_Q = 104.0
MARK_K = 100.0
LOG2E = 1.4426950408889634
F32 = jnp.float32
BF16 = jnp.bfloat16


def iota(shape, dim):
    return lax.broadcasted_iota(jnp.int32, shape, dim)


def columns_of(table):
    tokens = table.shape[1]
    return jnp.transpose(
        jnp.concatenate([table, jnp.zeros((LANES - table.shape[0], tokens), F32)], axis=0)
    )


def pack_kernel(
    ids_ref, q_hbm, k_hbm, v_hbm,
    table_ref, h0_ref, h1_ref, h2_ref, h3_ref, send_hbm,
    x_ref, hot_ref, send_ref, sems, out_sems,
):
    heads, tokens = ids_ref.shape
    hd = q_hbm.shape[1] // heads
    devices = send_ref.shape[0]
    slots = devices * COLD
    step = 256
    loads = [
        [
            pltpu.make_async_copy(
                src.at[:, h * hd : (h + 1) * hd], x_ref.at[h, :, j * hd : (j + 1) * hd], sems.at[3 * h + j]
            )
            for j, src in enumerate((q_hbm, k_hbm, v_hbm))
        ]
        for h in range(heads)
    ]
    for row in loads:
        for load in row:
            load.start()
    ids = ids_ref[...]
    owner = ids // CL_DEV
    tags = (ids - owner * CL_DEV + 1).astype(F32)
    upper = (iota((step, step), 0) < iota((step, step), 1)).astype(BF16)
    dev_col = iota((devices, step), 0)
    slot_rows = []
    labels = jnp.zeros((devices, LANES), F32)
    for h in range(heads):
        carry = jnp.zeros((devices, 1), F32)
        ones, ranks = [], []
        for b in range(tokens // step):
            one = (owner[h : h + 1, b * step : (b + 1) * step] == dev_col).astype(F32)
            inside = jnp.dot(one.astype(BF16), upper, preferred_element_type=F32) + carry
            carry = carry + jnp.sum(one, axis=1, keepdims=True)
            ones.append(one)
            ranks.append(jnp.sum(one * inside, axis=0, keepdims=True))
        full = (carry > COLD).astype(F32)
        for b, one in enumerate(ones):
            ranks[b] = jnp.where(
                jnp.sum(one * full, axis=0, keepdims=True) > 0.5, ranks[b] + slots, ranks[b]
            )
            lane = jnp.where(
                ranks[b] < COLD, ranks[b] + COLD * h, ranks[b] + (HOT_LANE + HOT * h - slots)
            ).astype(jnp.int32)
            tag = jnp.where(
                lane == iota((LANES, step), 0), tags[h : h + 1, b * step : (b + 1) * step], 0.0
            )
            labels = labels + lax.dot_general(
                one.astype(BF16), tag.astype(BF16), NT, preferred_element_type=F32
            )
        rank = jnp.concatenate(ranks, axis=1).astype(jnp.int32)
        slot_rows.append(jnp.where(rank >= slots, rank, owner[h : h + 1] * COLD + rank))
    slot_all = jnp.concatenate(slot_rows, axis=0)
    table_ref[...] = jnp.concatenate([slot_all.astype(F32), tags], axis=0)
    asked_tags = jnp.sum(labels, axis=0, keepdims=True)
    cold_lane = iota((1, LANES), 1) < HOT_LANE
    for h in range(heads):
        own = iota((HOT, LANES), 1) == iota((HOT, LANES), 0) + (HOT_LANE + HOT * h)
        tag = jnp.sum(jnp.where(own, asked_tags, 0.0), axis=1, keepdims=True)
        hot_ref[h, 3:6] = jnp.broadcast_to(tag, (HOT, hd)).reshape(3, COLD, hd).astype(BF16)
    rows = HOT // SHARE * COLD
    row = iota((rows + HOT_PAD, 1), 0)
    row_share, row_at = row // COLD, row % COLD
    want = jnp.where(row_at < SHARE, SHARE * row_share + row_at, SHARE * (row_share - 1) + row_at)
    want = jnp.where(row_at < 2 * SHARE, want, -9)
    want = jnp.where(row < rows, want, row - rows) + slots
    tile_at = iota((rows, hd), 0) % COLD
    hot_tiles = []
    for h in range(heads):
        for load in loads[h]:
            load.wait()
        moved = jnp.dot(
            (slot_all[h : h + 1] == want).astype(BF16), x_ref[h], preferred_element_type=F32
        )
        tiles = jnp.where(tile_at < SHARE, moved[:rows, hd : 2 * hd], moved[:rows, 2 * hd :])
        tiles = jnp.where(tile_at == COLD - 1, asked_tags, tiles)
        hot_tiles.append(tiles)
        hot_ref[h, 0:3] = moved[rows : rows + HOT, :hd].reshape(3, COLD, hd).astype(BF16)
    y = lax.axis_index("y")
    for d, ref in enumerate((h0_ref, h1_ref, h2_ref, h3_ref)):
        ref[...] = hot_ref[lax.rem(y + d, heads)]
    labels = jnp.where(cold_lane, labels, 0.0)
    part = 256
    sub = iota((COLD, LANES), 0)
    sent = []
    for c in range(slots // part):
        first, stop = c * part // COLD, (c + 1) * part // COLD
        for h in range(heads):
            place = (slot_all[h : h + 1] == iota((part, tokens), 0) + c * part).astype(BF16)
            moved = jnp.dot(place, x_ref[h], preferred_element_type=F32)
            for j in range(3):
                send_ref[first:stop, 3 * h + j] = (
                    moved[:, j * hd : (j + 1) * hd].reshape(stop - first, COLD, hd).astype(BF16)
                )
        for dev in range(first, stop):
            share, head = dev // 16, dev % heads
            tile = hot_tiles[head][share * COLD : (share + 1) * COLD]
            tile = jnp.where(sub == 2 * SHARE, labels[dev : dev + 1], tile)
            send_ref[dev, 3 * heads] = tile.astype(BF16)
        out = pltpu.make_async_copy(
            send_ref.at[first:stop], send_hbm.at[first:stop], out_sems.at[c]
        )
        out.start()
        sent.append(out)
    for out in sent:
        out.wait()


def softmax_rows(scores, allowed, scale, values):
    masked = jnp.where(allowed, scores, NEG_FILL)
    top = jnp.max(masked, axis=1, keepdims=True)
    weights = jnp.exp2((masked - top) * scale)
    total = jnp.sum(weights, axis=1, keepdims=True)
    out = jnp.dot(weights.astype(BF16), values, preferred_element_type=F32)
    return out / total


NT = (((1,), (1,)), ((), ()))


def cold_kernel(got_ref, out_ref):
    devices, tiles, _, hd = got_ref.shape
    heads = tiles // 3
    slots = devices * COLD
    scale = hd ** (-0.5) * LOG2E
    extra = got_ref[:, 3 * heads].astype(F32)
    spread = jnp.broadcast_to(
        extra[:, 2 * SHARE : 2 * SHARE + 1], (devices, COLD, LANES)
    ).reshape(slots, LANES)
    pick = iota((slots, LANES), 1) - iota((slots, LANES), 0) % COLD
    ones = jnp.ones((LANES, LANES), BF16)
    part = 512
    causal = iota((part, part), 1) <= iota((part, part), 0)
    for h in range(heads):
        tags = jnp.where(pick == COLD * h, spread, 0.0).astype(BF16)
        label_cols = jnp.dot(tags, ones, preferred_element_type=F32)
        q, k, v = (
            got_ref[:, 3 * h + j].astype(F32).reshape(slots, hd).astype(BF16) for j in range(3)
        )
        marked = label_cols == (iota((slots, LANES), 1) + 1).astype(F32)
        q = jnp.concatenate([q, jnp.where(marked, MARK_Q, 0.0).astype(BF16)], axis=1)
        k = jnp.concatenate([k, jnp.where(marked, MARK_K, 0.0).astype(BF16)], axis=1)
        for c in range(slots // part):
            stop = (c + 1) * part
            scores = lax.dot_general(
                q[c * part : stop], k[:stop], NT, preferred_element_type=F32
            )
            last = jnp.where(causal, scores[:, c * part :], NEG_FILL)
            if c > 0:
                last = jnp.concatenate([scores[:, : c * part], last], axis=1)
            top = jnp.max(last, axis=1, keepdims=True)
            weights = jnp.exp2((last - top) * scale)
            total = jnp.sum(weights, axis=1, keepdims=True)
            out = jnp.dot(weights.astype(BF16), v[:stop], preferred_element_type=F32) / total
            devs = slice(c * part // COLD, stop // COLD)
            out_ref[devs, h] = out.reshape(part // COLD, COLD, hd).astype(BF16)


def mid_kernel(got_ref, kv_ref):
    devices, tiles, _, hd = got_ref.shape
    slots = devices * COLD
    keys = devices * SHARE
    extra = got_ref[:, tiles - 1].astype(F32).reshape(slots, hd).astype(BF16)
    n = iota((keys, 1), 0)
    source, at = n // SHARE, n % SHARE
    col = iota((keys, slots), 1)

    def rows_at(offset):
        place = (col == source * COLD + offset).astype(BF16)
        return jnp.dot(place, extra, preferred_element_type=F32)

    kv_ref[0:48] = rows_at(at).reshape(48, COLD, hd).astype(BF16)
    kv_ref[48:96] = rows_at(at + SHARE).reshape(48, COLD, hd).astype(BF16)
    y, core, z = (lax.axis_index(a) for a in ("y", "core", "z"))
    lane = HOT_LANE + HOT * y + SHARE * (z * 2 + core) + at
    tags = jnp.where(iota((keys, hd), 1) == lane, rows_at(COLD - 1), 0.0).astype(BF16)
    flat = lax.dot_general(jnp.ones((COLD, hd), BF16), tags, NT, preferred_element_type=F32)
    label = [flat[0:1, j * LANES : (j + 1) * LANES] for j in range(keys // LANES)]
    label.append(jnp.zeros((COLD - len(label), LANES), F32))
    kv_ref[96] = jnp.concatenate(label, axis=0).astype(BF16)


def hot_kernel(
    b0_ref, b1_ref, b2_ref, b3_ref, near_ref, far_ref,
    o0_ref, o1_ref, o2_ref, o3_ref, all_ref, k_ref, v_ref, o_ref,
):
    hd = b0_ref.shape[-1]
    rows = 4 * HOT
    keys = k_ref.shape[0] // 8
    scale = hd ** (-0.5) * LOG2E
    y, x, core, z = (lax.axis_index(a) for a in ("y", "x", "core", "z"))
    for d, ref in enumerate((b0_ref, b1_ref, b2_ref, b3_ref)):
        all_ref[lax.rem(y + 4 - d, 4)] = ref[...].astype(F32)
    q = all_ref[:, 0:3].reshape(rows, hd).astype(BF16)
    label_col = all_ref[:, 3:6].reshape(rows, hd)[:, 0:1]
    row = iota((rows, 1), 0)
    asked_at = (((z * 2 + core) * 16 + x * 4) * HOT + row).astype(F32)
    n = iota((1, keys), 1)
    key_at = (n // SHARE) * HOT + n % SHARE
    allowed = []
    for dc, ref in enumerate((near_ref, far_ref)):
        for dz in range(4):
            tile = 97 * dz
            at = slice((dc * 4 + dz) * keys, (dc * 4 + dz + 1) * keys)
            k_ref[at] = ref[tile : tile + 48].astype(F32).reshape(keys, hd).astype(BF16)
            v_ref[at] = ref[tile + 48 : tile + 96].astype(F32).reshape(keys, hd).astype(BF16)
            tags = ref[tile + 96].astype(F32)
            label = jnp.concatenate([tags[j : j + 1] for j in range(keys // LANES)], axis=1)
            share = lax.rem(z + 4 - dz, 4) * 2 + lax.rem(core + dc, 2)
            there = (key_at + SHARE * share).astype(F32)
            allowed.append((label_col == label) & (there <= asked_at))
    scores = lax.dot_general(q, k_ref[...], NT, preferred_element_type=F32)
    out = softmax_rows(scores, jnp.concatenate(allowed, axis=1), scale, v_ref[...])
    o_ref[...] = out.reshape(4, 3, COLD, hd)
    for d, ref in enumerate((o0_ref, o1_ref, o2_ref, o3_ref)):
        ref[...] = o_ref[lax.rem(y + 4 - d, 4)].astype(BF16)


def unpack_kernel(table_ref, back_ref, o0_ref, o1_ref, o2_ref, o3_ref, out_ref, hot_ref):
    devices, heads, _, hd = back_ref.shape
    tokens = table_ref.shape[1]
    cols = columns_of(table_ref[...])
    slots = devices * COLD
    part = 256
    for d, ref in enumerate((o0_ref, o1_ref, o2_ref, o3_ref)):
        hot_ref[d] = ref[...].astype(F32)
    for h in range(heads):
        rows = back_ref[:, h].astype(F32).reshape(slots, hd).astype(BF16)
        hot = hot_ref[lax.rem(h + 4 - lax.axis_index("y"), 4)].reshape(HOT, hd)
        hot = jnp.concatenate([hot, jnp.zeros((LANES - HOT, hd), F32)], axis=0).astype(BF16)
        for c in range(tokens // part):
            slot = cols[c * part : (c + 1) * part, h : h + 1].astype(jnp.int32)
            place = (slot == lax.broadcasted_iota(jnp.int32, (part, slots), 1)).astype(BF16)
            hot_place = (
                slot == lax.broadcasted_iota(jnp.int32, (part, LANES), 1) + slots
            ).astype(BF16)
            got = jnp.dot(place, rows, preferred_element_type=F32) + jnp.dot(
                hot_place, hot, preferred_element_type=F32
            )
            out_ref[c * part : (c + 1) * part, h * hd : (h + 1) * hd] = got.astype(BF16)


VMEM = pl.BlockSpec(memory_space=pltpu.VMEM)
HBM = pl.BlockSpec(memory_space=pl.ANY)
AXES = ("z", "core", "x", "y")
MIB = 1024 * 1024


def call(kernel, name, limit, ins, outs, scratch, *arrays):
    return pl.pallas_call(
        kernel,
        out_shape=tuple(jax.ShapeDtypeStruct(*out[1:]) for out in outs),
        in_specs=ins,
        out_specs=tuple(out[0] for out in outs),
        scratch_shapes=scratch,
        compiler_params=pltpu.CompilerParams(vmem_limit_bytes=limit * MIB),
        name=name,
    )(*arrays)


def shift(block, axis, by):
    size = lax.axis_size(axis)
    return lax.ppermute(block, axis, [(i, (i + by) % size) for i in range(size)])


def local(query_rows, key_rows, value_rows, cluster_ids):
    devices = lax.axis_size(AXES)
    heads, tokens = cluster_ids.shape
    hd = query_rows.shape[1] // heads
    tile = (COLD, hd)
    payload = (devices, 3 * heads + 1, *tile)
    table, h0, h1, h2, h3, send = call(
        pack_kernel, "pack", 58, [VMEM, HBM, HBM, HBM],
        [(VMEM, (2 * heads, tokens), F32)] + [(VMEM, (6, *tile), BF16)] * 4 + [(HBM, payload, BF16)],
        [
            pltpu.VMEM((heads, tokens, 3 * hd), BF16),
            pltpu.VMEM((heads, 6, *tile), BF16), pltpu.VMEM(payload, BF16),
            pltpu.SemaphoreType.DMA((3 * heads,)), pltpu.SemaphoreType.DMA((4,)),
        ],
        cluster_ids, query_rows, key_rows, value_rows,
    )
    got = lax.all_to_all(send, AXES, split_axis=0, concat_axis=0, tiled=True)
    asked = [h0] + [shift(b, "y", d + 1) for d, b in enumerate((h1, h2, h3))]
    got, asked = lax.optimization_barrier((got, asked))
    (kv,) = call(mid_kernel, "mid", 24, [VMEM], [(VMEM, (97, *tile), BF16)], [], got)
    got, kv = lax.optimization_barrier((got, kv))
    below, above = shift(kv, "z", 1), shift(kv, "z", 3)
    (answer,) = call(
        cold_kernel, "cold", 24, [VMEM], [(VMEM, (devices, heads, *tile), BF16)], [], got
    )
    below, above, answer = lax.optimization_barrier((below, above, answer))
    beyond = [shift(below[:49], "z", 1), shift(above[49:], "z", 3)]
    near = jnp.concatenate([kv, below, *beyond, above], axis=0)
    far = shift(near, "core", 1)
    outs = call(
        hot_kernel, "hot", 24, [VMEM] * 6, [(VMEM, (3, *tile), BF16)] * 4,
        [
            pltpu.VMEM((4, 6, *tile), F32), pltpu.VMEM((devices * HOT, hd), BF16),
            pltpu.VMEM((devices * HOT, hd), BF16), pltpu.VMEM((4, 3, *tile), F32),
        ],
        *asked, near, far,
    )
    hot_out = [outs[0]] + [shift(b, "y", 3 - d) for d, b in enumerate(outs[1:])]
    back = lax.all_to_all(answer, AXES, split_axis=0, concat_axis=0, tiled=True)
    (result,) = call(
        unpack_kernel, "unpack", 24, [VMEM] * 6, [(VMEM, (tokens, heads * hd), BF16)],
        [pltpu.VMEM((4, 3, *tile), F32)],
        table, back, *hot_out,
    )
    return result


def solution(mesh):
    split = jax.sharding.Mesh(mesh.devices.reshape(4, 2, 4, 4), AXES)
    return jax.shard_map(
        local,
        mesh=split,
        in_specs=(P(AXES, None), P(AXES, None), P(AXES, None), P(None, AXES)),
        out_specs=P(AXES, None),
        check_vma=False,
    )
```

```python
import jax
import jax.numpy as jnp
from jax import lax
from jax.experimental import pallas as pl
from jax.experimental.pallas import tpu as pltpu
from jax.sharding import PartitionSpec as P

CL_DEV = 8
COLD = 8
HOT = 24
HOT_PAD = 32
LANES = 128
NEG_FILL = -1e30
SHARE = 3
HOT_LANE = 32
MARK_Q = 104.0
MARK_K = 100.0
LOG2E = 1.4426950408889634
F32 = jnp.float32
BF16 = jnp.bfloat16


def iota(shape, dim):
    return lax.broadcasted_iota(jnp.int32, shape, dim)


def columns_of(table):
    tokens = table.shape[1]
    return jnp.transpose(
        jnp.concatenate([table, jnp.zeros((LANES - table.shape[0], tokens), F32)], axis=0)
    )


def pack_kernel(
    ids_ref, q_hbm, k_hbm, v_hbm,
    table_ref, h0_ref, h1_ref, h2_ref, h3_ref, send_hbm,
    x_ref, hot_ref, send_ref, sems, out_sems,
):
    heads, tokens = ids_ref.shape
    hd = q_hbm.shape[1] // heads
    devices = send_ref.shape[0]
    slots = devices * COLD
    step = 256
    loads = [
        [
            pltpu.make_async_copy(
                src.at[:, h * hd : (h + 1) * hd], x_ref.at[h, :, j * hd : (j + 1) * hd], sems.at[3 * h + j]
            )
            for j, src in enumerate((q_hbm, k_hbm, v_hbm))
        ]
        for h in range(heads)
    ]
    for row in loads:
        for load in row:
            load.start()
    ids = ids_ref[...]
    owner = ids // CL_DEV
    tags = (ids - owner * CL_DEV + 1).astype(F32)
    upper = (iota((step, step), 0) < iota((step, step), 1)).astype(BF16)
    dev_col = iota((devices, step), 0)
    slot_rows = []
    labels = jnp.zeros((devices, LANES), F32)
    for h in range(heads):
        carry = jnp.zeros((devices, 1), F32)
        ones, ranks = [], []
        for b in range(tokens // step):
            one = (owner[h : h + 1, b * step : (b + 1) * step] == dev_col).astype(F32)
            inside = jnp.dot(one.astype(BF16), upper, preferred_element_type=F32) + carry
            carry = carry + jnp.sum(one, axis=1, keepdims=True)
            ones.append(one)
            ranks.append(jnp.sum(one * inside, axis=0, keepdims=True))
        full = (carry > COLD).astype(F32)
        for b, one in enumerate(ones):
            ranks[b] = jnp.where(
                jnp.sum(one * full, axis=0, keepdims=True) > 0.5, ranks[b] + slots, ranks[b]
            )
            lane = jnp.where(
                ranks[b] < COLD, ranks[b] + COLD * h, ranks[b] + (HOT_LANE + HOT * h - slots)
            ).astype(jnp.int32)
            tag = jnp.where(
                lane == iota((LANES, step), 0), tags[h : h + 1, b * step : (b + 1) * step], 0.0
            )
            labels = labels + lax.dot_general(
                one.astype(BF16), tag.astype(BF16), NT, preferred_element_type=F32
            )
        rank = jnp.concatenate(ranks, axis=1).astype(jnp.int32)
        slot_rows.append(jnp.where(rank >= slots, rank, owner[h : h + 1] * COLD + rank))
    slot_all = jnp.concatenate(slot_rows, axis=0)
    table_ref[...] = jnp.concatenate([slot_all.astype(F32), tags], axis=0)
    asked_tags = jnp.sum(labels, axis=0, keepdims=True)
    cold_lane = iota((1, LANES), 1) < HOT_LANE
    for h in range(heads):
        own = iota((HOT, LANES), 1) == iota((HOT, LANES), 0) + (HOT_LANE + HOT * h)
        tag = jnp.sum(jnp.where(own, asked_tags, 0.0), axis=1, keepdims=True)
        hot_ref[h, 3:6] = jnp.broadcast_to(tag, (HOT, hd)).reshape(3, COLD, hd).astype(BF16)
    rows = HOT // SHARE * COLD
    row = iota((rows + HOT_PAD, 1), 0)
    row_share, row_at = row // COLD, row % COLD
    want = jnp.where(row_at < SHARE, SHARE * row_share + row_at, SHARE * (row_share - 1) + row_at)
    want = jnp.where(row_at < 2 * SHARE, want, -9)
    want = jnp.where(row < rows, want, row - rows) + slots
    tile_at = iota((rows, hd), 0) % COLD
    hot_tiles = []
    for h in range(heads):
        for load in loads[h]:
            load.wait()
        moved = jnp.dot(
            (slot_all[h : h + 1] == want).astype(BF16), x_ref[h], preferred_element_type=F32
        )
        tiles = jnp.where(tile_at < SHARE, moved[:rows, hd : 2 * hd], moved[:rows, 2 * hd :])
        tiles = jnp.where(tile_at == COLD - 1, asked_tags, tiles)
        hot_tiles.append(tiles)
        hot_ref[h, 0:3] = moved[rows : rows + HOT, :hd].reshape(3, COLD, hd).astype(BF16)
    y = lax.axis_index("y")
    for d, ref in enumerate((h0_ref, h1_ref, h2_ref, h3_ref)):
        ref[...] = hot_ref[lax.rem(y + d, heads)]
    labels = jnp.where(cold_lane, labels, 0.0)
    part = 256
    sub = iota((COLD, LANES), 0)
    sent = []
    for c in range(slots // part):
        first, stop = c * part // COLD, (c + 1) * part // COLD
        for h in range(heads):
            place = (slot_all[h : h + 1] == iota((part, tokens), 0) + c * part).astype(BF16)
            moved = jnp.dot(place, x_ref[h], preferred_element_type=F32)
            for j in range(3):
                send_ref[first:stop, 3 * h + j] = (
                    moved[:, j * hd : (j + 1) * hd].reshape(stop - first, COLD, hd).astype(BF16)
                )
        for dev in range(first, stop):
            share, head = dev // 16, dev % heads
            tile = hot_tiles[head][share * COLD : (share + 1) * COLD]
            tile = jnp.where(sub == 2 * SHARE, labels[dev : dev + 1], tile)
            send_ref[dev, 3 * heads] = tile.astype(BF16)
        out = pltpu.make_async_copy(
            send_ref.at[first:stop], send_hbm.at[first:stop], out_sems.at[c]
        )
        out.start()
        sent.append(out)
    for out in sent:
        out.wait()


def softmax_rows(scores, allowed, scale, values):
    masked = jnp.where(allowed, scores, NEG_FILL)
    top = jnp.max(masked, axis=1, keepdims=True)
    weights = jnp.exp2((masked - top) * scale)
    total = jnp.sum(weights, axis=1, keepdims=True)
    out = jnp.dot(weights.astype(BF16), values, preferred_element_type=F32)
    return out / total


NT = (((1,), (1,)), ((), ()))


def cold_kernel(got_ref, out_ref):
    devices, tiles, _, hd = got_ref.shape
    heads = tiles // 3
    slots = devices * COLD
    scale = hd ** (-0.5) * LOG2E
    extra = got_ref[:, 3 * heads].astype(F32)
    spread = jnp.broadcast_to(
        extra[:, 2 * SHARE : 2 * SHARE + 1], (devices, COLD, LANES)
    ).reshape(slots, LANES)
    pick = iota((slots, LANES), 1) - iota((slots, LANES), 0) % COLD
    ones = jnp.ones((LANES, LANES), BF16)
    part = 512
    causal = iota((part, part), 1) <= iota((part, part), 0)
    for h in range(heads):
        tags = jnp.where(pick == COLD * h, spread, 0.0).astype(BF16)
        label_cols = jnp.dot(tags, ones, preferred_element_type=F32)
        q, k, v = (
            got_ref[:, 3 * h + j].astype(F32).reshape(slots, hd).astype(BF16) for j in range(3)
        )
        marked = label_cols == (iota((slots, LANES), 1) + 1).astype(F32)
        q = jnp.concatenate([q, jnp.where(marked, MARK_Q, 0.0).astype(BF16)], axis=1)
        k = jnp.concatenate([k, jnp.where(marked, MARK_K, 0.0).astype(BF16)], axis=1)
        for c in range(slots // part):
            stop = (c + 1) * part
            scores = lax.dot_general(
                q[c * part : stop], k[:stop], NT, preferred_element_type=F32
            )
            last = jnp.where(causal, scores[:, c * part :], NEG_FILL)
            if c > 0:
                last = jnp.concatenate([scores[:, : c * part], last], axis=1)
            top = jnp.max(last, axis=1, keepdims=True)
            weights = jnp.exp2((last - top) * scale)
            total = jnp.sum(weights, axis=1, keepdims=True)
            out = jnp.dot(weights.astype(BF16), v[:stop], preferred_element_type=F32) / total
            devs = slice(c * part // COLD, stop // COLD)
            out_ref[devs, h] = out.reshape(part // COLD, COLD, hd).astype(BF16)


def mid_kernel(got_ref, kv_ref):
    devices, tiles, _, hd = got_ref.shape
    slots = devices * COLD
    keys = devices * SHARE
    extra = got_ref[:, tiles - 1].astype(F32).reshape(slots, hd).astype(BF16)
    n = iota((keys, 1), 0)
    source, at = n // SHARE, n % SHARE
    col = iota((keys, slots), 1)

    def rows_at(offset):
        place = (col == source * COLD + offset).astype(BF16)
        return jnp.dot(place, extra, preferred_element_type=F32)

    kv_ref[0:48] = rows_at(at).reshape(48, COLD, hd).astype(BF16)
    kv_ref[48:96] = rows_at(at + SHARE).reshape(48, COLD, hd).astype(BF16)
    y, core, z = (lax.axis_index(a) for a in ("y", "core", "z"))
    lane = HOT_LANE + HOT * y + SHARE * (z * 2 + core) + at
    tags = jnp.where(iota((keys, hd), 1) == lane, rows_at(COLD - 1), 0.0).astype(BF16)
    flat = lax.dot_general(jnp.ones((COLD, hd), BF16), tags, NT, preferred_element_type=F32)
    label = [flat[0:1, j * LANES : (j + 1) * LANES] for j in range(keys // LANES)]
    label.append(jnp.zeros((COLD - len(label), LANES), F32))
    kv_ref[96] = jnp.concatenate(label, axis=0).astype(BF16)


def hot_kernel(
    b0_ref, b1_ref, b2_ref, b3_ref, near_ref, far_ref,
    o0_ref, o1_ref, o2_ref, o3_ref, all_ref, k_ref, v_ref, o_ref,
):
    hd = b0_ref.shape[-1]
    rows = 4 * HOT
    keys = k_ref.shape[0] // 8
    scale = hd ** (-0.5) * LOG2E
    y, x, core, z = (lax.axis_index(a) for a in ("y", "x", "core", "z"))
    for d, ref in enumerate((b0_ref, b1_ref, b2_ref, b3_ref)):
        all_ref[lax.rem(y + 4 - d, 4)] = ref[...].astype(F32)
    q = all_ref[:, 0:3].reshape(rows, hd).astype(BF16)
    label_col = all_ref[:, 3:6].reshape(rows, hd)[:, 0:1]
    row = iota((rows, 1), 0)
    asked_at = (((z * 2 + core) * 16 + x * 4) * HOT + row).astype(F32)
    n = iota((1, keys), 1)
    key_at = (n // SHARE) * HOT + n % SHARE
    allowed = []
    for dc, ref in enumerate((near_ref, far_ref)):
        for dz in range(4):
            tile = 97 * dz
            at = slice((dc * 4 + dz) * keys, (dc * 4 + dz + 1) * keys)
            k_ref[at] = ref[tile : tile + 48].astype(F32).reshape(keys, hd).astype(BF16)
            v_ref[at] = ref[tile + 48 : tile + 96].astype(F32).reshape(keys, hd).astype(BF16)
            tags = ref[tile + 96].astype(F32)
            label = jnp.concatenate([tags[j : j + 1] for j in range(keys // LANES)], axis=1)
            share = lax.rem(z + 4 - dz, 4) * 2 + lax.rem(core + dc, 2)
            there = (key_at + SHARE * share).astype(F32)
            allowed.append((label_col == label) & (there <= asked_at))
    scores = lax.dot_general(q, k_ref[...], NT, preferred_element_type=F32)
    out = softmax_rows(scores, jnp.concatenate(allowed, axis=1), scale, v_ref[...])
    o_ref[...] = out.reshape(4, 3, COLD, hd)
    for d, ref in enumerate((o0_ref, o1_ref, o2_ref, o3_ref)):
        ref[...] = o_ref[lax.rem(y + 4 - d, 4)].astype(BF16)


def unpack_kernel(table_ref, back_ref, o0_ref, o1_ref, o2_ref, o3_ref, out_ref, hot_ref):
    devices, heads, _, hd = back_ref.shape
    tokens = table_ref.shape[1]
    cols = columns_of(table_ref[...])
    slots = devices * COLD
    part = 256
    for d, ref in enumerate((o0_ref, o1_ref, o2_ref, o3_ref)):
        hot_ref[d] = ref[...].astype(F32)
    for h in range(heads):
        rows = back_ref[:, h].astype(F32).reshape(slots, hd).astype(BF16)
        hot = hot_ref[lax.rem(h + 4 - lax.axis_index("y"), 4)].reshape(HOT, hd)
        hot = jnp.concatenate([hot, jnp.zeros((LANES - HOT, hd), F32)], axis=0).astype(BF16)
        for c in range(tokens // part):
            slot = cols[c * part : (c + 1) * part, h : h + 1].astype(jnp.int32)
            place = (slot == lax.broadcasted_iota(jnp.int32, (part, slots), 1)).astype(BF16)
            hot_place = (
                slot == lax.broadcasted_iota(jnp.int32, (part, LANES), 1) + slots
            ).astype(BF16)
            got = jnp.dot(place, rows, preferred_element_type=F32) + jnp.dot(
                hot_place, hot, preferred_element_type=F32
            )
            out_ref[c * part : (c + 1) * part, h * hd : (h + 1) * hd] = got.astype(BF16)


VMEM = pl.BlockSpec(memory_space=pltpu.VMEM)
HBM = pl.BlockSpec(memory_space=pl.ANY)
AXES = ("z", "core", "x", "y")
MIB = 1024 * 1024


def call(kernel, name, limit, ins, outs, scratch, *arrays, flops=None):
    return pl.pallas_call(
        kernel,
        out_shape=tuple(jax.ShapeDtypeStruct(*out[1:]) for out in outs),
        in_specs=ins,
        out_specs=tuple(out[0] for out in outs),
        scratch_shapes=scratch,
        compiler_params=pltpu.CompilerParams(vmem_limit_bytes=limit * MIB),
        name=name,
        cost_estimate=None if flops is None else pl.CostEstimate(flops=flops, bytes_accessed=0, transcendentals=0),
    )(*arrays)


def shift(block, axis, by):
    size = lax.axis_size(axis)
    return lax.ppermute(block, axis, [(i, (i + by) % size) for i in range(size)])


def local(query_rows, key_rows, value_rows, cluster_ids):
    devices = lax.axis_size(AXES)
    heads, tokens = cluster_ids.shape
    hd = query_rows.shape[1] // heads
    tile = (COLD, hd)
    payload = (devices, 3 * heads + 1, *tile)
    table, h0, h1, h2, h3, send = call(
        pack_kernel, "pack", 58, [VMEM, HBM, HBM, HBM],
        [(VMEM, (2 * heads, tokens), F32)] + [(VMEM, (6, *tile), BF16)] * 4 + [(HBM, payload, BF16)],
        [
            pltpu.VMEM((heads, tokens, 3 * hd), BF16),
            pltpu.VMEM((heads, 6, *tile), BF16), pltpu.VMEM(payload, BF16),
            pltpu.SemaphoreType.DMA((3 * heads,)), pltpu.SemaphoreType.DMA((4,)),
        ],
        cluster_ids, query_rows, key_rows, value_rows,
    )
    got = lax.all_to_all(send, AXES, split_axis=0, concat_axis=0, tiled=True)
    asked = [h0] + [shift(b, "y", d + 1) for d, b in enumerate((h1, h2, h3))]
    got, asked = lax.optimization_barrier((got, asked))
    (kv,) = call(mid_kernel, "mid", 24, [VMEM], [(VMEM, (97, *tile), BF16)], [], got)
    got, kv = lax.optimization_barrier((got, kv))
    near = [kv] + [shift(kv, "z", d) for d in (1, 2, 3)]
    (answer,) = call(
        cold_kernel, "cold", 24, [VMEM], [(VMEM, (devices, heads, *tile), BF16)], [], got, flops=20_000_000_000,
    )
    near, _ = lax.optimization_barrier((near, answer))
    near = jnp.concatenate(near, axis=0)
    far = shift(near, "core", 1)
    outs = call(
        hot_kernel, "hot", 24, [VMEM] * 6, [(VMEM, (3, *tile), BF16)] * 4,
        [
            pltpu.VMEM((4, 6, *tile), F32), pltpu.VMEM((devices * HOT, hd), BF16),
            pltpu.VMEM((devices * HOT, hd), BF16), pltpu.VMEM((4, 3, *tile), F32),
        ],
        *asked, near, far,
        flops=2_000_000_000,
    )
    hot_out = [outs[0]] + [shift(b, "y", 3 - d) for d, b in enumerate(outs[1:])]
    back = lax.all_to_all(answer, AXES, split_axis=0, concat_axis=0, tiled=True)
    (result,) = call(
        unpack_kernel, "unpack", 24, [VMEM] * 6, [(VMEM, (tokens, heads * hd), BF16)],
        [pltpu.VMEM((4, 3, *tile), F32)],
        table, back, *hot_out,
    )
    return result


def solution(mesh):
    split = jax.sharding.Mesh(mesh.devices.reshape(4, 2, 4, 4), AXES)
    return jax.shard_map(
        local,
        mesh=split,
        in_specs=(P(AXES, None), P(AXES, None), P(AXES, None), P(None, AXES)),
        out_specs=P(AXES, None),
        check_vma=False,
    )
```

```python
import jax
import jax.numpy as jnp
from jax import lax
from jax.experimental import pallas as pl
from jax.experimental.pallas import tpu as pltpu
from jax.sharding import PartitionSpec as P

CL_DEV = 8
COLD = 8
HOT = 24
HOT_PAD = 32
LANES = 128
NEG_FILL = -1e30
SHARE = 3
HOT_LANE = 32
MARK_Q = 104.0
MARK_K = 100.0
LOG2E = 1.4426950408889634
F32 = jnp.float32
BF16 = jnp.bfloat16


def iota(shape, dim):
    return lax.broadcasted_iota(jnp.int32, shape, dim)


def columns_of(table):
    tokens = table.shape[1]
    return jnp.transpose(
        jnp.concatenate([table, jnp.zeros((LANES - table.shape[0], tokens), F32)], axis=0)
    )


def pack_kernel(
    ids_hbm, q_hbm, k_hbm, v_hbm,
    table_hbm, h0_hbm, h1_hbm, h2_hbm, h3_hbm, send_hbm,
    ids_ref, table_ref, x_ref, hot_ref, send_ref, sems, out_sems,
):
    heads, tokens = ids_ref.shape
    hd = q_hbm.shape[1] // heads
    devices = send_ref.shape[0]
    slots = devices * COLD
    step = 256
    ids_load = pltpu.make_async_copy(ids_hbm, ids_ref, sems.at[3 * heads])
    ids_load.start()
    loads = [
        [
            pltpu.make_async_copy(
                src.at[:, h * hd : (h + 1) * hd], x_ref.at[h, :, j * hd : (j + 1) * hd], sems.at[3 * h + j]
            )
            for j, src in enumerate((q_hbm, k_hbm, v_hbm))
        ]
        for h in range(heads)
    ]
    for row in loads:
        for load in row:
            load.start()
    ids_load.wait()
    ids = ids_ref[...]
    owner = ids // CL_DEV
    tags = (ids - owner * CL_DEV + 1).astype(F32)
    upper = (iota((step, step), 0) < iota((step, step), 1)).astype(BF16)
    dev_col = iota((devices, step), 0)
    slot_rows = []
    labels = jnp.zeros((devices, LANES), F32)
    for h in range(heads):
        carry = jnp.zeros((devices, 1), F32)
        ones, ranks = [], []
        for b in range(tokens // step):
            one = (owner[h : h + 1, b * step : (b + 1) * step] == dev_col).astype(F32)
            inside = jnp.dot(one.astype(BF16), upper, preferred_element_type=F32) + carry
            carry = carry + jnp.sum(one, axis=1, keepdims=True)
            ones.append(one)
            ranks.append(jnp.sum(one * inside, axis=0, keepdims=True))
        full = (carry > COLD).astype(F32)
        for b, one in enumerate(ones):
            ranks[b] = jnp.where(
                jnp.sum(one * full, axis=0, keepdims=True) > 0.5, ranks[b] + slots, ranks[b]
            )
            lane = jnp.where(
                ranks[b] < COLD, ranks[b] + COLD * h, ranks[b] + (HOT_LANE + HOT * h - slots)
            ).astype(jnp.int32)
            tag = jnp.where(
                lane == iota((LANES, step), 0), tags[h : h + 1, b * step : (b + 1) * step], 0.0
            )
            labels = labels + lax.dot_general(
                one.astype(BF16), tag.astype(BF16), NT, preferred_element_type=F32
            )
        rank = jnp.concatenate(ranks, axis=1).astype(jnp.int32)
        slot_rows.append(jnp.where(rank >= slots, rank, owner[h : h + 1] * COLD + rank))
    slot_all = jnp.concatenate(slot_rows, axis=0)
    table_ref[...] = jnp.concatenate([slot_all.astype(F32), tags], axis=0)
    sent = [pltpu.make_async_copy(table_ref, table_hbm, out_sems.at[4])]
    sent[0].start()
    asked_tags = jnp.sum(labels, axis=0, keepdims=True)
    cold_lane = iota((1, LANES), 1) < HOT_LANE
    for h in range(heads):
        own = iota((HOT, LANES), 1) == iota((HOT, LANES), 0) + (HOT_LANE + HOT * h)
        tag = jnp.sum(jnp.where(own, asked_tags, 0.0), axis=1, keepdims=True)
        hot_ref[h, 3:6] = jnp.broadcast_to(tag, (HOT, hd)).reshape(3, COLD, hd).astype(BF16)
    rows = HOT // SHARE * COLD
    row = iota((rows + HOT_PAD, 1), 0)
    row_share, row_at = row // COLD, row % COLD
    want = jnp.where(row_at < SHARE, SHARE * row_share + row_at, SHARE * (row_share - 1) + row_at)
    want = jnp.where(row_at < 2 * SHARE, want, -9)
    want = jnp.where(row < rows, want, row - rows) + slots
    tile_at = iota((rows, hd), 0) % COLD
    hot_tiles = []
    for h in range(heads):
        for load in loads[h]:
            load.wait()
        moved = jnp.dot(
            (slot_all[h : h + 1] == want).astype(BF16), x_ref[h], preferred_element_type=F32
        )
        tiles = jnp.where(tile_at < SHARE, moved[:rows, hd : 2 * hd], moved[:rows, 2 * hd :])
        tiles = jnp.where(tile_at == COLD - 1, asked_tags, tiles)
        hot_tiles.append(tiles)
        hot_ref[h, 0:3] = moved[rows : rows + HOT, :hd].reshape(3, COLD, hd).astype(BF16)
    y = lax.axis_index("y")
    for d, ref in enumerate((h0_hbm, h1_hbm, h2_hbm, h3_hbm)):
        sent.append(pltpu.make_async_copy(hot_ref.at[lax.rem(y + d, heads)], ref, out_sems.at[5 + d]))
        sent[-1].start()
    labels = jnp.where(cold_lane, labels, 0.0)
    part = 256
    sub = iota((COLD, LANES), 0)
    for c in range(slots // part):
        first, stop = c * part // COLD, (c + 1) * part // COLD
        for h in range(heads):
            place = (slot_all[h : h + 1] == iota((part, tokens), 0) + c * part).astype(BF16)
            moved = jnp.dot(place, x_ref[h], preferred_element_type=F32)
            for j in range(3):
                send_ref[first:stop, 3 * h + j] = (
                    moved[:, j * hd : (j + 1) * hd].reshape(stop - first, COLD, hd).astype(BF16)
                )
        for dev in range(first, stop):
            share, head = dev // 16, dev % heads
            tile = hot_tiles[head][share * COLD : (share + 1) * COLD]
            tile = jnp.where(sub == 2 * SHARE, labels[dev : dev + 1], tile)
            send_ref[dev, 3 * heads] = tile.astype(BF16)
        out = pltpu.make_async_copy(
            send_ref.at[first:stop], send_hbm.at[first:stop], out_sems.at[c]
        )
        out.start()
        sent.append(out)
    for out in sent:
        out.wait()


def softmax_rows(scores, allowed, scale, values):
    masked = jnp.where(allowed, scores, NEG_FILL)
    top = jnp.max(masked, axis=1, keepdims=True)
    weights = jnp.exp2((masked - top) * scale)
    total = jnp.sum(weights, axis=1, keepdims=True)
    out = jnp.dot(weights.astype(BF16), values, preferred_element_type=F32)
    return out / total


NT = (((1,), (1,)), ((), ()))


def cold_kernel(got_ref, out_hbm, out_ref, out_sems):
    devices, tiles, _, hd = got_ref.shape
    heads = tiles // 3
    slots = devices * COLD
    scale = hd ** (-0.5) * LOG2E
    extra = got_ref[:, 3 * heads].astype(F32)
    spread = jnp.broadcast_to(
        extra[:, 2 * SHARE : 2 * SHARE + 1], (devices, COLD, LANES)
    ).reshape(slots, LANES)
    pick = iota((slots, LANES), 1) - iota((slots, LANES), 0) % COLD
    ones = jnp.ones((LANES, LANES), BF16)
    part = 512
    causal = iota((part, part), 1) <= iota((part, part), 0)
    sent = []
    for h in range(heads):
        tags = jnp.where(pick == COLD * h, spread, 0.0).astype(BF16)
        label_cols = jnp.dot(tags, ones, preferred_element_type=F32)
        q, k, v = (
            got_ref[:, 3 * h + j].astype(F32).reshape(slots, hd).astype(BF16) for j in range(3)
        )
        marked = label_cols == (iota((slots, LANES), 1) + 1).astype(F32)
        q = jnp.concatenate([q, jnp.where(marked, MARK_Q, 0.0).astype(BF16)], axis=1)
        k = jnp.concatenate([k, jnp.where(marked, MARK_K, 0.0).astype(BF16)], axis=1)
        for c in range(slots // part):
            stop = (c + 1) * part
            scores = lax.dot_general(
                q[c * part : stop], k[:stop], NT, preferred_element_type=F32
            )
            last = jnp.where(causal, scores[:, c * part :], NEG_FILL)
            if c > 0:
                last = jnp.concatenate([scores[:, : c * part], last], axis=1)
            top = jnp.max(last, axis=1, keepdims=True)
            weights = jnp.exp2((last - top) * scale)
            total = jnp.sum(weights, axis=1, keepdims=True)
            out = jnp.dot(weights.astype(BF16), v[:stop], preferred_element_type=F32) / total
            devs = slice(c * part // COLD, stop // COLD)
            out_ref[devs, h] = out.reshape(part // COLD, COLD, hd).astype(BF16)
        out = pltpu.make_async_copy(out_ref.at[:, h], out_hbm.at[:, h], out_sems.at[h])
        out.start()
        sent.append(out)
    for out in sent:
        out.wait()


def mid_kernel(got_ref, kv_ref):
    devices, tiles, _, hd = got_ref.shape
    slots = devices * COLD
    keys = devices * SHARE
    extra = got_ref[:, tiles - 1].astype(F32).reshape(slots, hd).astype(BF16)
    n = iota((keys, 1), 0)
    source, at = n // SHARE, n % SHARE
    col = iota((keys, slots), 1)

    def rows_at(offset):
        place = (col == source * COLD + offset).astype(BF16)
        return jnp.dot(place, extra, preferred_element_type=F32)

    kv_ref[0:48] = rows_at(at).reshape(48, COLD, hd).astype(BF16)
    kv_ref[48:96] = rows_at(at + SHARE).reshape(48, COLD, hd).astype(BF16)
    y, core, z = (lax.axis_index(a) for a in ("y", "core", "z"))
    lane = HOT_LANE + HOT * y + SHARE * (z * 2 + core) + at
    tags = jnp.where(iota((keys, hd), 1) == lane, rows_at(COLD - 1), 0.0).astype(BF16)
    flat = lax.dot_general(jnp.ones((COLD, hd), BF16), tags, NT, preferred_element_type=F32)
    label = [flat[0:1, j * LANES : (j + 1) * LANES] for j in range(keys // LANES)]
    label.append(jnp.zeros((COLD - len(label), LANES), F32))
    kv_ref[96] = jnp.concatenate(label, axis=0).astype(BF16)


def hot_kernel(
    b0_ref, b1_ref, b2_ref, b3_ref, near_ref, far_ref,
    o0_ref, o1_ref, o2_ref, o3_ref, all_ref, k_ref, v_ref, o_ref,
):
    hd = b0_ref.shape[-1]
    rows = 4 * HOT
    keys = k_ref.shape[0] // 8
    scale = hd ** (-0.5) * LOG2E
    y, x, core, z = (lax.axis_index(a) for a in ("y", "x", "core", "z"))
    for d, ref in enumerate((b0_ref, b1_ref, b2_ref, b3_ref)):
        all_ref[lax.rem(y + 4 - d, 4)] = ref[...].astype(F32)
    q = all_ref[:, 0:3].reshape(rows, hd).astype(BF16)
    label_col = all_ref[:, 3:6].reshape(rows, hd)[:, 0:1]
    row = iota((rows, 1), 0)
    asked_at = (((z * 2 + core) * 16 + x * 4) * HOT + row).astype(F32)
    n = iota((1, keys), 1)
    key_at = (n // SHARE) * HOT + n % SHARE
    allowed = []
    for dc, ref in enumerate((near_ref, far_ref)):
        for dz in range(4):
            tile = 97 * dz
            at = slice((dc * 4 + dz) * keys, (dc * 4 + dz + 1) * keys)
            k_ref[at] = ref[tile : tile + 48].astype(F32).reshape(keys, hd).astype(BF16)
            v_ref[at] = ref[tile + 48 : tile + 96].astype(F32).reshape(keys, hd).astype(BF16)
            tags = ref[tile + 96].astype(F32)
            label = jnp.concatenate([tags[j : j + 1] for j in range(keys // LANES)], axis=1)
            share = lax.rem(z + 4 - dz, 4) * 2 + lax.rem(core + dc, 2)
            there = (key_at + SHARE * share).astype(F32)
            allowed.append((label_col == label) & (there <= asked_at))
    scores = lax.dot_general(q, k_ref[...], NT, preferred_element_type=F32)
    out = softmax_rows(scores, jnp.concatenate(allowed, axis=1), scale, v_ref[...])
    o_ref[...] = out.reshape(4, 3, COLD, hd)
    for d, ref in enumerate((o0_ref, o1_ref, o2_ref, o3_ref)):
        ref[...] = o_ref[lax.rem(y + 4 - d, 4)].astype(BF16)


def unpack_kernel(table_ref, back_ref, o0_ref, o1_ref, o2_ref, o3_ref, out_hbm, hot_ref, out_ref, sems):
    devices, heads, _, hd = back_ref.shape
    tokens = table_ref.shape[1]
    cols = columns_of(table_ref[...])
    slots = devices * COLD
    part = 256
    for d, ref in enumerate((o0_ref, o1_ref, o2_ref, o3_ref)):
        hot_ref[d] = ref[...].astype(F32)
    y = lax.axis_index("y")
    rows, hots = [], []
    for h in range(heads):
        rows.append(back_ref[:, h].astype(F32).reshape(slots, hd).astype(BF16))
        hot = hot_ref[lax.rem(h + 4 - y, 4)].reshape(HOT, hd)
        hots.append(jnp.concatenate([hot, jnp.zeros((LANES - HOT, hd), F32)], axis=0).astype(BF16))
    sent = []
    for c in range(tokens // part):
        at = slice(c * part, (c + 1) * part)
        for h in range(heads):
            slot = cols[at, h : h + 1].astype(jnp.int32)
            place = (slot == iota((part, slots), 1)).astype(BF16)
            hot_place = (slot == iota((part, LANES), 1) + slots).astype(BF16)
            got = jnp.dot(place, rows[h], preferred_element_type=F32) + jnp.dot(
                hot_place, hots[h], preferred_element_type=F32
            )
            out_ref[at, h * hd : (h + 1) * hd] = got.astype(BF16)
        out = pltpu.make_async_copy(out_ref.at[at], out_hbm.at[at], sems.at[c])
        out.start()
        sent.append(out)
    for out in sent:
        out.wait()


VMEM = pl.BlockSpec(memory_space=pltpu.VMEM)
HBM = pl.BlockSpec(memory_space=pl.ANY)
AXES = ("z", "core", "x", "y")
MIB = 1024 * 1024


def call(kernel, name, limit, ins, outs, scratch, *arrays, flops=None):
    return pl.pallas_call(
        kernel,
        out_shape=tuple(
            pltpu.HBM(*out[1:]) if out[0] is HBM else jax.ShapeDtypeStruct(*out[1:]) for out in outs
        ),
        in_specs=ins,
        out_specs=tuple(out[0] for out in outs),
        scratch_shapes=scratch,
        compiler_params=pltpu.CompilerParams(vmem_limit_bytes=limit * MIB),
        name=name,
        cost_estimate=None if flops is None else pl.CostEstimate(flops=flops, bytes_accessed=0, transcendentals=0),
    )(*arrays)


def shift(block, axis, by):
    size = lax.axis_size(axis)
    return lax.ppermute(block, axis, [(i, (i + by) % size) for i in range(size)])


def local(query_rows, key_rows, value_rows, cluster_ids):
    devices = lax.axis_size(AXES)
    heads, tokens = cluster_ids.shape
    hd = query_rows.shape[1] // heads
    tile = (COLD, hd)
    payload = (devices, 3 * heads + 1, *tile)
    table, h0, h1, h2, h3, send = call(
        pack_kernel, "pack", 58, [HBM] * 4,
        [(HBM, (2 * heads, tokens), F32)] + [(HBM, (6, *tile), BF16)] * 4 + [(HBM, payload, BF16)],
        [
            pltpu.VMEM((heads, tokens), jnp.int32), pltpu.VMEM((2 * heads, tokens), F32),
            pltpu.VMEM((heads, tokens, 3 * hd), BF16),
            pltpu.VMEM((heads, 6, *tile), BF16), pltpu.VMEM(payload, BF16),
            pltpu.SemaphoreType.DMA((3 * heads + 1,)), pltpu.SemaphoreType.DMA((9,)),
        ],
        cluster_ids, query_rows, key_rows, value_rows,
    )
    got = lax.all_to_all(send, AXES, split_axis=0, concat_axis=0, tiled=True)
    asked = [h0] + [shift(b, "y", d + 1) for d, b in enumerate((h1, h2, h3))]
    got, asked = lax.optimization_barrier((got, asked))
    (kv,) = call(mid_kernel, "mid", 24, [VMEM], [(VMEM, (97, *tile), BF16)], [], got)
    got, kv = lax.optimization_barrier((got, kv))
    near = [kv] + [shift(kv, "z", d) for d in (1, 2, 3)]
    (answer,) = call(
        cold_kernel, "cold", 24, [VMEM], [(HBM, (devices, heads, *tile), BF16)],
        [pltpu.VMEM((devices, heads, *tile), BF16), pltpu.SemaphoreType.DMA((heads,))],
        got, flops=20_000_000_000,
    )
    near, _ = lax.optimization_barrier((near, answer))
    near = jnp.concatenate(near, axis=0)
    far = shift(near, "core", 1)
    outs = call(
        hot_kernel, "hot", 24, [VMEM] * 6, [(VMEM, (3, *tile), BF16)] * 4,
        [
            pltpu.VMEM((4, 6, *tile), F32), pltpu.VMEM((devices * HOT, hd), BF16),
            pltpu.VMEM((devices * HOT, hd), BF16), pltpu.VMEM((4, 3, *tile), F32),
        ],
        *asked, near, far,
        flops=2_000_000_000,
    )
    hot_out = [outs[0]] + [shift(b, "y", 3 - d) for d, b in enumerate(outs[1:])]
    back = lax.all_to_all(answer, AXES, split_axis=0, concat_axis=0, tiled=True)
    (result,) = call(
        unpack_kernel, "unpack", 24, [VMEM] * 6, [(HBM, (tokens, heads * hd), BF16)],
        [
            pltpu.VMEM((4, 3, *tile), F32), pltpu.VMEM((tokens, heads * hd), BF16),
            pltpu.SemaphoreType.DMA((4,)),
        ],
        table, back, *hot_out,
    )
    return result


def solution(mesh):
    split = jax.sharding.Mesh(mesh.devices.reshape(4, 2, 4, 4), AXES)
    return jax.shard_map(
        local,
        mesh=split,
        in_specs=(P(AXES, None), P(AXES, None), P(AXES, None), P(None, AXES)),
        out_specs=P(AXES, None),
        check_vma=False,
    )
```

```python
import jax
import jax.numpy as jnp
from jax import lax
from jax.experimental import pallas as pl
from jax.experimental.pallas import tpu as pltpu
from jax.sharding import PartitionSpec as P

CL_DEV = 8
COLD = 8
HOT = 24
HOT_PAD = 32
LANES = 128
NEG_FILL = -1e30
SHARE = 3
HOT_LANE = 32
MARK_Q = 104.0
MARK_K = 100.0
LOG2E = 1.4426950408889634
F32 = jnp.float32
BF16 = jnp.bfloat16


def iota(shape, dim):
    return lax.broadcasted_iota(jnp.int32, shape, dim)


def columns_of(table):
    tokens = table.shape[1]
    return jnp.transpose(
        jnp.concatenate([table, jnp.zeros((LANES - table.shape[0], tokens), F32)], axis=0)
    )


def pack_kernel(
    ids_hbm, q_hbm, k_hbm, v_hbm,
    table_hbm, h0_hbm, h1_hbm, h2_hbm, h3_hbm, send_hbm,
    ids_ref, table_ref, q_ref, k_ref, v_ref, hot_ref, send_ref, sems, out_sems,
):
    heads, tokens = ids_ref.shape
    hd = q_hbm.shape[1] // heads
    devices = send_ref.shape[0]
    slots = devices * COLD
    step = 256
    ids_load = pltpu.make_async_copy(ids_hbm, ids_ref, sems.at[3 * heads])
    ids_load.start()
    loads = [
        pltpu.make_async_copy(src.at[r * 512 : (r + 1) * 512], dst.at[r * 512 : (r + 1) * 512], sems.at[2 * j + r])
        for j, (src, dst) in enumerate(((q_hbm, q_ref), (k_hbm, k_ref), (v_hbm, v_ref)))
        for r in range(2)
    ]
    for load in loads:
        load.start()
    ids_load.wait()
    ids = ids_ref[...]
    owner = ids // CL_DEV
    tags = (ids - owner * CL_DEV + 1).astype(F32)
    upper = (iota((step, step), 0) < iota((step, step), 1)).astype(BF16)
    dev_col = iota((devices, step), 0)
    slot_rows = []
    labels = jnp.zeros((devices, LANES), F32)
    for h in range(heads):
        carry = jnp.zeros((devices, 1), F32)
        ones, ranks = [], []
        for b in range(tokens // step):
            one = (owner[h : h + 1, b * step : (b + 1) * step] == dev_col).astype(F32)
            inside = jnp.dot(one.astype(BF16), upper, preferred_element_type=F32) + carry
            carry = carry + jnp.sum(one, axis=1, keepdims=True)
            ones.append(one)
            ranks.append(jnp.sum(one * inside, axis=0, keepdims=True))
        full = (carry > COLD).astype(F32)
        for b, one in enumerate(ones):
            ranks[b] = jnp.where(
                jnp.sum(one * full, axis=0, keepdims=True) > 0.5, ranks[b] + slots, ranks[b]
            )
            lane = jnp.where(
                ranks[b] < COLD, ranks[b] + COLD * h, ranks[b] + (HOT_LANE + HOT * h - slots)
            ).astype(jnp.int32)
            tag = jnp.where(
                lane == iota((LANES, step), 0), tags[h : h + 1, b * step : (b + 1) * step], 0.0
            )
            labels = labels + lax.dot_general(
                one.astype(BF16), tag.astype(BF16), NT, preferred_element_type=F32
            )
        rank = jnp.concatenate(ranks, axis=1).astype(jnp.int32)
        slot_rows.append(jnp.where(rank >= slots, rank, owner[h : h + 1] * COLD + rank))
    slot_all = jnp.concatenate(slot_rows, axis=0)
    table_ref[...] = jnp.concatenate([slot_all.astype(F32), tags], axis=0)
    sent = [pltpu.make_async_copy(table_ref, table_hbm, out_sems.at[4])]
    sent[0].start()
    asked_tags = jnp.sum(labels, axis=0, keepdims=True)
    cold_lane = iota((1, LANES), 1) < HOT_LANE
    for h in range(heads):
        own = iota((HOT, LANES), 1) == iota((HOT, LANES), 0) + (HOT_LANE + HOT * h)
        tag = jnp.sum(jnp.where(own, asked_tags, 0.0), axis=1, keepdims=True)
        hot_ref[h, 3:6] = jnp.broadcast_to(tag, (HOT, hd)).reshape(3, COLD, hd).astype(BF16)
    rows = HOT // SHARE * COLD
    row = iota((rows + HOT_PAD, 1), 0)
    row_share, row_at = row // COLD, row % COLD
    want = jnp.where(row_at < SHARE, SHARE * row_share + row_at, SHARE * (row_share - 1) + row_at)
    want = jnp.where(row_at < 2 * SHARE, want, -9)
    want = jnp.where(row < rows, want, row - rows) + slots
    tile_at = iota((rows, hd), 0) % COLD
    hot_tiles = []
    xs = []
    for load in loads:
        load.wait()
    for h in range(heads):
        xs.append(jnp.concatenate([ref[:, h * hd : (h + 1) * hd] for ref in (q_ref, k_ref, v_ref)], axis=1))
        moved = jnp.dot(
            (slot_all[h : h + 1] == want).astype(BF16), xs[h], preferred_element_type=F32
        )
        tiles = jnp.where(tile_at < SHARE, moved[:rows, hd : 2 * hd], moved[:rows, 2 * hd :])
        tiles = jnp.where(tile_at == COLD - 1, asked_tags, tiles)
        hot_tiles.append(tiles)
        hot_ref[h, 0:3] = moved[rows : rows + HOT, :hd].reshape(3, COLD, hd).astype(BF16)
    y = lax.axis_index("y")
    for d, ref in enumerate((h0_hbm, h1_hbm, h2_hbm, h3_hbm)):
        sent.append(pltpu.make_async_copy(hot_ref.at[lax.rem(y + d, heads)], ref, out_sems.at[5 + d]))
        sent[-1].start()
    labels = jnp.where(cold_lane, labels, 0.0)
    part = 256
    sub = iota((COLD, LANES), 0)
    for c in range(slots // part):
        first, stop = c * part // COLD, (c + 1) * part // COLD
        for h in range(heads):
            place = (slot_all[h : h + 1] == iota((part, tokens), 0) + c * part).astype(BF16)
            moved = jnp.dot(place, xs[h], preferred_element_type=F32)
            for j in range(3):
                send_ref[first:stop, 3 * h + j] = (
                    moved[:, j * hd : (j + 1) * hd].reshape(stop - first, COLD, hd).astype(BF16)
                )
        for dev in range(first, stop):
            share, head = dev // 16, dev % heads
            tile = hot_tiles[head][share * COLD : (share + 1) * COLD]
            tile = jnp.where(sub == 2 * SHARE, labels[dev : dev + 1], tile)
            send_ref[dev, 3 * heads] = tile.astype(BF16)
        out = pltpu.make_async_copy(
            send_ref.at[first:stop], send_hbm.at[first:stop], out_sems.at[c]
        )
        out.start()
        sent.append(out)
    for out in sent:
        out.wait()


def softmax_rows(scores, allowed, scale, values):
    masked = jnp.where(allowed, scores, NEG_FILL)
    top = jnp.max(masked, axis=1, keepdims=True)
    weights = jnp.exp2((masked - top) * scale)
    total = jnp.sum(weights, axis=1, keepdims=True)
    out = jnp.dot(weights.astype(BF16), values, preferred_element_type=F32)
    return out / total


NT = (((1,), (1,)), ((), ()))


def cold_kernel(got_ref, out_hbm, out_ref, out_sems):
    devices, tiles, _, hd = got_ref.shape
    heads = tiles // 3
    slots = devices * COLD
    scale = hd ** (-0.5) * LOG2E
    extra = got_ref[:, 3 * heads].astype(F32)
    spread = jnp.broadcast_to(
        extra[:, 2 * SHARE : 2 * SHARE + 1], (devices, COLD, LANES)
    ).reshape(slots, LANES)
    pick = iota((slots, LANES), 1) - iota((slots, LANES), 0) % COLD
    ones = jnp.ones((LANES, LANES), BF16)
    part = 512
    causal = iota((part, part), 1) <= iota((part, part), 0)
    sent = []
    for h in range(heads):
        tags = jnp.where(pick == COLD * h, spread, 0.0).astype(BF16)
        label_cols = jnp.dot(tags, ones, preferred_element_type=F32)
        q, k, v = (
            got_ref[:, 3 * h + j].astype(F32).reshape(slots, hd).astype(BF16) for j in range(3)
        )
        marked = label_cols == (iota((slots, LANES), 1) + 1).astype(F32)
        q = jnp.concatenate([q, jnp.where(marked, MARK_Q, 0.0).astype(BF16)], axis=1)
        k = jnp.concatenate([k, jnp.where(marked, MARK_K, 0.0).astype(BF16)], axis=1)
        for c in range(slots // part):
            stop = (c + 1) * part
            scores = lax.dot_general(
                q[c * part : stop], k[:stop], NT, preferred_element_type=F32
            )
            last = jnp.where(causal, scores[:, c * part :], NEG_FILL)
            if c > 0:
                last = jnp.concatenate([scores[:, : c * part], last], axis=1)
            top = jnp.max(last, axis=1, keepdims=True)
            weights = jnp.exp2((last - top) * scale)
            total = jnp.sum(weights, axis=1, keepdims=True)
            out = jnp.dot(weights.astype(BF16), v[:stop], preferred_element_type=F32) / total
            devs = slice(c * part // COLD, stop // COLD)
            out_ref[devs, h] = out.reshape(part // COLD, COLD, hd).astype(BF16)
        out = pltpu.make_async_copy(out_ref.at[:, h], out_hbm.at[:, h], out_sems.at[h])
        out.start()
        sent.append(out)
    for out in sent:
        out.wait()


def mid_kernel(got_ref, kv_hbm, kv_ref, sems):
    devices, tiles, _, hd = got_ref.shape
    slots = devices * COLD
    keys = devices * SHARE
    extra = got_ref[:, tiles - 1].astype(F32).reshape(slots, hd).astype(BF16)
    n = iota((keys, 1), 0)
    source, at = n // SHARE, n % SHARE
    col = iota((keys, slots), 1)

    def rows_at(offset):
        place = (col == source * COLD + offset).astype(BF16)
        return jnp.dot(place, extra, preferred_element_type=F32)

    parts = (slice(0, 48), slice(48, 96), slice(96, 97))
    sent = [
        pltpu.make_async_copy(kv_ref.at[part], kv_hbm.at[part], sems.at[i])
        for i, part in enumerate(parts)
    ]
    kv_ref[0:48] = rows_at(at).reshape(48, COLD, hd).astype(BF16)
    sent[0].start()
    kv_ref[48:96] = rows_at(at + SHARE).reshape(48, COLD, hd).astype(BF16)
    sent[1].start()
    y, core, z = (lax.axis_index(a) for a in ("y", "core", "z"))
    lane = HOT_LANE + HOT * y + SHARE * (z * 2 + core) + at
    tags = jnp.where(iota((keys, hd), 1) == lane, rows_at(COLD - 1), 0.0).astype(BF16)
    flat = lax.dot_general(jnp.ones((COLD, hd), BF16), tags, NT, preferred_element_type=F32)
    label = [flat[0:1, j * LANES : (j + 1) * LANES] for j in range(keys // LANES)]
    label.append(jnp.zeros((COLD - len(label), LANES), F32))
    kv_ref[96] = jnp.concatenate(label, axis=0).astype(BF16)
    sent[2].start()
    for out in sent:
        out.wait()


def hot_kernel(
    b0_ref, b1_ref, b2_ref, b3_ref, near_ref, far_ref,
    o0_ref, o1_ref, o2_ref, o3_ref, all_ref, k_ref, v_ref, o_ref,
):
    hd = b0_ref.shape[-1]
    rows = 4 * HOT
    keys = k_ref.shape[0] // 8
    scale = hd ** (-0.5) * LOG2E
    y, x, core, z = (lax.axis_index(a) for a in ("y", "x", "core", "z"))
    for d, ref in enumerate((b0_ref, b1_ref, b2_ref, b3_ref)):
        all_ref[lax.rem(y + 4 - d, 4)] = ref[...].astype(F32)
    q = all_ref[:, 0:3].reshape(rows, hd).astype(BF16)
    label_col = all_ref[:, 3:6].reshape(rows, hd)[:, 0:1]
    row = iota((rows, 1), 0)
    asked_at = (((z * 2 + core) * 16 + x * 4) * HOT + row).astype(F32)
    n = iota((1, keys), 1)
    key_at = (n // SHARE) * HOT + n % SHARE
    allowed = []
    for dc, ref in enumerate((near_ref, far_ref)):
        for dz in range(4):
            tile = 97 * dz
            at = slice((dc * 4 + dz) * keys, (dc * 4 + dz + 1) * keys)
            k_ref[at] = ref[tile : tile + 48].astype(F32).reshape(keys, hd).astype(BF16)
            v_ref[at] = ref[tile + 48 : tile + 96].astype(F32).reshape(keys, hd).astype(BF16)
            tags = ref[tile + 96].astype(F32)
            label = jnp.concatenate([tags[j : j + 1] for j in range(keys // LANES)], axis=1)
            share = lax.rem(z + 4 - dz, 4) * 2 + lax.rem(core + dc, 2)
            there = (key_at + SHARE * share).astype(F32)
            allowed.append((label_col == label) & (there <= asked_at))
    scores = lax.dot_general(q, k_ref[...], NT, preferred_element_type=F32)
    out = softmax_rows(scores, jnp.concatenate(allowed, axis=1), scale, v_ref[...])
    o_ref[...] = out.reshape(4, 3, COLD, hd)
    for d, ref in enumerate((o0_ref, o1_ref, o2_ref, o3_ref)):
        ref[...] = o_ref[lax.rem(y + 4 - d, 4)].astype(BF16)


def unpack_kernel(table_ref, back_ref, o0_ref, o1_ref, o2_ref, o3_ref, out_hbm, hot_ref, out_ref, sems):
    devices, heads, _, hd = back_ref.shape
    tokens = table_ref.shape[1]
    cols = columns_of(table_ref[...])
    slots = devices * COLD
    part = 256
    for d, ref in enumerate((o0_ref, o1_ref, o2_ref, o3_ref)):
        hot_ref[d] = ref[...].astype(F32)
    y = lax.axis_index("y")
    rows, hots = [], []
    for h in range(heads):
        rows.append(back_ref[:, h].astype(F32).reshape(slots, hd).astype(BF16))
        hot = hot_ref[lax.rem(h + 4 - y, 4)].reshape(HOT, hd)
        hots.append(jnp.concatenate([hot, jnp.zeros((LANES - HOT, hd), F32)], axis=0).astype(BF16))
    sent = []
    for c in range(tokens // part):
        at = slice(c * part, (c + 1) * part)
        for h in range(heads):
            slot = cols[at, h : h + 1].astype(jnp.int32)
            place = (slot == iota((part, slots), 1)).astype(BF16)
            hot_place = (slot == iota((part, LANES), 1) + slots).astype(BF16)
            got = jnp.dot(place, rows[h], preferred_element_type=F32) + jnp.dot(
                hot_place, hots[h], preferred_element_type=F32
            )
            out_ref[at, h * hd : (h + 1) * hd] = got.astype(BF16)
        out = pltpu.make_async_copy(out_ref.at[at], out_hbm.at[at], sems.at[c])
        out.start()
        sent.append(out)
    for out in sent:
        out.wait()


VMEM = pl.BlockSpec(memory_space=pltpu.VMEM)
HBM = pl.BlockSpec(memory_space=pl.ANY)
AXES = ("z", "core", "x", "y")
MIB = 1024 * 1024


def call(kernel, name, limit, ins, outs, scratch, *arrays, flops=None):
    return pl.pallas_call(
        kernel,
        out_shape=tuple(
            pltpu.HBM(*out[1:]) if out[0] is HBM else jax.ShapeDtypeStruct(*out[1:]) for out in outs
        ),
        in_specs=ins,
        out_specs=tuple(out[0] for out in outs),
        scratch_shapes=scratch,
        compiler_params=pltpu.CompilerParams(vmem_limit_bytes=limit * MIB),
        name=name,
        cost_estimate=None if flops is None else pl.CostEstimate(flops=flops, bytes_accessed=0, transcendentals=0),
    )(*arrays)


def shift(block, axis, by):
    size = lax.axis_size(axis)
    return lax.ppermute(block, axis, [(i, (i + by) % size) for i in range(size)])


def local(query_rows, key_rows, value_rows, cluster_ids):
    devices = lax.axis_size(AXES)
    heads, tokens = cluster_ids.shape
    hd = query_rows.shape[1] // heads
    tile = (COLD, hd)
    payload = (devices, 3 * heads + 1, *tile)
    table, h0, h1, h2, h3, send = call(
        pack_kernel, "pack", 58, [HBM] * 4,
        [(HBM, (2 * heads, tokens), F32)] + [(HBM, (6, *tile), BF16)] * 4 + [(HBM, payload, BF16)],
        [
            pltpu.VMEM((heads, tokens), jnp.int32), pltpu.VMEM((2 * heads, tokens), F32),
            *[pltpu.VMEM((tokens, heads * hd), BF16)] * 3,
            pltpu.VMEM((heads, 6, *tile), BF16), pltpu.VMEM(payload, BF16),
            pltpu.SemaphoreType.DMA((3 * heads + 1,)), pltpu.SemaphoreType.DMA((9,)),
        ],
        cluster_ids, query_rows, key_rows, value_rows,
    )
    got = lax.all_to_all(send, AXES, split_axis=0, concat_axis=0, tiled=True)
    asked = [h0] + [shift(b, "y", d + 1) for d, b in enumerate((h1, h2, h3))]
    got, asked = lax.optimization_barrier((got, asked))
    (kv,) = call(
        mid_kernel, "mid", 24, [VMEM], [(HBM, (97, *tile), BF16)],
        [pltpu.VMEM((97, *tile), BF16), pltpu.SemaphoreType.DMA((3,))], got,
    )
    got, kv = lax.optimization_barrier((got, kv))
    near = [kv] + [shift(kv, "z", d) for d in (1, 2, 3)]
    (answer,) = call(
        cold_kernel, "cold", 24, [VMEM], [(HBM, (devices, heads, *tile), BF16)],
        [pltpu.VMEM((devices, heads, *tile), BF16), pltpu.SemaphoreType.DMA((heads,))],
        got, flops=20_000_000_000,
    )
    near, _ = lax.optimization_barrier((near, answer))
    near = jnp.concatenate(near, axis=0)
    far = shift(near, "core", 1)
    outs = call(
        hot_kernel, "hot", 24, [VMEM] * 6, [(VMEM, (3, *tile), BF16)] * 4,
        [
            pltpu.VMEM((4, 6, *tile), F32), pltpu.VMEM((devices * HOT, hd), BF16),
            pltpu.VMEM((devices * HOT, hd), BF16), pltpu.VMEM((4, 3, *tile), F32),
        ],
        *asked, near, far,
        flops=2_000_000_000,
    )
    hot_out = [outs[0]] + [shift(b, "y", 3 - d) for d, b in enumerate(outs[1:])]
    back = lax.all_to_all(answer, AXES, split_axis=0, concat_axis=0, tiled=True)
    (result,) = call(
        unpack_kernel, "unpack", 24, [VMEM] * 6, [(HBM, (tokens, heads * hd), BF16)],
        [
            pltpu.VMEM((4, 3, *tile), F32), pltpu.VMEM((tokens, heads * hd), BF16),
            pltpu.SemaphoreType.DMA((4,)),
        ],
        table, back, *hot_out,
    )
    return result


def solution(mesh):
    split = jax.sharding.Mesh(mesh.devices.reshape(4, 2, 4, 4), AXES)
    return jax.shard_map(
        local,
        mesh=split,
        in_specs=(P(AXES, None), P(AXES, None), P(AXES, None), P(None, AXES)),
        out_specs=P(AXES, None),
        check_vma=False,
    )
```

```python
import jax
import jax.numpy as jnp
from jax import lax
from jax.experimental import pallas as pl
from jax.experimental.pallas import tpu as pltpu
from jax.sharding import PartitionSpec as P

CL_DEV = 8
COLD = 8
HOT = 24
HOT_PAD = 32
LANES = 128
NEG_FILL = -1e30
SHARE = 3
HOT_LANE = 32
MARK_Q = 104.0
MARK_K = 100.0
LOG2E = 1.4426950408889634
F32 = jnp.float32
BF16 = jnp.bfloat16


def iota(shape, dim):
    return lax.broadcasted_iota(jnp.int32, shape, dim)


def columns_of(table):
    tokens = table.shape[1]
    return jnp.transpose(
        jnp.concatenate([table, jnp.zeros((LANES - table.shape[0], tokens), F32)], axis=0)
    )


def pack_kernel(
    ids_hbm, q_hbm, k_hbm, v_hbm,
    table_hbm, h0_hbm, h1_hbm, h2_hbm, h3_hbm, send_hbm,
    ids_ref, table_ref, q_ref, k_ref, v_ref, hot_ref, send_ref, sems, out_sems,
):
    heads, tokens = ids_ref.shape
    hd = q_hbm.shape[1] // heads
    devices = send_ref.shape[0]
    slots = devices * COLD
    step = 256
    ids_load = pltpu.make_async_copy(ids_hbm, ids_ref, sems.at[3 * heads])
    ids_load.start()
    loads = [
        pltpu.make_async_copy(src.at[r * 512 : (r + 1) * 512], dst.at[r * 512 : (r + 1) * 512], sems.at[2 * j + r])
        for j, (src, dst) in enumerate(((q_hbm, q_ref), (k_hbm, k_ref), (v_hbm, v_ref)))
        for r in range(2)
    ]
    for load in loads:
        load.start()
    ids_load.wait()
    ids = ids_ref[...]
    owner = ids // CL_DEV
    tags = (ids - owner * CL_DEV + 1).astype(F32)
    upper = (iota((step, step), 0) < iota((step, step), 1)).astype(BF16)
    dev_col = iota((devices, step), 0)
    slot_rows = []
    labels = jnp.zeros((devices, LANES), F32)
    for h in range(heads):
        carry = jnp.zeros((devices, 1), F32)
        ones, ranks = [], []
        for b in range(tokens // step):
            one = (owner[h : h + 1, b * step : (b + 1) * step] == dev_col).astype(F32)
            inside = jnp.dot(one.astype(BF16), upper, preferred_element_type=F32) + carry
            carry = carry + jnp.sum(one, axis=1, keepdims=True)
            ones.append(one)
            ranks.append(jnp.sum(one * inside, axis=0, keepdims=True))
        full = (carry > COLD).astype(F32)
        for b, one in enumerate(ones):
            ranks[b] = jnp.where(
                jnp.sum(one * full, axis=0, keepdims=True) > 0.5, ranks[b] + slots, ranks[b]
            )
            lane = jnp.where(
                ranks[b] < COLD, ranks[b] + COLD * h, ranks[b] + (HOT_LANE + HOT * h - slots)
            ).astype(jnp.int32)
            tag = jnp.where(
                lane == iota((LANES, step), 0), tags[h : h + 1, b * step : (b + 1) * step], 0.0
            )
            labels = labels + lax.dot_general(
                one.astype(BF16), tag.astype(BF16), NT, preferred_element_type=F32
            )
        rank = jnp.concatenate(ranks, axis=1).astype(jnp.int32)
        slot_rows.append(jnp.where(rank >= slots, rank, owner[h : h + 1] * COLD + rank))
    slot_all = jnp.concatenate(slot_rows, axis=0)
    table_ref[...] = jnp.concatenate([slot_all.astype(F32), tags], axis=0)
    sent = [pltpu.make_async_copy(table_ref, table_hbm, out_sems.at[4])]
    sent[0].start()
    asked_tags = jnp.sum(labels, axis=0, keepdims=True)
    cold_lane = iota((1, LANES), 1) < HOT_LANE
    for h in range(heads):
        own = iota((HOT, LANES), 1) == iota((HOT, LANES), 0) + (HOT_LANE + HOT * h)
        tag = jnp.sum(jnp.where(own, asked_tags, 0.0), axis=1, keepdims=True)
        hot_ref[h, 3:6] = jnp.broadcast_to(tag, (HOT, hd)).reshape(3, COLD, hd).astype(BF16)
    rows = HOT // SHARE * COLD
    row = iota((rows + HOT_PAD, 1), 0)
    row_share, row_at = row // COLD, row % COLD
    want = jnp.where(row_at < SHARE, SHARE * row_share + row_at, SHARE * (row_share - 1) + row_at)
    want = jnp.where(row_at < 2 * SHARE, want, -9)
    want = jnp.where(row < rows, want, row - rows) + slots
    tile_at = iota((rows, hd), 0) % COLD
    hot_tiles = []
    xs = []
    for load in loads:
        load.wait()
    for h in range(heads):
        xs.append(jnp.concatenate([ref[:, h * hd : (h + 1) * hd] for ref in (q_ref, k_ref, v_ref)], axis=1))
        moved = jnp.dot(
            (slot_all[h : h + 1] == want).astype(BF16), xs[h], preferred_element_type=F32
        )
        tiles = jnp.where(tile_at < SHARE, moved[:rows, hd : 2 * hd], moved[:rows, 2 * hd :])
        tiles = jnp.where(tile_at == COLD - 1, asked_tags, tiles)
        hot_tiles.append(tiles)
        hot_ref[h, 0:3] = moved[rows : rows + HOT, :hd].reshape(3, COLD, hd).astype(BF16)
    y = lax.axis_index("y")
    for d, ref in enumerate((h0_hbm, h1_hbm, h2_hbm, h3_hbm)):
        sent.append(pltpu.make_async_copy(hot_ref.at[lax.rem(y + d, heads)], ref, out_sems.at[5 + d]))
        sent[-1].start()
    labels = jnp.where(cold_lane, labels, 0.0)
    part = 256
    sub = iota((COLD, LANES), 0)
    for c in range(slots // part):
        first, stop = c * part // COLD, (c + 1) * part // COLD
        for h in range(heads):
            place = (slot_all[h : h + 1] == iota((part, tokens), 0) + c * part).astype(BF16)
            moved = jnp.dot(place, xs[h], preferred_element_type=F32)
            for j in range(3):
                send_ref[first:stop, 3 * h + j] = (
                    moved[:, j * hd : (j + 1) * hd].reshape(stop - first, COLD, hd).astype(BF16)
                )
        for dev in range(first, stop):
            share, head = dev // 16, dev % heads
            tile = hot_tiles[head][share * COLD : (share + 1) * COLD]
            tile = jnp.where(sub == 2 * SHARE, labels[dev : dev + 1], tile)
            send_ref[dev, 3 * heads] = tile.astype(BF16)
        out = pltpu.make_async_copy(
            send_ref.at[first:stop], send_hbm.at[first:stop], out_sems.at[c]
        )
        out.start()
        sent.append(out)
    for out in sent:
        out.wait()


def softmax_rows(scores, allowed, scale, values):
    masked = jnp.where(allowed, scores, NEG_FILL)
    top = jnp.max(masked, axis=1, keepdims=True)
    weights = jnp.exp2((masked - top) * scale)
    total = jnp.sum(weights, axis=1, keepdims=True)
    out = jnp.dot(weights.astype(BF16), values, preferred_element_type=F32)
    return out / total


NT = (((1,), (1,)), ((), ()))


def cold_kernel(got_ref, out_hbm, out_ref, out_sems):
    devices, tiles, _, hd = got_ref.shape
    heads = tiles // 3
    slots = devices * COLD
    scale = hd ** (-0.5) * LOG2E
    extra = got_ref[:, 3 * heads].astype(F32)
    spread = jnp.broadcast_to(
        extra[:, 2 * SHARE : 2 * SHARE + 1], (devices, COLD, LANES)
    ).reshape(slots, LANES)
    pick = iota((slots, LANES), 1) - iota((slots, LANES), 0) % COLD
    ones = jnp.ones((LANES, LANES), BF16)
    part = 512
    causal = iota((part, part), 1) <= iota((part, part), 0)
    sent = []
    for h in range(heads):
        tags = jnp.where(pick == COLD * h, spread, 0.0).astype(BF16)
        label_cols = jnp.dot(tags, ones, preferred_element_type=F32)
        q, k, v = (
            got_ref[:, 3 * h + j].astype(F32).reshape(slots, hd).astype(BF16) for j in range(3)
        )
        marked = label_cols == (iota((slots, LANES), 1) + 1).astype(F32)
        q = jnp.concatenate([q, jnp.where(marked, MARK_Q, 0.0).astype(BF16)], axis=1)
        k = jnp.concatenate([k, jnp.where(marked, MARK_K, 0.0).astype(BF16)], axis=1)
        for c in range(slots // part):
            stop = (c + 1) * part
            scores = lax.dot_general(
                q[c * part : stop], k[:stop], NT, preferred_element_type=F32
            )
            last = jnp.where(causal, scores[:, c * part :], NEG_FILL)
            if c > 0:
                last = jnp.concatenate([scores[:, : c * part], last], axis=1)
            top = jnp.max(last, axis=1, keepdims=True)
            weights = jnp.exp2((last - top) * scale)
            total = jnp.sum(weights, axis=1, keepdims=True)
            out = jnp.dot(weights.astype(BF16), v[:stop], preferred_element_type=F32) / total
            devs = slice(c * part // COLD, stop // COLD)
            out_ref[devs, h] = out.reshape(part // COLD, COLD, hd).astype(BF16)
            copy = pltpu.make_async_copy(
                out_ref.at[devs, h], out_hbm.at[devs, h], out_sems.at[h * (slots // part) + c]
            )
            copy.start()
            sent.append(copy)
    for out in sent:
        out.wait()


def mid_kernel(got_ref, kv_hbm, kv_ref, sems):
    devices, tiles, _, hd = got_ref.shape
    slots = devices * COLD
    keys = devices * SHARE
    extra = got_ref[:, tiles - 1].astype(F32).reshape(slots, hd).astype(BF16)
    runs = slots // LANES
    each = keys // runs
    row = iota((3 * each, 1), 0)
    kind, n = row // each, row % each
    at = n % SHARE
    col = n // SHARE * COLD + jnp.where(kind == 0, at, jnp.where(kind == 1, at + SHARE, COLD - 1))
    place = (col == iota((3 * each, LANES), 1)).astype(BF16)
    y, core, z = (lax.axis_index(a) for a in ("y", "core", "z"))
    lane = HOT_LANE + HOT * y + SHARE * (z * 2 + core) + iota((each, 1), 0) % SHARE
    own = iota((each, hd), 1) == lane
    tiles_each = each // COLD
    tags = []
    for b in range(runs):
        moved = jnp.dot(place, extra[b * LANES : (b + 1) * LANES], preferred_element_type=F32)
        first = b * tiles_each
        kv_ref[first : first + tiles_each] = moved[:each].reshape(tiles_each, COLD, hd).astype(BF16)
        kv_ref[48 + first : 48 + first + tiles_each] = (
            moved[each : 2 * each].reshape(tiles_each, COLD, hd).astype(BF16)
        )
        tags.append(jnp.where(own, moved[2 * each :], 0.0))
    sent = [pltpu.make_async_copy(kv_ref.at[0:96], kv_hbm.at[0:96], sems.at[0])]
    sent[0].start()
    tags = jnp.concatenate(tags, axis=0).astype(BF16)
    flat = lax.dot_general(jnp.ones((COLD, hd), BF16), tags, NT, preferred_element_type=F32)
    label = [flat[0:1, j * LANES : (j + 1) * LANES] for j in range(keys // LANES)]
    label.append(jnp.zeros((COLD - len(label), LANES), F32))
    kv_ref[96] = jnp.concatenate(label, axis=0).astype(BF16)
    sent.append(pltpu.make_async_copy(kv_ref.at[96:97], kv_hbm.at[96:97], sems.at[1]))
    sent[1].start()
    for out in sent:
        out.wait()


def hot_kernel(
    b0_ref, b1_ref, b2_ref, b3_ref, near_ref, far_ref,
    o0_ref, o1_ref, o2_ref, o3_ref, all_ref, k_ref, v_ref, o_ref,
):
    hd = b0_ref.shape[-1]
    rows = 4 * HOT
    keys = k_ref.shape[0] // 8
    scale = hd ** (-0.5) * LOG2E
    y, x, core, z = (lax.axis_index(a) for a in ("y", "x", "core", "z"))
    for d, ref in enumerate((b0_ref, b1_ref, b2_ref, b3_ref)):
        all_ref[lax.rem(y + 4 - d, 4)] = ref[...].astype(F32)
    q = all_ref[:, 0:3].reshape(rows, hd).astype(BF16)
    label_col = all_ref[:, 3:6].reshape(rows, hd)[:, 0:1]
    row = iota((rows, 1), 0)
    asked_at = (((z * 2 + core) * 16 + x * 4) * HOT + row).astype(F32)
    n = iota((1, keys), 1)
    key_at = (n // SHARE) * HOT + n % SHARE
    allowed = []
    for dc, ref in enumerate((near_ref, far_ref)):
        for dz in range(4):
            tile = 97 * dz
            at = slice((dc * 4 + dz) * keys, (dc * 4 + dz + 1) * keys)
            k_ref[at] = ref[tile : tile + 48].astype(F32).reshape(keys, hd).astype(BF16)
            v_ref[at] = ref[tile + 48 : tile + 96].astype(F32).reshape(keys, hd).astype(BF16)
            tags = ref[tile + 96].astype(F32)
            label = jnp.concatenate([tags[j : j + 1] for j in range(keys // LANES)], axis=1)
            share = lax.rem(z + 4 - dz, 4) * 2 + lax.rem(core + dc, 2)
            there = (key_at + SHARE * share).astype(F32)
            allowed.append((label_col == label) & (there <= asked_at))
    scores = lax.dot_general(q, k_ref[...], NT, preferred_element_type=F32)
    out = softmax_rows(scores, jnp.concatenate(allowed, axis=1), scale, v_ref[...])
    o_ref[...] = out.reshape(4, 3, COLD, hd)
    for d, ref in enumerate((o0_ref, o1_ref, o2_ref, o3_ref)):
        ref[...] = o_ref[lax.rem(y + 4 - d, 4)].astype(BF16)


def unpack_kernel(table_ref, back_ref, o0_ref, o1_ref, o2_ref, o3_ref, out_hbm, hot_ref, out_ref, sems):
    devices, heads, _, hd = back_ref.shape
    tokens = table_ref.shape[1]
    cols = columns_of(table_ref[...])
    slots = devices * COLD
    part = 256
    for d, ref in enumerate((o0_ref, o1_ref, o2_ref, o3_ref)):
        hot_ref[d] = ref[...].astype(F32)
    y = lax.axis_index("y")
    rows, hots = [], []
    for h in range(heads):
        rows.append(back_ref[:, h].astype(F32).reshape(slots, hd).astype(BF16))
        hot = hot_ref[lax.rem(h + 4 - y, 4)].reshape(HOT, hd)
        hots.append(jnp.concatenate([hot, jnp.zeros((LANES - HOT, hd), F32)], axis=0).astype(BF16))
    sent = []
    for c in range(tokens // part):
        at = slice(c * part, (c + 1) * part)
        for h in range(heads):
            slot = cols[at, h : h + 1].astype(jnp.int32)
            place = (slot == iota((part, slots), 1)).astype(BF16)
            hot_place = (slot == iota((part, LANES), 1) + slots).astype(BF16)
            got = jnp.dot(place, rows[h], preferred_element_type=F32) + jnp.dot(
                hot_place, hots[h], preferred_element_type=F32
            )
            out_ref[at, h * hd : (h + 1) * hd] = got.astype(BF16)
        out = pltpu.make_async_copy(out_ref.at[at], out_hbm.at[at], sems.at[c])
        out.start()
        sent.append(out)
    for out in sent:
        out.wait()


VMEM = pl.BlockSpec(memory_space=pltpu.VMEM)
HBM = pl.BlockSpec(memory_space=pl.ANY)
AXES = ("z", "core", "x", "y")
MIB = 1024 * 1024


def call(kernel, name, limit, ins, outs, scratch, *arrays, flops=None):
    return pl.pallas_call(
        kernel,
        out_shape=tuple(
            pltpu.HBM(*out[1:]) if out[0] is HBM else jax.ShapeDtypeStruct(*out[1:]) for out in outs
        ),
        in_specs=ins,
        out_specs=tuple(out[0] for out in outs),
        scratch_shapes=scratch,
        compiler_params=pltpu.CompilerParams(vmem_limit_bytes=limit * MIB),
        name=name,
        cost_estimate=None if flops is None else pl.CostEstimate(flops=flops, bytes_accessed=0, transcendentals=0),
    )(*arrays)


def shift(block, axis, by):
    size = lax.axis_size(axis)
    return lax.ppermute(block, axis, [(i, (i + by) % size) for i in range(size)])


def local(query_rows, key_rows, value_rows, cluster_ids):
    devices = lax.axis_size(AXES)
    heads, tokens = cluster_ids.shape
    hd = query_rows.shape[1] // heads
    tile = (COLD, hd)
    payload = (devices, 3 * heads + 1, *tile)
    table, h0, h1, h2, h3, send = call(
        pack_kernel, "pack", 58, [HBM] * 4,
        [(HBM, (2 * heads, tokens), F32)] + [(HBM, (6, *tile), BF16)] * 4 + [(HBM, payload, BF16)],
        [
            pltpu.VMEM((heads, tokens), jnp.int32), pltpu.VMEM((2 * heads, tokens), F32),
            *[pltpu.VMEM((tokens, heads * hd), BF16)] * 3,
            pltpu.VMEM((heads, 6, *tile), BF16), pltpu.VMEM(payload, BF16),
            pltpu.SemaphoreType.DMA((3 * heads + 1,)), pltpu.SemaphoreType.DMA((9,)),
        ],
        cluster_ids, query_rows, key_rows, value_rows,
    )
    got = lax.all_to_all(send, AXES, split_axis=0, concat_axis=0, tiled=True)
    asked = [h0] + [shift(b, "y", d + 1) for d, b in enumerate((h1, h2, h3))]
    got, asked = lax.optimization_barrier((got, asked))
    (kv,) = call(
        mid_kernel, "mid", 24, [VMEM], [(HBM, (97, *tile), BF16)],
        [pltpu.VMEM((97, *tile), BF16), pltpu.SemaphoreType.DMA((2,))], got,
    )
    got, kv = lax.optimization_barrier((got, kv))
    near = [kv] + [shift(kv, "z", d) for d in (1, 2, 3)]
    (answer,) = call(
        cold_kernel, "cold", 24, [VMEM], [(HBM, (devices, heads, *tile), BF16)],
        [pltpu.VMEM((devices, heads, *tile), BF16), pltpu.SemaphoreType.DMA((2 * heads,))],
        got, flops=20_000_000_000,
    )
    near, _ = lax.optimization_barrier((near, answer))
    near = jnp.concatenate(near, axis=0)
    far = shift(near, "core", 1)
    outs = call(
        hot_kernel, "hot", 24, [VMEM] * 6, [(VMEM, (3, *tile), BF16)] * 4,
        [
            pltpu.VMEM((4, 6, *tile), F32), pltpu.VMEM((devices * HOT, hd), BF16),
            pltpu.VMEM((devices * HOT, hd), BF16), pltpu.VMEM((4, 3, *tile), F32),
        ],
        *asked, near, far,
        flops=2_000_000_000,
    )
    hot_out = [outs[0]] + [shift(b, "y", 3 - d) for d, b in enumerate(outs[1:])]
    back = lax.all_to_all(answer, AXES, split_axis=0, concat_axis=0, tiled=True)
    (result,) = call(
        unpack_kernel, "unpack", 24, [VMEM] * 6, [(HBM, (tokens, heads * hd), BF16)],
        [
            pltpu.VMEM((4, 3, *tile), F32), pltpu.VMEM((tokens, heads * hd), BF16),
            pltpu.SemaphoreType.DMA((4,)),
        ],
        table, back, *hot_out,
    )
    return result


def solution(mesh):
    split = jax.sharding.Mesh(mesh.devices.reshape(4, 2, 4, 4), AXES)
    return jax.shard_map(
        local,
        mesh=split,
        in_specs=(P(AXES, None), P(AXES, None), P(AXES, None), P(None, AXES)),
        out_specs=P(AXES, None),
        check_vma=False,
    )
```

```python
import jax
import jax.numpy as jnp
from jax import lax
from jax.experimental import pallas as pl
from jax.experimental.pallas import tpu as pltpu
from jax.sharding import PartitionSpec as P

CL_DEV = 8
COLD = 8
HOT = 24
HOT_PAD = 32
LANES = 128
NEG_FILL = -1e30
SHARE = 3
HOT_LANE = 32
MARK_Q = 104.0
MARK_K = 100.0
LOG2E = 1.4426950408889634
F32 = jnp.float32
BF16 = jnp.bfloat16


def iota(shape, dim):
    return lax.broadcasted_iota(jnp.int32, shape, dim)


def columns_of(table):
    tokens = table.shape[1]
    return jnp.transpose(
        jnp.concatenate([table, jnp.zeros((LANES - table.shape[0], tokens), F32)], axis=0)
    )


def pack_kernel(
    ids_hbm, q_hbm, k_hbm, v_hbm,
    table_hbm, h0_hbm, h1_hbm, h2_hbm, h3_hbm, send_hbm,
    ids_ref, table_ref, q_ref, k_ref, v_ref, hot_ref, send_ref, sems, out_sems,
):
    heads, tokens = ids_ref.shape
    hd = q_hbm.shape[1] // heads
    devices = send_ref.shape[0]
    slots = devices * COLD
    step = 256
    ids_load = pltpu.make_async_copy(ids_hbm, ids_ref, sems.at[3 * heads])
    ids_load.start()
    loads = [
        pltpu.make_async_copy(src.at[r * 512 : (r + 1) * 512], dst.at[r * 512 : (r + 1) * 512], sems.at[2 * j + r])
        for j, (src, dst) in enumerate(((q_hbm, q_ref), (k_hbm, k_ref), (v_hbm, v_ref)))
        for r in range(2)
    ]
    for load in loads:
        load.start()
    ids_load.wait()
    ids = ids_ref[...]
    owner = ids // CL_DEV
    tags = (ids - owner * CL_DEV + 1).astype(F32)
    upper = (iota((step, step), 0) < iota((step, step), 1)).astype(BF16)
    dev_col = iota((devices, step), 0)
    slot_rows = []
    labels = jnp.zeros((devices, LANES), F32)
    for h in range(heads):
        carry = jnp.zeros((devices, 1), F32)
        ones, ranks = [], []
        for b in range(tokens // step):
            one = (owner[h : h + 1, b * step : (b + 1) * step] == dev_col).astype(F32)
            inside = jnp.dot(one.astype(BF16), upper, preferred_element_type=F32) + carry
            carry = carry + jnp.sum(one, axis=1, keepdims=True)
            ones.append(one)
            ranks.append(jnp.sum(one * inside, axis=0, keepdims=True))
        full = (carry > COLD).astype(F32)
        for b, one in enumerate(ones):
            ranks[b] = jnp.where(
                jnp.sum(one * full, axis=0, keepdims=True) > 0.5, ranks[b] + slots, ranks[b]
            )
            lane = jnp.where(
                ranks[b] < COLD, ranks[b] + COLD * h, ranks[b] + (HOT_LANE + HOT * h - slots)
            ).astype(jnp.int32)
            tag = jnp.where(
                lane == iota((LANES, step), 0), tags[h : h + 1, b * step : (b + 1) * step], 0.0
            )
            labels = labels + lax.dot_general(
                one.astype(BF16), tag.astype(BF16), NT, preferred_element_type=F32
            )
        rank = jnp.concatenate(ranks, axis=1).astype(jnp.int32)
        slot_rows.append(jnp.where(rank >= slots, rank, owner[h : h + 1] * COLD + rank))
    slot_all = jnp.concatenate(slot_rows, axis=0)
    table_ref[...] = jnp.concatenate([slot_all.astype(F32), tags], axis=0)
    sent = [pltpu.make_async_copy(table_ref, table_hbm, out_sems.at[4])]
    sent[0].start()
    asked_tags = jnp.sum(labels, axis=0, keepdims=True)
    cold_lane = iota((1, LANES), 1) < HOT_LANE
    for h in range(heads):
        own = iota((HOT, LANES), 1) == iota((HOT, LANES), 0) + (HOT_LANE + HOT * h)
        tag = jnp.sum(jnp.where(own, asked_tags, 0.0), axis=1, keepdims=True)
        hot_ref[h, 3:6] = jnp.broadcast_to(tag, (HOT, hd)).reshape(3, COLD, hd).astype(BF16)
    rows = HOT // SHARE * COLD
    row = iota((rows + HOT_PAD, 1), 0)
    row_share, row_at = row // COLD, row % COLD
    want = jnp.where(row_at < SHARE, SHARE * row_share + row_at, SHARE * (row_share - 1) + row_at)
    want = jnp.where(row_at < 2 * SHARE, want, -9)
    want = jnp.where(row < rows, want, row - rows) + slots
    tile_at = iota((rows, hd), 0) % COLD
    hot_tiles = []
    xs = []
    for load in loads:
        load.wait()
    for h in range(heads):
        xs.append(jnp.concatenate([ref[:, h * hd : (h + 1) * hd] for ref in (q_ref, k_ref, v_ref)], axis=1))
        moved = jnp.dot(
            (slot_all[h : h + 1] == want).astype(BF16), xs[h], preferred_element_type=F32
        )
        tiles = jnp.where(tile_at < SHARE, moved[:rows, hd : 2 * hd], moved[:rows, 2 * hd :])
        tiles = jnp.where(tile_at == COLD - 1, asked_tags, tiles)
        hot_tiles.append(tiles)
        hot_ref[h, 0:3] = moved[rows : rows + HOT, :hd].reshape(3, COLD, hd).astype(BF16)
    y = lax.axis_index("y")
    for d, ref in enumerate((h0_hbm, h1_hbm, h2_hbm, h3_hbm)):
        sent.append(pltpu.make_async_copy(hot_ref.at[lax.rem(y + d, heads)], ref, out_sems.at[5 + d]))
        sent[-1].start()
    labels = jnp.where(cold_lane, labels, 0.0)
    part = 256
    sub = iota((COLD, LANES), 0)
    for c in range(slots // part):
        first, stop = c * part // COLD, (c + 1) * part // COLD
        for h in range(heads):
            place = (slot_all[h : h + 1] == iota((part, tokens), 0) + c * part).astype(BF16)
            moved = jnp.dot(place, xs[h], preferred_element_type=F32)
            for j in range(3):
                send_ref[first:stop, 3 * h + j] = (
                    moved[:, j * hd : (j + 1) * hd].reshape(stop - first, COLD, hd).astype(BF16)
                )
        for dev in range(first, stop):
            share, head = dev // 16, dev % heads
            tile = hot_tiles[head][share * COLD : (share + 1) * COLD]
            tile = jnp.where(sub == 2 * SHARE, labels[dev : dev + 1], tile)
            send_ref[dev, 3 * heads] = tile.astype(BF16)
        out = pltpu.make_async_copy(
            send_ref.at[first:stop], send_hbm.at[first:stop], out_sems.at[c]
        )
        out.start()
        sent.append(out)
    for out in sent:
        out.wait()


def softmax_rows(scores, allowed, scale, values):
    masked = jnp.where(allowed, scores, NEG_FILL)
    top = jnp.max(masked, axis=1, keepdims=True)
    weights = jnp.exp2((masked - top) * scale)
    total = jnp.sum(weights, axis=1, keepdims=True)
    out = jnp.dot(weights.astype(BF16), values, preferred_element_type=F32)
    return out / total


NT = (((1,), (1,)), ((), ()))


def cold_kernel(got_ref, out_hbm, out_ref, out_sems):
    devices, tiles, _, hd = got_ref.shape
    heads = tiles // 3
    slots = devices * COLD
    scale = hd ** (-0.5) * LOG2E
    extra = got_ref[:, 3 * heads].astype(F32)
    spread = jnp.broadcast_to(
        extra[:, 2 * SHARE : 2 * SHARE + 1], (devices, COLD, LANES)
    ).reshape(slots, LANES)
    pick = iota((slots, LANES), 1) - iota((slots, LANES), 0) % COLD
    ones = jnp.ones((LANES, LANES), BF16)
    part = 512
    causal = iota((part, part), 1) <= iota((part, part), 0)
    sent = []
    for h in range(heads):
        tags = jnp.where(pick == COLD * h, spread, 0.0).astype(BF16)
        label_cols = jnp.dot(tags, ones, preferred_element_type=F32)
        q, k, v = (
            got_ref[:, 3 * h + j].astype(F32).reshape(slots, hd).astype(BF16) for j in range(3)
        )
        marked = label_cols == (iota((slots, LANES), 1) + 1).astype(F32)
        q = jnp.concatenate([q, jnp.where(marked, MARK_Q, 0.0).astype(BF16)], axis=1)
        k = jnp.concatenate([k, jnp.where(marked, MARK_K, 0.0).astype(BF16)], axis=1)
        for c in range(slots // part):
            stop = (c + 1) * part
            scores = lax.dot_general(
                q[c * part : stop], k[:stop], NT, preferred_element_type=F32
            )
            last = jnp.where(causal, scores[:, c * part :], NEG_FILL)
            if c > 0:
                last = jnp.concatenate([scores[:, : c * part], last], axis=1)
            top = jnp.max(last, axis=1, keepdims=True)
            weights = jnp.exp2((last - top) * scale)
            total = jnp.sum(weights, axis=1, keepdims=True)
            out = jnp.dot(weights.astype(BF16), v[:stop], preferred_element_type=F32) / total
            devs = slice(c * part // COLD, stop // COLD)
            out_ref[devs, h] = out.reshape(part // COLD, COLD, hd).astype(BF16)
            copy = pltpu.make_async_copy(
                out_ref.at[devs, h], out_hbm.at[devs, h], out_sems.at[h * (slots // part) + c]
            )
            copy.start()
            sent.append(copy)
    for out in sent:
        out.wait()


def mid_kernel(got_ref, kv_hbm, kv_ref, sems):
    devices, tiles, _, hd = got_ref.shape
    slots = devices * COLD
    keys = devices * SHARE
    extra = got_ref[:, tiles - 1].astype(F32).reshape(slots, hd).astype(BF16)
    runs = slots // LANES
    each = keys // runs
    row = iota((3 * each, 1), 0)
    kind, n = row // each, row % each
    at = n % SHARE
    col = n // SHARE * COLD + jnp.where(kind == 0, at, jnp.where(kind == 1, at + SHARE, COLD - 1))
    place = (col == iota((3 * each, LANES), 1)).astype(BF16)
    y, core, z = (lax.axis_index(a) for a in ("y", "core", "z"))
    lane = HOT_LANE + HOT * y + SHARE * (z * 2 + core) + iota((each, 1), 0) % SHARE
    own = iota((each, hd), 1) == lane
    tiles_each = each // COLD
    tags = []
    for b in range(runs):
        moved = jnp.dot(place, extra[b * LANES : (b + 1) * LANES], preferred_element_type=F32)
        first = b * tiles_each
        kv_ref[first : first + tiles_each] = moved[:each].reshape(tiles_each, COLD, hd).astype(BF16)
        kv_ref[48 + first : 48 + first + tiles_each] = (
            moved[each : 2 * each].reshape(tiles_each, COLD, hd).astype(BF16)
        )
        tags.append(jnp.where(own, moved[2 * each :], 0.0))
    sent = [pltpu.make_async_copy(kv_ref.at[0:96], kv_hbm.at[0:96], sems.at[0])]
    sent[0].start()
    tags = jnp.concatenate(tags, axis=0).astype(BF16)
    flat = lax.dot_general(jnp.ones((COLD, hd), BF16), tags, NT, preferred_element_type=F32)
    label = [flat[0:1, j * LANES : (j + 1) * LANES] for j in range(keys // LANES)]
    label.append(jnp.zeros((COLD - len(label), LANES), F32))
    kv_ref[96] = jnp.concatenate(label, axis=0).astype(BF16)
    sent.append(pltpu.make_async_copy(kv_ref.at[96:97], kv_hbm.at[96:97], sems.at[1]))
    sent[1].start()
    for out in sent:
        out.wait()


def hot_kernel(
    b0_ref, b1_ref, b2_ref, b3_ref, near_ref, far_ref,
    o0_ref, o1_ref, o2_ref, o3_ref, all_ref, k_ref, v_ref, o_ref,
):
    hd = b0_ref.shape[-1]
    rows = 4 * HOT
    keys = k_ref.shape[0] // 8
    scale = hd ** (-0.5) * LOG2E
    y, x, core, z = (lax.axis_index(a) for a in ("y", "x", "core", "z"))
    for d, ref in enumerate((b0_ref, b1_ref, b2_ref, b3_ref)):
        all_ref[lax.rem(y + 4 - d, 4)] = ref[...].astype(F32)
    q = all_ref[:, 0:3].reshape(rows, hd).astype(BF16)
    label_col = all_ref[:, 3:6].reshape(rows, hd)[:, 0:1]
    row = iota((rows, 1), 0)
    asked_at = (((z * 2 + core) * 16 + x * 4) * HOT + row).astype(F32)
    n = iota((1, keys), 1)
    key_at = (n // SHARE) * HOT + n % SHARE
    allowed = []
    for dc, ref in enumerate((near_ref, far_ref)):
        for dz in range(4):
            tile = 97 * dz
            at = slice((dc * 4 + dz) * keys, (dc * 4 + dz + 1) * keys)
            k_ref[at] = ref[tile : tile + 48].astype(F32).reshape(keys, hd).astype(BF16)
            v_ref[at] = ref[tile + 48 : tile + 96].astype(F32).reshape(keys, hd).astype(BF16)
            tags = ref[tile + 96].astype(F32)
            label = jnp.concatenate([tags[j : j + 1] for j in range(keys // LANES)], axis=1)
            share = lax.rem(z + 4 - dz, 4) * 2 + lax.rem(core + dc, 2)
            there = (key_at + SHARE * share).astype(F32)
            allowed.append((label_col == label) & (there <= asked_at))
    scores = lax.dot_general(q, k_ref[...], NT, preferred_element_type=F32)
    out = softmax_rows(scores, jnp.concatenate(allowed, axis=1), scale, v_ref[...])
    o_ref[...] = out.reshape(4, 3, COLD, hd)
    for d, ref in enumerate((o0_ref, o1_ref, o2_ref, o3_ref)):
        ref[...] = o_ref[lax.rem(y + 4 - d, 4)].astype(BF16)


def unpack_kernel(table_ref, back_ref, o0_ref, o1_ref, o2_ref, o3_ref, out_hbm, hot_ref, out_ref, sems):
    devices, heads, _, hd = back_ref.shape
    tokens = table_ref.shape[1]
    cols = columns_of(table_ref[...])
    slots = devices * COLD
    part = 256
    for d, ref in enumerate((o0_ref, o1_ref, o2_ref, o3_ref)):
        hot_ref[d] = ref[...].astype(F32)
    y = lax.axis_index("y")
    rows = []
    for h in range(heads):
        rows.append(back_ref[:, h].astype(F32).reshape(slots, hd).astype(BF16))
        hot = hot_ref[lax.rem(h + 4 - y, 4)].reshape(HOT, hd)
        spare = jnp.zeros((LANES - HOT, hd), F32)
        rows[h] = jnp.concatenate([rows[h], jnp.concatenate([hot, spare], axis=0).astype(BF16)], axis=0)
    sent = []
    for c in range(tokens // part):
        at = slice(c * part, (c + 1) * part)
        for h in range(heads):
            slot = cols[at, h : h + 1].astype(jnp.int32)
            place = (slot == iota((part, slots + LANES), 1)).astype(BF16)
            got = jnp.dot(place, rows[h], preferred_element_type=F32)
            out_ref[at, h * hd : (h + 1) * hd] = got.astype(BF16)
        out = pltpu.make_async_copy(out_ref.at[at], out_hbm.at[at], sems.at[c])
        out.start()
        sent.append(out)
    for out in sent:
        out.wait()


VMEM = pl.BlockSpec(memory_space=pltpu.VMEM)
HBM = pl.BlockSpec(memory_space=pl.ANY)
AXES = ("z", "core", "x", "y")
MIB = 1024 * 1024


def call(kernel, name, limit, ins, outs, scratch, *arrays, flops=None):
    return pl.pallas_call(
        kernel,
        out_shape=tuple(
            pltpu.HBM(*out[1:]) if out[0] is HBM else jax.ShapeDtypeStruct(*out[1:]) for out in outs
        ),
        in_specs=ins,
        out_specs=tuple(out[0] for out in outs),
        scratch_shapes=scratch,
        compiler_params=pltpu.CompilerParams(vmem_limit_bytes=limit * MIB),
        name=name,
        cost_estimate=None if flops is None else pl.CostEstimate(flops=flops, bytes_accessed=0, transcendentals=0),
    )(*arrays)


def shift(block, axis, by):
    size = lax.axis_size(axis)
    return lax.ppermute(block, axis, [(i, (i + by) % size) for i in range(size)])


def local(query_rows, key_rows, value_rows, cluster_ids):
    devices = lax.axis_size(AXES)
    heads, tokens = cluster_ids.shape
    hd = query_rows.shape[1] // heads
    tile = (COLD, hd)
    payload = (devices, 3 * heads + 1, *tile)
    table, h0, h1, h2, h3, send = call(
        pack_kernel, "pack", 58, [HBM] * 4,
        [(HBM, (2 * heads, tokens), F32)] + [(HBM, (6, *tile), BF16)] * 4 + [(HBM, payload, BF16)],
        [
            pltpu.VMEM((heads, tokens), jnp.int32), pltpu.VMEM((2 * heads, tokens), F32),
            *[pltpu.VMEM((tokens, heads * hd), BF16)] * 3,
            pltpu.VMEM((heads, 6, *tile), BF16), pltpu.VMEM(payload, BF16),
            pltpu.SemaphoreType.DMA((3 * heads + 1,)), pltpu.SemaphoreType.DMA((9,)),
        ],
        cluster_ids, query_rows, key_rows, value_rows,
    )
    got = lax.all_to_all(send, AXES, split_axis=0, concat_axis=0, tiled=True)
    asked = [h0] + [shift(b, "y", d + 1) for d, b in enumerate((h1, h2, h3))]
    got, asked = lax.optimization_barrier((got, asked))
    (kv,) = call(
        mid_kernel, "mid", 24, [VMEM], [(HBM, (97, *tile), BF16)],
        [pltpu.VMEM((97, *tile), BF16), pltpu.SemaphoreType.DMA((2,))], got,
    )
    got, kv = lax.optimization_barrier((got, kv))
    near = [kv] + [shift(kv, "z", d) for d in (1, 2, 3)]
    (answer,) = call(
        cold_kernel, "cold", 24, [VMEM], [(HBM, (devices, heads, *tile), BF16)],
        [pltpu.VMEM((devices, heads, *tile), BF16), pltpu.SemaphoreType.DMA((2 * heads,))],
        got, flops=20_000_000_000,
    )
    near, _ = lax.optimization_barrier((near, answer))
    near = jnp.concatenate(near, axis=0)
    far = shift(near, "core", 1)
    outs = call(
        hot_kernel, "hot", 24, [VMEM] * 6, [(VMEM, (3, *tile), BF16)] * 4,
        [
            pltpu.VMEM((4, 6, *tile), F32), pltpu.VMEM((devices * HOT, hd), BF16),
            pltpu.VMEM((devices * HOT, hd), BF16), pltpu.VMEM((4, 3, *tile), F32),
        ],
        *asked, near, far,
        flops=2_000_000_000,
    )
    hot_out = [outs[0]] + [shift(b, "y", 3 - d) for d, b in enumerate(outs[1:])]
    back = lax.all_to_all(answer, AXES, split_axis=0, concat_axis=0, tiled=True)
    (result,) = call(
        unpack_kernel, "unpack", 24, [VMEM] * 6, [(HBM, (tokens, heads * hd), BF16)],
        [
            pltpu.VMEM((4, 3, *tile), F32), pltpu.VMEM((tokens, heads * hd), BF16),
            pltpu.SemaphoreType.DMA((4,)),
        ],
        table, back, *hot_out,
    )
    return result


def solution(mesh):
    split = jax.sharding.Mesh(mesh.devices.reshape(4, 2, 4, 4), AXES)
    return jax.shard_map(
        local,
        mesh=split,
        in_specs=(P(AXES, None), P(AXES, None), P(AXES, None), P(None, AXES)),
        out_specs=P(AXES, None),
        check_vma=False,
    )
```

```python
import jax
import jax.numpy as jnp
from jax import lax
from jax.experimental import pallas as pl
from jax.experimental.pallas import tpu as pltpu
from jax.sharding import PartitionSpec as P

CL_DEV = 8
COLD = 8
HOT = 24
HOT_PAD = 32
LANES = 128
NEG_FILL = -1e30
SHARE = 3
HOT_LANE = 32
MARK_Q = 104.0
MARK_K = 100.0
LOG2E = 1.4426950408889634
F32 = jnp.float32
BF16 = jnp.bfloat16


def iota(shape, dim):
    return lax.broadcasted_iota(jnp.int32, shape, dim)


def columns_of(table):
    tokens = table.shape[1]
    return jnp.transpose(
        jnp.concatenate([table, jnp.zeros((LANES - table.shape[0], tokens), F32)], axis=0)
    )


def pack_kernel(
    ids_hbm, q_hbm, k_hbm, v_hbm,
    table_hbm, h0_hbm, h1_hbm, h2_hbm, h3_hbm, send_hbm,
    ids_ref, table_ref, q_ref, k_ref, v_ref, hot_ref, send_ref, sems, out_sems,
):
    heads, tokens = ids_ref.shape
    hd = q_hbm.shape[1] // heads
    devices = send_ref.shape[0]
    slots = devices * COLD
    step = 256
    ids_load = pltpu.make_async_copy(ids_hbm, ids_ref, sems.at[3 * heads])
    ids_load.start()
    loads = [
        pltpu.make_async_copy(src.at[r * 512 : (r + 1) * 512], dst.at[r * 512 : (r + 1) * 512], sems.at[2 * j + r])
        for j, (src, dst) in enumerate(((q_hbm, q_ref), (k_hbm, k_ref), (v_hbm, v_ref)))
        for r in range(2)
    ]
    for load in loads:
        load.start()
    ids_load.wait()
    ids = ids_ref[...]
    owner = ids // CL_DEV
    tags = (ids - owner * CL_DEV + 1).astype(F32)
    upper = (iota((step, step), 0) < iota((step, step), 1)).astype(BF16)
    dev_col = iota((devices, step), 0)
    slot_rows = []
    labels = jnp.zeros((devices, LANES), F32)
    for h in range(heads):
        carry = jnp.zeros((devices, 1), F32)
        ones, ranks = [], []
        for b in range(tokens // step):
            one = (owner[h : h + 1, b * step : (b + 1) * step] == dev_col).astype(F32)
            inside = jnp.dot(one.astype(BF16), upper, preferred_element_type=F32) + carry
            carry = carry + jnp.sum(one, axis=1, keepdims=True)
            ones.append(one)
            ranks.append(jnp.sum(one * inside, axis=0, keepdims=True))
        full = (carry > COLD).astype(F32)
        for b, one in enumerate(ones):
            ranks[b] = jnp.where(
                jnp.sum(one * full, axis=0, keepdims=True) > 0.5, ranks[b] + slots, ranks[b]
            )
            lane = jnp.where(
                ranks[b] < COLD, ranks[b] + COLD * h, ranks[b] + (HOT_LANE + HOT * h - slots)
            ).astype(jnp.int32)
            tag = jnp.where(
                lane == iota((LANES, step), 0), tags[h : h + 1, b * step : (b + 1) * step], 0.0
            )
            labels = labels + lax.dot_general(
                one.astype(BF16), tag.astype(BF16), NT, preferred_element_type=F32
            )
        rank = jnp.concatenate(ranks, axis=1).astype(jnp.int32)
        slot_rows.append(jnp.where(rank >= slots, rank, owner[h : h + 1] * COLD + rank))
    slot_all = jnp.concatenate(slot_rows, axis=0)
    table_ref[...] = jnp.concatenate([slot_all.astype(F32), tags], axis=0)
    sent = [pltpu.make_async_copy(table_ref, table_hbm, out_sems.at[4])]
    sent[0].start()
    asked_tags = jnp.sum(labels, axis=0, keepdims=True)
    cold_lane = iota((1, LANES), 1) < HOT_LANE
    for h in range(heads):
        hot_ref[h, 3] = jnp.broadcast_to(asked_tags, (COLD, LANES)).astype(BF16)
    rows = HOT // SHARE * COLD
    row = iota((rows + HOT_PAD, 1), 0)
    row_share, row_at = row // COLD, row % COLD
    want = jnp.where(row_at < SHARE, SHARE * row_share + row_at, SHARE * (row_share - 1) + row_at)
    want = jnp.where(row_at < 2 * SHARE, want, -9)
    want = jnp.where(row < rows, want, row - rows) + slots
    tile_at = iota((rows, hd), 0) % COLD
    hot_tiles = []
    xs = []
    for load in loads:
        load.wait()
    for h in range(heads):
        xs.append(jnp.concatenate([ref[:, h * hd : (h + 1) * hd] for ref in (q_ref, k_ref, v_ref)], axis=1))
        moved = jnp.dot(
            (slot_all[h : h + 1] == want).astype(BF16), xs[h], preferred_element_type=F32
        )
        tiles = jnp.where(tile_at < SHARE, moved[:rows, hd : 2 * hd], moved[:rows, 2 * hd :])
        tiles = jnp.where(tile_at == COLD - 1, asked_tags, tiles)
        hot_tiles.append(tiles)
        hot_ref[h, 0:3] = moved[rows : rows + HOT, :hd].reshape(3, COLD, hd).astype(BF16)
    y = lax.axis_index("y")
    for d, ref in enumerate((h0_hbm, h1_hbm, h2_hbm, h3_hbm)):
        sent.append(pltpu.make_async_copy(hot_ref.at[lax.rem(y + d, heads)], ref, out_sems.at[5 + d]))
        sent[-1].start()
    labels = jnp.where(cold_lane, labels, 0.0)
    part = 256
    sub = iota((COLD, LANES), 0)
    for c in range(slots // part):
        first, stop = c * part // COLD, (c + 1) * part // COLD
        for h in range(heads):
            place = (slot_all[h : h + 1] == iota((part, tokens), 0) + c * part).astype(BF16)
            moved = jnp.dot(place, xs[h], preferred_element_type=F32)
            for j in range(3):
                send_ref[first:stop, 3 * h + j] = (
                    moved[:, j * hd : (j + 1) * hd].reshape(stop - first, COLD, hd).astype(BF16)
                )
        for dev in range(first, stop):
            share, head = dev // 16, dev % heads
            tile = hot_tiles[head][share * COLD : (share + 1) * COLD]
            tile = jnp.where(sub == 2 * SHARE, labels[dev : dev + 1], tile)
            send_ref[dev, 3 * heads] = tile.astype(BF16)
        out = pltpu.make_async_copy(
            send_ref.at[first:stop], send_hbm.at[first:stop], out_sems.at[c]
        )
        out.start()
        sent.append(out)
    for out in sent:
        out.wait()


def softmax_rows(scores, allowed, scale, values):
    masked = jnp.where(allowed, scores, NEG_FILL)
    top = jnp.max(masked, axis=1, keepdims=True)
    weights = jnp.exp2((masked - top) * scale)
    total = jnp.sum(weights, axis=1, keepdims=True)
    out = jnp.dot(weights.astype(BF16), values, preferred_element_type=F32)
    return out / total


NT = (((1,), (1,)), ((), ()))


def cold_kernel(got_ref, out_hbm, out_ref, out_sems):
    devices, tiles, _, hd = got_ref.shape
    heads = tiles // 3
    slots = devices * COLD
    scale = hd ** (-0.5) * LOG2E
    extra = got_ref[:, 3 * heads].astype(F32)
    spread = jnp.broadcast_to(
        extra[:, 2 * SHARE : 2 * SHARE + 1], (devices, COLD, LANES)
    ).reshape(slots, LANES)
    pick = iota((slots, LANES), 1) - iota((slots, LANES), 0) % COLD
    ones = jnp.ones((LANES, LANES), BF16)
    part = 512
    causal = iota((part, part), 1) <= iota((part, part), 0)
    sent = []
    for h in range(heads):
        tags = jnp.where(pick == COLD * h, spread, 0.0).astype(BF16)
        label_cols = jnp.dot(tags, ones, preferred_element_type=F32)
        q, k, v = (
            got_ref[:, 3 * h + j].astype(F32).reshape(slots, hd).astype(BF16) for j in range(3)
        )
        marked = label_cols == (iota((slots, LANES), 1) + 1).astype(F32)
        q = jnp.concatenate([q, jnp.where(marked, MARK_Q, 0.0).astype(BF16)], axis=1)
        k = jnp.concatenate([k, jnp.where(marked, MARK_K, 0.0).astype(BF16)], axis=1)
        for c in range(slots // part):
            stop = (c + 1) * part
            scores = lax.dot_general(
                q[c * part : stop], k[:stop], NT, preferred_element_type=F32
            )
            last = jnp.where(causal, scores[:, c * part :], NEG_FILL)
            if c > 0:
                last = jnp.concatenate([scores[:, : c * part], last], axis=1)
            top = jnp.max(last, axis=1, keepdims=True)
            weights = jnp.exp2((last - top) * scale)
            total = jnp.sum(weights, axis=1, keepdims=True)
            out = jnp.dot(weights.astype(BF16), v[:stop], preferred_element_type=F32) / total
            devs = slice(c * part // COLD, stop // COLD)
            out_ref[devs, h] = out.reshape(part // COLD, COLD, hd).astype(BF16)
            copy = pltpu.make_async_copy(
                out_ref.at[devs, h], out_hbm.at[devs, h], out_sems.at[h * (slots // part) + c]
            )
            copy.start()
            sent.append(copy)
    for out in sent:
        out.wait()


def mid_kernel(got_ref, kv_hbm, kv_ref, sems):
    devices, tiles, _, hd = got_ref.shape
    slots = devices * COLD
    keys = devices * SHARE
    extra = got_ref[:, tiles - 1].astype(F32).reshape(slots, hd).astype(BF16)
    runs = slots // LANES
    each = keys // runs
    row = iota((3 * each, 1), 0)
    kind, n = row // each, row % each
    at = n % SHARE
    col = n // SHARE * COLD + jnp.where(kind == 0, at, jnp.where(kind == 1, at + SHARE, COLD - 1))
    place = (col == iota((3 * each, LANES), 1)).astype(BF16)
    y, core, z = (lax.axis_index(a) for a in ("y", "core", "z"))
    lane = HOT_LANE + HOT * y + SHARE * (z * 2 + core) + iota((each, 1), 0) % SHARE
    own = iota((each, hd), 1) == lane
    tiles_each = each // COLD
    tags = []
    for b in range(runs):
        moved = jnp.dot(place, extra[b * LANES : (b + 1) * LANES], preferred_element_type=F32)
        first = b * tiles_each
        kv_ref[first : first + tiles_each] = moved[:each].reshape(tiles_each, COLD, hd).astype(BF16)
        kv_ref[48 + first : 48 + first + tiles_each] = (
            moved[each : 2 * each].reshape(tiles_each, COLD, hd).astype(BF16)
        )
        tags.append(jnp.where(own, moved[2 * each :], 0.0))
    sent = [pltpu.make_async_copy(kv_ref.at[0:96], kv_hbm.at[0:96], sems.at[0])]
    sent[0].start()
    tags = jnp.concatenate(tags, axis=0).astype(BF16)
    flat = lax.dot_general(jnp.ones((COLD, hd), BF16), tags, NT, preferred_element_type=F32)
    label = [flat[0:1, j * LANES : (j + 1) * LANES] for j in range(keys // LANES)]
    label.append(jnp.zeros((COLD - len(label), LANES), F32))
    kv_ref[96] = jnp.concatenate(label, axis=0).astype(BF16)
    sent.append(pltpu.make_async_copy(kv_ref.at[96:97], kv_hbm.at[96:97], sems.at[1]))
    sent[1].start()
    for out in sent:
        out.wait()


def hot_kernel(
    b0_ref, b1_ref, b2_ref, b3_ref, near_ref, far_ref,
    o0_ref, o1_ref, o2_ref, o3_ref, all_ref, k_ref, v_ref, o_ref,
):
    hd = b0_ref.shape[-1]
    rows = 4 * HOT
    keys = k_ref.shape[0] // 8
    scale = hd ** (-0.5) * LOG2E
    y, x, core, z = (lax.axis_index(a) for a in ("y", "x", "core", "z"))
    for d, ref in enumerate((b0_ref, b1_ref, b2_ref, b3_ref)):
        all_ref[lax.rem(y + 4 - d, 4)] = ref[...].astype(F32)
    q = all_ref[:, 0:3].reshape(rows, hd).astype(BF16)
    row = iota((rows, 1), 0)
    tags = jnp.broadcast_to(all_ref[:, 3, 0:1], (4, HOT, LANES)).reshape(rows, LANES)
    own = iota((rows, LANES), 1) == HOT_LANE + HOT * y + row % HOT
    label_col = jnp.sum(jnp.where(own, tags, 0.0), axis=1, keepdims=True)
    asked_at = (((z * 2 + core) * 16 + x * 4) * HOT + row).astype(F32)
    n = iota((1, keys), 1)
    key_at = (n // SHARE) * HOT + n % SHARE
    allowed = []
    for dc, ref in enumerate((near_ref, far_ref)):
        for dz in range(4):
            tile = 97 * dz
            at = slice((dc * 4 + dz) * keys, (dc * 4 + dz + 1) * keys)
            k_ref[at] = ref[tile : tile + 48].astype(F32).reshape(keys, hd).astype(BF16)
            v_ref[at] = ref[tile + 48 : tile + 96].astype(F32).reshape(keys, hd).astype(BF16)
            tags = ref[tile + 96].astype(F32)
            label = jnp.concatenate([tags[j : j + 1] for j in range(keys // LANES)], axis=1)
            share = lax.rem(z + 4 - dz, 4) * 2 + lax.rem(core + dc, 2)
            there = (key_at + SHARE * share).astype(F32)
            allowed.append((label_col == label) & (there <= asked_at))
    scores = lax.dot_general(q, k_ref[...], NT, preferred_element_type=F32)
    out = softmax_rows(scores, jnp.concatenate(allowed, axis=1), scale, v_ref[...])
    o_ref[...] = out.reshape(4, 3, COLD, hd)
    for d, ref in enumerate((o0_ref, o1_ref, o2_ref, o3_ref)):
        ref[...] = o_ref[lax.rem(y + 4 - d, 4)].astype(BF16)


def unpack_kernel(table_ref, back_ref, o0_ref, o1_ref, o2_ref, o3_ref, out_hbm, hot_ref, out_ref, sems):
    devices, heads, _, hd = back_ref.shape
    tokens = table_ref.shape[1]
    cols = columns_of(table_ref[...])
    slots = devices * COLD
    part = 256
    for d, ref in enumerate((o0_ref, o1_ref, o2_ref, o3_ref)):
        hot_ref[d] = ref[...].astype(F32)
    y = lax.axis_index("y")
    rows = []
    for h in range(heads):
        rows.append(back_ref[:, h].astype(F32).reshape(slots, hd).astype(BF16))
        hot = hot_ref[lax.rem(h + 4 - y, 4)].reshape(HOT, hd)
        spare = jnp.zeros((LANES - HOT, hd), F32)
        rows[h] = jnp.concatenate([rows[h], jnp.concatenate([hot, spare], axis=0).astype(BF16)], axis=0)
    sent = []
    for c in range(tokens // part):
        at = slice(c * part, (c + 1) * part)
        for h in range(heads):
            slot = cols[at, h : h + 1].astype(jnp.int32)
            place = (slot == iota((part, slots + LANES), 1)).astype(BF16)
            got = jnp.dot(place, rows[h], preferred_element_type=F32)
            out_ref[at, h * hd : (h + 1) * hd] = got.astype(BF16)
        out = pltpu.make_async_copy(out_ref.at[at], out_hbm.at[at], sems.at[c])
        out.start()
        sent.append(out)
    for out in sent:
        out.wait()


VMEM = pl.BlockSpec(memory_space=pltpu.VMEM)
HBM = pl.BlockSpec(memory_space=pl.ANY)
AXES = ("z", "core", "x", "y")
MIB = 1024 * 1024


def call(kernel, name, limit, ins, outs, scratch, *arrays, flops=None):
    return pl.pallas_call(
        kernel,
        out_shape=tuple(
            pltpu.HBM(*out[1:]) if out[0] is HBM else jax.ShapeDtypeStruct(*out[1:]) for out in outs
        ),
        in_specs=ins,
        out_specs=tuple(out[0] for out in outs),
        scratch_shapes=scratch,
        compiler_params=pltpu.CompilerParams(vmem_limit_bytes=limit * MIB),
        name=name,
        cost_estimate=None if flops is None else pl.CostEstimate(flops=flops, bytes_accessed=0, transcendentals=0),
    )(*arrays)


def shift(block, axis, by):
    size = lax.axis_size(axis)
    return lax.ppermute(block, axis, [(i, (i + by) % size) for i in range(size)])


def local(query_rows, key_rows, value_rows, cluster_ids):
    devices = lax.axis_size(AXES)
    heads, tokens = cluster_ids.shape
    hd = query_rows.shape[1] // heads
    tile = (COLD, hd)
    payload = (devices, 3 * heads + 1, *tile)
    table, h0, h1, h2, h3, send = call(
        pack_kernel, "pack", 58, [HBM] * 4,
        [(HBM, (2 * heads, tokens), F32)] + [(HBM, (4, *tile), BF16)] * 4 + [(HBM, payload, BF16)],
        [
            pltpu.VMEM((heads, tokens), jnp.int32), pltpu.VMEM((2 * heads, tokens), F32),
            *[pltpu.VMEM((tokens, heads * hd), BF16)] * 3,
            pltpu.VMEM((heads, 4, *tile), BF16), pltpu.VMEM(payload, BF16),
            pltpu.SemaphoreType.DMA((3 * heads + 1,)), pltpu.SemaphoreType.DMA((9,)),
        ],
        cluster_ids, query_rows, key_rows, value_rows,
    )
    got = lax.all_to_all(send, AXES, split_axis=0, concat_axis=0, tiled=True)
    asked = [h0] + [shift(b, "y", d + 1) for d, b in enumerate((h1, h2, h3))]
    got, asked = lax.optimization_barrier((got, asked))
    (kv,) = call(
        mid_kernel, "mid", 24, [VMEM], [(HBM, (97, *tile), BF16)],
        [pltpu.VMEM((97, *tile), BF16), pltpu.SemaphoreType.DMA((2,))], got,
    )
    got, kv = lax.optimization_barrier((got, kv))
    near = [kv] + [shift(kv, "z", d) for d in (1, 2, 3)]
    (answer,) = call(
        cold_kernel, "cold", 24, [VMEM], [(HBM, (devices, heads, *tile), BF16)],
        [pltpu.VMEM((devices, heads, *tile), BF16), pltpu.SemaphoreType.DMA((2 * heads,))],
        got, flops=20_000_000_000,
    )
    near, _ = lax.optimization_barrier((near, answer))
    near = jnp.concatenate(near, axis=0)
    far = shift(near, "core", 1)
    outs = call(
        hot_kernel, "hot", 24, [VMEM] * 6, [(VMEM, (3, *tile), BF16)] * 4,
        [
            pltpu.VMEM((4, 4, *tile), F32), pltpu.VMEM((devices * HOT, hd), BF16),
            pltpu.VMEM((devices * HOT, hd), BF16), pltpu.VMEM((4, 3, *tile), F32),
        ],
        *asked, near, far,
        flops=2_000_000_000,
    )
    hot_out = [outs[0]] + [shift(b, "y", 3 - d) for d, b in enumerate(outs[1:])]
    back = lax.all_to_all(answer, AXES, split_axis=0, concat_axis=0, tiled=True)
    (result,) = call(
        unpack_kernel, "unpack", 24, [VMEM] * 6, [(HBM, (tokens, heads * hd), BF16)],
        [
            pltpu.VMEM((4, 3, *tile), F32), pltpu.VMEM((tokens, heads * hd), BF16),
            pltpu.SemaphoreType.DMA((4,)),
        ],
        table, back, *hot_out,
    )
    return result


def solution(mesh):
    split = jax.sharding.Mesh(mesh.devices.reshape(4, 2, 4, 4), AXES)
    return jax.shard_map(
        local,
        mesh=split,
        in_specs=(P(AXES, None), P(AXES, None), P(AXES, None), P(None, AXES)),
        out_specs=P(AXES, None),
        check_vma=False,
    )
```

```python
import jax
import jax.numpy as jnp
from jax import lax
from jax.experimental import pallas as pl
from jax.experimental.pallas import tpu as pltpu
from jax.sharding import PartitionSpec as P

CL_DEV = 8
COLD = 8
HOT = 24
HOT_PAD = 32
LANES = 128
NEG_FILL = -1e30
SHARE = 3
HOT_LANE = 32
MARK_Q = 104.0
MARK_K = 100.0
LOG2E = 1.4426950408889634
F32 = jnp.float32
BF16 = jnp.bfloat16


def iota(shape, dim):
    return lax.broadcasted_iota(jnp.int32, shape, dim)


def columns_of(table):
    tokens = table.shape[1]
    return jnp.transpose(
        jnp.concatenate([table, jnp.zeros((LANES - table.shape[0], tokens), F32)], axis=0)
    )


def pack_kernel(
    ids_hbm, q_hbm, k_hbm, v_hbm,
    table_hbm, h0_hbm, h1_hbm, h2_hbm, h3_hbm, send_hbm,
    ids_ref, table_ref, q_ref, k_ref, v_ref, hot_ref, send_ref, sems, out_sems,
):
    heads, tokens = ids_ref.shape
    hd = q_hbm.shape[1] // heads
    devices = send_ref.shape[0]
    slots = devices * COLD
    step = 256
    ids_load = pltpu.make_async_copy(ids_hbm, ids_ref, sems.at[3 * heads])
    ids_load.start()
    loads = [
        pltpu.make_async_copy(src.at[r * 512 : (r + 1) * 512], dst.at[r * 512 : (r + 1) * 512], sems.at[2 * j + r])
        for j, (src, dst) in enumerate(((q_hbm, q_ref), (k_hbm, k_ref), (v_hbm, v_ref)))
        for r in range(2)
    ]
    for load in loads:
        load.start()
    ids_load.wait()
    ids = ids_ref[...]
    owner = ids // CL_DEV
    tags = (ids - owner * CL_DEV + 1).astype(F32)
    upper = (iota((step, step), 0) < iota((step, step), 1)).astype(BF16)
    dev_col = iota((devices, step), 0)
    slot_rows = []
    labels = jnp.zeros((devices, LANES), F32)
    for h in range(heads):
        carry = jnp.zeros((devices, 1), F32)
        ones, ranks = [], []
        for b in range(tokens // step):
            one = (owner[h : h + 1, b * step : (b + 1) * step] == dev_col).astype(F32)
            inside = jnp.dot(one.astype(BF16), upper, preferred_element_type=F32) + carry
            carry = carry + jnp.sum(one, axis=1, keepdims=True)
            ones.append(one)
            ranks.append(jnp.sum(one * inside, axis=0, keepdims=True))
        full = (carry > COLD).astype(F32)
        for b, one in enumerate(ones):
            ranks[b] = jnp.where(
                jnp.sum(one * full, axis=0, keepdims=True) > 0.5, ranks[b] + slots, ranks[b]
            )
            lane = jnp.where(
                ranks[b] < COLD, ranks[b] + COLD * h, ranks[b] + (HOT_LANE + HOT * h - slots)
            ).astype(jnp.int32)
            tag = jnp.where(
                lane == iota((LANES, step), 0), tags[h : h + 1, b * step : (b + 1) * step], 0.0
            )
            labels = labels + lax.dot_general(
                one.astype(BF16), tag.astype(BF16), NT, preferred_element_type=F32
            )
        rank = jnp.concatenate(ranks, axis=1).astype(jnp.int32)
        slot_rows.append(jnp.where(rank >= slots, rank, owner[h : h + 1] * COLD + rank))
    slot_all = jnp.concatenate(slot_rows, axis=0)
    table_ref[...] = jnp.concatenate([slot_all.astype(F32), tags], axis=0)
    sent = [pltpu.make_async_copy(table_ref, table_hbm, out_sems.at[4])]
    sent[0].start()
    asked_tags = jnp.sum(labels, axis=0, keepdims=True)
    cold_lane = iota((1, LANES), 1) < HOT_LANE
    for h in range(heads):
        hot_ref[h, 3] = jnp.broadcast_to(asked_tags, (COLD, LANES)).astype(BF16)
    rows = HOT // SHARE * COLD
    row = iota((rows + HOT_PAD, 1), 0)
    row_share, row_at = row // COLD, row % COLD
    want = jnp.where(row_at < SHARE, SHARE * row_share + row_at, SHARE * (row_share - 1) + row_at)
    want = jnp.where(row_at < 2 * SHARE, want, -9)
    want = jnp.where(row < rows, want, row - rows) + slots
    tile_at = iota((rows, hd), 0) % COLD
    hot_tiles = []
    xs = []
    for load in loads:
        load.wait()
    for h in range(heads):
        xs.append(jnp.concatenate([ref[:, h * hd : (h + 1) * hd] for ref in (q_ref, k_ref, v_ref)], axis=1))
    labels = jnp.where(cold_lane, labels, 0.0)
    part = 256
    sub = iota((COLD, LANES), 0)
    for c in range(slots // part):
        first, stop = c * part // COLD, (c + 1) * part // COLD
        for h in range(heads):
            place = (slot_all[h : h + 1] == iota((part, tokens), 0) + c * part).astype(BF16)
            if c == 0:
                hot = (slot_all[h : h + 1] == want).astype(BF16)
                moved = jnp.dot(
                    jnp.concatenate([place, hot], axis=0), xs[h], preferred_element_type=F32
                )
                hot, moved = moved[part:], moved[:part]
                tiles = jnp.where(tile_at < SHARE, hot[:rows, hd : 2 * hd], hot[:rows, 2 * hd :])
                hot_tiles.append(jnp.where(tile_at == COLD - 1, asked_tags, tiles))
                hot_ref[h, 0:3] = hot[rows : rows + HOT, :hd].reshape(3, COLD, hd).astype(BF16)
            else:
                moved = jnp.dot(place, xs[h], preferred_element_type=F32)
            for j in range(3):
                send_ref[first:stop, 3 * h + j] = (
                    moved[:, j * hd : (j + 1) * hd].reshape(stop - first, COLD, hd).astype(BF16)
                )
        for dev in range(first, stop):
            share, head = dev // 16, dev % heads
            tile = hot_tiles[head][share * COLD : (share + 1) * COLD]
            tile = jnp.where(sub == 2 * SHARE, labels[dev : dev + 1], tile)
            send_ref[dev, 3 * heads] = tile.astype(BF16)
        out = pltpu.make_async_copy(
            send_ref.at[first:stop], send_hbm.at[first:stop], out_sems.at[c]
        )
        out.start()
        sent.append(out)
    y = lax.axis_index("y")
    for d, ref in enumerate((h0_hbm, h1_hbm, h2_hbm, h3_hbm)):
        sent.append(pltpu.make_async_copy(hot_ref.at[lax.rem(y + d, heads)], ref, out_sems.at[5 + d]))
        sent[-1].start()
    for out in sent:
        out.wait()


def softmax_rows(scores, allowed, scale, values):
    masked = jnp.where(allowed, scores, NEG_FILL)
    top = jnp.max(masked, axis=1, keepdims=True)
    weights = jnp.exp2((masked - top) * scale)
    total = jnp.sum(weights, axis=1, keepdims=True)
    out = jnp.dot(weights.astype(BF16), values, preferred_element_type=F32)
    return out / total


NT = (((1,), (1,)), ((), ()))


def cold_kernel(got_ref, out_hbm, out_ref, out_sems):
    devices, tiles, _, hd = got_ref.shape
    heads = tiles // 3
    slots = devices * COLD
    scale = hd ** (-0.5) * LOG2E
    extra = got_ref[:, 3 * heads].astype(F32)
    spread = jnp.broadcast_to(
        extra[:, 2 * SHARE : 2 * SHARE + 1], (devices, COLD, LANES)
    ).reshape(slots, LANES)
    pick = iota((slots, LANES), 1) - iota((slots, LANES), 0) % COLD
    ones = jnp.ones((LANES, LANES), BF16)
    part = 512
    causal = iota((part, part), 1) <= iota((part, part), 0)
    sent = []
    for h in range(heads):
        tags = jnp.where(pick == COLD * h, spread, 0.0).astype(BF16)
        label_cols = jnp.dot(tags, ones, preferred_element_type=F32)
        q, k, v = (
            got_ref[:, 3 * h + j].astype(F32).reshape(slots, hd).astype(BF16) for j in range(3)
        )
        marked = label_cols == (iota((slots, LANES), 1) + 1).astype(F32)
        q = jnp.concatenate([q, jnp.where(marked, MARK_Q, 0.0).astype(BF16)], axis=1)
        k = jnp.concatenate([k, jnp.where(marked, MARK_K, 0.0).astype(BF16)], axis=1)
        for c in range(slots // part):
            stop = (c + 1) * part
            scores = lax.dot_general(
                q[c * part : stop], k[:stop], NT, preferred_element_type=F32
            )
            last = jnp.where(causal, scores[:, c * part :], NEG_FILL)
            if c > 0:
                last = jnp.concatenate([scores[:, : c * part], last], axis=1)
            top = jnp.max(last, axis=1, keepdims=True)
            weights = jnp.exp2((last - top) * scale)
            total = jnp.sum(weights, axis=1, keepdims=True)
            out = jnp.dot(weights.astype(BF16), v[:stop], preferred_element_type=F32) / total
            devs = slice(c * part // COLD, stop // COLD)
            out_ref[devs, h] = out.reshape(part // COLD, COLD, hd).astype(BF16)
            copy = pltpu.make_async_copy(
                out_ref.at[devs, h], out_hbm.at[devs, h], out_sems.at[h * (slots // part) + c]
            )
            copy.start()
            sent.append(copy)
    for out in sent:
        out.wait()


def mid_kernel(got_ref, kv_hbm, kv_ref, sems):
    devices, tiles, _, hd = got_ref.shape
    slots = devices * COLD
    keys = devices * SHARE
    extra = got_ref[:, tiles - 1].astype(F32).reshape(slots, hd).astype(BF16)
    runs = slots // LANES
    each = keys // runs
    row = iota((3 * each, 1), 0)
    kind, n = row // each, row % each
    at = n % SHARE
    col = n // SHARE * COLD + jnp.where(kind == 0, at, jnp.where(kind == 1, at + SHARE, COLD - 1))
    place = (col == iota((3 * each, LANES), 1)).astype(BF16)
    y, core, z = (lax.axis_index(a) for a in ("y", "core", "z"))
    lane = HOT_LANE + HOT * y + SHARE * (z * 2 + core) + iota((each, 1), 0) % SHARE
    own = iota((each, hd), 1) == lane
    tiles_each = each // COLD
    tags = []
    for b in range(runs):
        moved = jnp.dot(place, extra[b * LANES : (b + 1) * LANES], preferred_element_type=F32)
        first = b * tiles_each
        kv_ref[first : first + tiles_each] = moved[:each].reshape(tiles_each, COLD, hd).astype(BF16)
        kv_ref[48 + first : 48 + first + tiles_each] = (
            moved[each : 2 * each].reshape(tiles_each, COLD, hd).astype(BF16)
        )
        tags.append(jnp.where(own, moved[2 * each :], 0.0))
    sent = [pltpu.make_async_copy(kv_ref.at[0:96], kv_hbm.at[0:96], sems.at[0])]
    sent[0].start()
    tags = jnp.concatenate(tags, axis=0).astype(BF16)
    flat = lax.dot_general(jnp.ones((COLD, hd), BF16), tags, NT, preferred_element_type=F32)
    label = [flat[0:1, j * LANES : (j + 1) * LANES] for j in range(keys // LANES)]
    label.append(jnp.zeros((COLD - len(label), LANES), F32))
    kv_ref[96] = jnp.concatenate(label, axis=0).astype(BF16)
    sent.append(pltpu.make_async_copy(kv_ref.at[96:97], kv_hbm.at[96:97], sems.at[1]))
    sent[1].start()
    for out in sent:
        out.wait()


def hot_kernel(
    b0_ref, b1_ref, b2_ref, b3_ref, near_ref, far_ref,
    o0_ref, o1_ref, o2_ref, o3_ref, all_ref, k_ref, v_ref, o_ref,
):
    hd = b0_ref.shape[-1]
    rows = 4 * HOT
    keys = k_ref.shape[0] // 8
    scale = hd ** (-0.5) * LOG2E
    y, x, core, z = (lax.axis_index(a) for a in ("y", "x", "core", "z"))
    for d, ref in enumerate((b0_ref, b1_ref, b2_ref, b3_ref)):
        all_ref[lax.rem(y + 4 - d, 4)] = ref[...].astype(F32)
    q = all_ref[:, 0:3].reshape(rows, hd).astype(BF16)
    row = iota((rows, 1), 0)
    tags = jnp.broadcast_to(all_ref[:, 3, 0:1], (4, HOT, LANES)).reshape(rows, LANES)
    own = iota((rows, LANES), 1) == HOT_LANE + HOT * y + row % HOT
    label_col = jnp.sum(jnp.where(own, tags, 0.0), axis=1, keepdims=True)
    asked_at = (((z * 2 + core) * 16 + x * 4) * HOT + row).astype(F32)
    n = iota((1, keys), 1)
    key_at = (n // SHARE) * HOT + n % SHARE
    allowed = []
    for dc, ref in enumerate((near_ref, far_ref)):
        for dz in range(4):
            tile = 97 * dz
            at = slice((dc * 4 + dz) * keys, (dc * 4 + dz + 1) * keys)
            k_ref[at] = ref[tile : tile + 48].astype(F32).reshape(keys, hd).astype(BF16)
            v_ref[at] = ref[tile + 48 : tile + 96].astype(F32).reshape(keys, hd).astype(BF16)
            tags = ref[tile + 96].astype(F32)
            label = jnp.concatenate([tags[j : j + 1] for j in range(keys // LANES)], axis=1)
            share = lax.rem(z + 4 - dz, 4) * 2 + lax.rem(core + dc, 2)
            there = (key_at + SHARE * share).astype(F32)
            allowed.append((label_col == label) & (there <= asked_at))
    scores = lax.dot_general(q, k_ref[...], NT, preferred_element_type=F32)
    out = softmax_rows(scores, jnp.concatenate(allowed, axis=1), scale, v_ref[...])
    o_ref[...] = out.reshape(4, 3, COLD, hd)
    for d, ref in enumerate((o0_ref, o1_ref, o2_ref, o3_ref)):
        ref[...] = o_ref[lax.rem(y + 4 - d, 4)].astype(BF16)


def unpack_kernel(table_ref, back_ref, o0_ref, o1_ref, o2_ref, o3_ref, out_hbm, hot_ref, out_ref, sems):
    devices, heads, _, hd = back_ref.shape
    tokens = table_ref.shape[1]
    cols = columns_of(table_ref[...])
    slots = devices * COLD
    part = 256
    for d, ref in enumerate((o0_ref, o1_ref, o2_ref, o3_ref)):
        hot_ref[d] = ref[...].astype(F32)
    y = lax.axis_index("y")
    rows = []
    for h in range(heads):
        rows.append(back_ref[:, h].astype(F32).reshape(slots, hd).astype(BF16))
        hot = hot_ref[lax.rem(h + 4 - y, 4)].reshape(HOT, hd)
        spare = jnp.zeros((LANES - HOT, hd), F32)
        rows[h] = jnp.concatenate([rows[h], jnp.concatenate([hot, spare], axis=0).astype(BF16)], axis=0)
    sent = []
    for c in range(tokens // part):
        at = slice(c * part, (c + 1) * part)
        for h in range(heads):
            slot = cols[at, h : h + 1].astype(jnp.int32)
            place = (slot == iota((part, slots + LANES), 1)).astype(BF16)
            got = jnp.dot(place, rows[h], preferred_element_type=F32)
            out_ref[at, h * hd : (h + 1) * hd] = got.astype(BF16)
        out = pltpu.make_async_copy(out_ref.at[at], out_hbm.at[at], sems.at[c])
        out.start()
        sent.append(out)
    for out in sent:
        out.wait()


VMEM = pl.BlockSpec(memory_space=pltpu.VMEM)
HBM = pl.BlockSpec(memory_space=pl.ANY)
AXES = ("z", "core", "x", "y")
MIB = 1024 * 1024


def call(kernel, name, limit, ins, outs, scratch, *arrays, flops=None):
    return pl.pallas_call(
        kernel,
        out_shape=tuple(
            pltpu.HBM(*out[1:]) if out[0] is HBM else jax.ShapeDtypeStruct(*out[1:]) for out in outs
        ),
        in_specs=ins,
        out_specs=tuple(out[0] for out in outs),
        scratch_shapes=scratch,
        compiler_params=pltpu.CompilerParams(vmem_limit_bytes=limit * MIB),
        name=name,
        cost_estimate=None if flops is None else pl.CostEstimate(flops=flops, bytes_accessed=0, transcendentals=0),
    )(*arrays)


def shift(block, axis, by):
    size = lax.axis_size(axis)
    return lax.ppermute(block, axis, [(i, (i + by) % size) for i in range(size)])


def local(query_rows, key_rows, value_rows, cluster_ids):
    devices = lax.axis_size(AXES)
    heads, tokens = cluster_ids.shape
    hd = query_rows.shape[1] // heads
    tile = (COLD, hd)
    payload = (devices, 3 * heads + 1, *tile)
    table, h0, h1, h2, h3, send = call(
        pack_kernel, "pack", 58, [HBM] * 4,
        [(HBM, (2 * heads, tokens), F32)] + [(HBM, (4, *tile), BF16)] * 4 + [(HBM, payload, BF16)],
        [
            pltpu.VMEM((heads, tokens), jnp.int32), pltpu.VMEM((2 * heads, tokens), F32),
            *[pltpu.VMEM((tokens, heads * hd), BF16)] * 3,
            pltpu.VMEM((heads, 4, *tile), BF16), pltpu.VMEM(payload, BF16),
            pltpu.SemaphoreType.DMA((3 * heads + 1,)), pltpu.SemaphoreType.DMA((9,)),
        ],
        cluster_ids, query_rows, key_rows, value_rows,
    )
    got = lax.all_to_all(send, AXES, split_axis=0, concat_axis=0, tiled=True)
    asked = [h0] + [shift(b, "y", d + 1) for d, b in enumerate((h1, h2, h3))]
    got, asked = lax.optimization_barrier((got, asked))
    (kv,) = call(
        mid_kernel, "mid", 24, [VMEM], [(HBM, (97, *tile), BF16)],
        [pltpu.VMEM((97, *tile), BF16), pltpu.SemaphoreType.DMA((2,))], got,
    )
    got, kv = lax.optimization_barrier((got, kv))
    near = [kv] + [shift(kv, "z", d) for d in (1, 2, 3)]
    (answer,) = call(
        cold_kernel, "cold", 24, [VMEM], [(HBM, (devices, heads, *tile), BF16)],
        [pltpu.VMEM((devices, heads, *tile), BF16), pltpu.SemaphoreType.DMA((2 * heads,))],
        got, flops=20_000_000_000,
    )
    near, _ = lax.optimization_barrier((near, answer))
    near = jnp.concatenate(near, axis=0)
    far = shift(near, "core", 1)
    outs = call(
        hot_kernel, "hot", 24, [VMEM] * 6, [(VMEM, (3, *tile), BF16)] * 4,
        [
            pltpu.VMEM((4, 4, *tile), F32), pltpu.VMEM((devices * HOT, hd), BF16),
            pltpu.VMEM((devices * HOT, hd), BF16), pltpu.VMEM((4, 3, *tile), F32),
        ],
        *asked, near, far,
        flops=2_000_000_000,
    )
    hot_out = [outs[0]] + [shift(b, "y", 3 - d) for d, b in enumerate(outs[1:])]
    back = lax.all_to_all(answer, AXES, split_axis=0, concat_axis=0, tiled=True)
    (result,) = call(
        unpack_kernel, "unpack", 24, [VMEM] * 6, [(HBM, (tokens, heads * hd), BF16)],
        [
            pltpu.VMEM((4, 3, *tile), F32), pltpu.VMEM((tokens, heads * hd), BF16),
            pltpu.SemaphoreType.DMA((4,)),
        ],
        table, back, *hot_out,
    )
    return result


def solution(mesh):
    split = jax.sharding.Mesh(mesh.devices.reshape(4, 2, 4, 4), AXES)
    return jax.shard_map(
        local,
        mesh=split,
        in_specs=(P(AXES, None), P(AXES, None), P(AXES, None), P(None, AXES)),
        out_specs=P(AXES, None),
        check_vma=False,
    )
```
